512 devices in a mesh: seq: 64 (over y_lo, z, core), head: 8 (over x, y_hi).
Axes of the slice: x: 4, y: 4 (y_hi: 2, y_lo: 2; y = y_hi * 2 + y_lo), z: 16, core: 2. Of those that a mesh axis runs over, the one named last changes fastest.
Arguments:
- qkv_fine: bfloat16 [64, 4, 4, 64, 3, 768], P('seq', None, None, 'head'), may hold values from -6 to 6
- grad_out: bfloat16 [64, 2, 2, 32, 768], P('seq', None, None, 'head'), may hold values from -24 to 24
- pool_weight: bfloat16 [27, 3, 768], replicated, may hold values from -1.25 to 1.25
- norm_gain: float32 [3, 96], replicated, may hold values from 0.25 to 1.75
Outputs:
- grad_qkv: bfloat16 [64, 4, 4, 64, 3, 768], P('seq', None, None, 'head')
- grad_pool: float32 [27, 3, 768], replicated
- grad_gain: float32 [3, 96], replicated
The draws below stay inside these ranges and needn't reach their ends.
All inputs are finite; a program needn't handle non-finite values.
Results may differ from the reference program's by a relative error of at most 0.0065.
Values may be sent and summed in bfloat16 or wider, within the bound.
A program may use at most 128 MiB of HBM per device.

```python
import math
import jax
import jax.numpy as jnp
from jax import lax

D = 768
HEADS = 8
HD = 96
COLS = 64
ROW_DEV = 4
ROW_GROUPS = 16
FR_DEV = 4
FRAMES = 16
ROWS = 64
N_SEQ = 64


def block_levels(stream_key, shape, cuts, least, high):
    def one(position, blocks):
        steps = jax.random.uniform(jax.random.fold_in(jax.random.fold_in(stream_key, 6), position), (blocks,), jnp.float32, least / len(cuts), high / len(cuts))
        return jnp.repeat(jnp.exp(steps), shape[position] // blocks).reshape((-1,) + (1,) * (len(shape) - position - 1))

    loudness = one(*cuts[0])
    for cut in cuts[1:]:
        loudness = loudness * one(*cut)
    return loudness


def noise(own_key, dims, scale, most, pieces=(), kind=jnp.bfloat16):
    factor_of = block_levels(own_key, dims, pieces, -0.22, 0.18) if pieces else 1.0
    values = jax.random.normal(own_key, dims, jnp.float32) * scale * factor_of
    return jnp.minimum(jnp.maximum(values, -most), most).astype(kind)


def setup_inputs(seed: int = 0) -> dict:
    splits = jax.random.split(jax.random.key(seed), 5)
    qkv_fine = noise(splits[0], (N_SEQ, FR_DEV, ROW_DEV, COLS, 3, D), 1.0, 6.0, ((0, 64), (3, 8)))
    grad_out = noise(splits[1], (N_SEQ, FR_DEV // 2, ROW_DEV // 2, COLS // 2, D), 4.0, 24.0, ((0, 64), (3, 8)))
    pool_weight = noise(splits[2], (27, 3, D), 27 ** -0.5, 1.25)
    norm_gain = jnp.clip(1.0 + 0.15 * jax.random.normal(splits[3], (3, HD), jnp.float32), 0.25, 1.75)
    return {"qkv_fine": qkv_fine, "grad_out": grad_out, "pool_weight": pool_weight, "norm_gain": norm_gain}


def normalize(values, gain):
    shaped = values.reshape(values.shape[:-1] + (values.shape[-1] // HD, HD))
    centred = shaped - lax.optimization_barrier(jnp.mean(shaped, -1, keepdims=True))
    spread = lax.optimization_barrier(jnp.mean(centred * centred, -1, keepdims=True))
    return (centred * lax.rsqrt(spread + 1e-06) * gain).reshape(values.shape)

def pool_grid(fine_head, weight_head, gain):
    results = []
    for member, stride in ((0, 2), (1, 4), (2, 4)):
        kernel = weight_head[:, member, :].reshape(3, 3, 3, 1, HD)
        pooled = lax.conv_general_dilated(fine_head[None, :, :, :, member, :], kernel, (stride, stride, stride), [(1, 1), (1, 1), (1, 1)], dimension_numbers=('NDHWC', 'DHWIO', 'NDHWC'), feature_group_count=HD, precision=lax.Precision.HIGHEST)[0]
        results.append(normalize(pooled, gain[member]))
    return tuple(results)

def reference(qkv_fine, grad_out, pool_weight, norm_gain):
    groups = N_SEQ // ROW_GROUPS
    fine_grid = qkv_fine.reshape(groups, ROW_GROUPS, FR_DEV, ROW_DEV, COLS, 3, HEADS, HD)
    fine_grid = fine_grid.transpose(6, 0, 2, 1, 3, 4, 5, 7).reshape(HEADS, FRAMES, ROWS, COLS, 3, HD)
    grad_grid = grad_out.reshape(groups, ROW_GROUPS, FR_DEV // 2, ROW_DEV // 2, COLS // 2, HEADS, HD)
    grad_grid = grad_grid.transpose(5, 0, 2, 1, 3, 4, 6).reshape(HEADS, FRAMES // 2, ROWS // 2, COLS // 2, HD)
    head_weight = pool_weight.reshape(27, 3, HEADS, HD).transpose(2, 0, 1, 3)
    gain_values = norm_gain.astype(jnp.float32)
    score_scale = HD ** (-0.5)

    def one_head(operands):
        fine_head, grad_head, weight_head = operands
        normed, pull_back = jax.vjp(pool_grid, fine_head.astype(jnp.float32), weight_head.astype(jnp.float32), gain_values)
        query_rows = normed[0].astype(jnp.bfloat16).reshape(-1, HD)
        key_rows = normed[1].astype(jnp.bfloat16).reshape(-1, HD)
        value_rows = normed[2].astype(jnp.bfloat16).reshape(-1, HD)
        grad_rows = grad_head.reshape(-1, HD)
        total_rows = query_rows.shape[0]
        block_rows = math.gcd(total_rows, 2048)

        def one_block(carry, index):
            first_row = (index * block_rows).astype(jnp.int32)
            query_block = lax.dynamic_slice_in_dim(query_rows, first_row, block_rows, 0)
            grad_block = lax.dynamic_slice_in_dim(grad_rows, first_row, block_rows, 0)
            scores = jnp.dot(query_block, key_rows.T, preferred_element_type=jnp.float32) * score_scale
            raised = jnp.exp(scores)
            attention = raised / lax.optimization_barrier(jnp.sum(raised, -1, keepdims=True))
            attention_low = attention.astype(jnp.bfloat16)
            grad_attention = jnp.dot(grad_block, value_rows.T, preferred_element_type=jnp.float32)
            row_delta = lax.optimization_barrier(jnp.sum(attention * grad_attention, -1, keepdims=True))
            grad_scores = (attention * (grad_attention - row_delta)).astype(jnp.bfloat16)
            grad_query = jnp.dot(grad_scores, key_rows, preferred_element_type=jnp.float32) * score_scale + grad_block.astype(jnp.float32)
            grad_key = carry[0] + jnp.dot(grad_scores.T, query_block, preferred_element_type=jnp.float32) * score_scale
            grad_value = carry[1] + jnp.dot(attention_low.T, grad_block, preferred_element_type=jnp.float32)
            return ((grad_key, grad_value), grad_query)
        empty = jnp.zeros(key_rows.shape, jnp.float32)
        (grad_key, grad_value), grad_blocks = lax.scan(one_block, (empty, empty), jnp.arange(total_rows // block_rows, dtype=jnp.int32))
        grad_normed = (grad_blocks.reshape(normed[0].shape), grad_key.reshape(normed[1].shape), grad_value.reshape(normed[2].shape))
        grad_fine, grad_weight, grad_gain = pull_back(grad_normed)
        return (grad_fine.astype(jnp.bfloat16), grad_weight, grad_gain)
    grad_fine, grad_weight, grad_gain = lax.map(one_head, (fine_grid, grad_grid, head_weight))
    grad_fine = grad_fine.reshape(HEADS, groups, FR_DEV, ROW_GROUPS, ROW_DEV, COLS, 3, HD)
    grad_qkv = grad_fine.transpose(1, 3, 2, 4, 5, 6, 0, 7).reshape(N_SEQ, FR_DEV, ROW_DEV, COLS, 3, D)
    grad_pool = grad_weight.transpose(1, 2, 0, 3).reshape(27, 3, D)
    return (grad_qkv, grad_pool, lax.optimization_barrier(jnp.sum(grad_gain, 0)))
```

```python
import jax
import jax.numpy as jnp
from jax import lax
from jax.experimental import pallas as pl
from jax.experimental.pallas import tpu as pltpu
from jax.sharding import PartitionSpec as P

MESH = pl.DeviceIdType.MESH
F32 = jnp.float32
BF16 = jnp.bfloat16
HD = 96
HEADS = 8
ROW_GROUPS = 16
SEQ = 64
ZS = 16
SCALE = HD ** -0.5

PAIRS_Q = (((0, 1), (1, 2)), ((1, 0), (2, 1), (3, 2)), ((3, 0),))
PAIRS_K = (((0, 1), (1, 2)), ((3, 0),))
OWN_Q = (0, 1, 3, 4)

(A2A_P, A2A_G, FWD_ROW, FWD_FRAME, FWD_CORNER, GATHER, QUAD, STATS, DQ, SCATTER,
 BWD_ROW, BWD_FRAME, BWD_CORNER, A2A_B, SUM_PLANE, SUM_Z, SPREAD) = range(17)


def iota(shape, dim):
    return lax.broadcasted_iota(jnp.int32, shape, dim)


def up(x, by):
    size = x.shape[0]
    return pltpu.roll(x, (size - by) % size, 0)


def split_heads(tiles):
    lane = iota(tiles[0].shape, 1)
    heads = []
    for n in range(HEADS):
        t = tiles[n // 4 * 3:n // 4 * 3 + 3]
        if n % 4 == 0:
            v = t[0]
        elif n % 4 == 1:
            v = jnp.where(lane < 32, pltpu.roll(t[0], 32, 1), pltpu.roll(t[1], 32, 1))
        elif n % 4 == 2:
            v = jnp.where(lane < 64, pltpu.roll(t[1], 64, 1), pltpu.roll(t[2], 64, 1))
        else:
            v = pltpu.roll(t[2], 96, 1)
        heads.append(jnp.where(lane < HD, v, 0.0))
    return heads


def merge_heads(h):
    lane = iota(h[0].shape, 1)
    tiles = []
    for half in (0, 4):
        a, b, c, d = h[half:half + 4]
        tiles.append(jnp.where(lane < 96, a, pltpu.roll(b, 96, 1)))
        tiles.append(jnp.where(lane < 64, pltpu.roll(b, 96, 1), pltpu.roll(c, 64, 1)))
        tiles.append(jnp.where(lane < 32, pltpu.roll(c, 64, 1), pltpu.roll(d, 32, 1)))
    return tiles


def tiles_of(v):
    return [v[:, j * 128:(j + 1) * 128] for j in range(6)]


def kernel(x_ref, g_ref, w_ref, gain_ref, gx_ref, gw_ref, gg_ref,
           wt, sb, gs, rb, gr, pe, hs, hr, norm, kvg, qgr, raised_ref, ga_ref, st, dqb, dqr, zb, zr,
           hb, hbr, ge, sb2, rb2, gall, ex, sw, wb, kr, zs, fr, flat, gsc, ss, rs):
    s = lax.axis_index("seq")
    n = lax.axis_index("head")
    group, u = s // ROW_GROUPS, s % ROW_GROUPS
    yl, z, core = s // (2 * ZS), s // 2 % ZS, s % 2

    def head_peer(k):
        return (s, lax.rem(n + k, HEADS))

    def z_peer(k):
        return (yl * (2 * ZS) + lax.rem(z + k, ZS) * 2 + core, n)

    def quad_seq(k):
        return lax.rem(yl + k // 2, 2) * (2 * ZS) + z * 2 + lax.rem(core + k % 2, 2)

    def plane_peer(p):
        return (quad_seq(p // HEADS), lax.rem(n + p % HEADS, HEADS))

    def seq_peer(d):
        return (lax.rem(s + d + SEQ, SEQ), n)

    barrier = pltpu.get_barrier_semaphore()

    def greet(peer):
        pl.semaphore_signal(barrier, inc=1, device_id=peer, device_id_type=MESH)

    def each(count, body):
        def step(k, carry):
            body(k)
            return carry
        lax.fori_loop(1, count, step, 0)

    each(32, lambda p: greet(plane_peer(p)))
    each(ZS, lambda k: greet(z_peer(k)))
    for d in (1, 16, 17, -1, -16, -17):
        greet(seq_peer(d))

    def send(stage, src, dst, peer):
        pltpu.make_async_remote_copy(src_ref=src, dst_ref=dst, send_sem=ss.at[stage], recv_sem=rs.at[stage],
                                     device_id=peer, device_id_type=MESH).start()

    def arrived(stage, ref):
        pltpu.make_async_copy(ref, ref, rs.at[stage]).wait()

    def sent(stage, ref):
        pltpu.make_async_copy(ref, ref, ss.at[stage]).wait()

    row = iota((8, 768), 0)

    def taps(ab, carry):
        def one(m, e):
            return jnp.broadcast_to(w_ref[m, pl.ds(ab * 3 + e, 1), :], (8, 768))
        wt[0, ab] = jnp.where(row % 2 == 0, one(0, 1), one(0, 2))
        wt[1, ab] = jnp.where(row % 2 == 1, one(0, 0), 0.0)
        for m in (1, 2):
            wt[1 + m, ab] = jnp.where(row % 4 == 0, one(m, 1), jnp.where(
                row % 4 == 1, one(m, 2), jnp.where(row % 4 == 3, one(m, 0), 0.0)))
        return carry
    lax.fori_loop(0, 9, taps, 0)

    def fine(m, f, r):
        return x_ref[f, r, m].astype(F32)

    def store_heads(grp, v):
        for h, part in enumerate(split_heads(tiles_of(v))):
            sb[h, grp * 8:grp * 8 + 8, :] = part

    for t in range(3):
        for y in range(3):
            a_sum = b_sum = None
            for f, a in PAIRS_Q[t]:
                for r, b in PAIRS_Q[y]:
                    v = fine(0, f, r)
                    ta, tb = v * wt[0, a * 3 + b], v * wt[1, a * 3 + b]
                    a_sum = ta if a_sum is None else a_sum + ta
                    b_sum = tb if b_sum is None else b_sum + tb
            b1 = pltpu.roll(b_sum, 1, 0)
            e = a_sum + up(a_sum, 1) + jnp.where(row == 0, 0.0, b1)
            v = jnp.where(row == 0, e, jnp.where(row == 1, up(e, 1), jnp.where(row == 2, up(e, 2), jnp.where(
                row == 3, up(e, 3), jnp.where(row == 4, up(b1, 4), 0.0)))))
            store_heads(t * 3 + y, v)
    for t in range(2):
        for y in range(2):
            both = []
            for m in (1, 2):
                k_sum = None
                for f, a in PAIRS_K[t]:
                    for r, b in PAIRS_K[y]:
                        tk = fine(m, f, r) * wt[1 + m, a * 3 + b]
                        k_sum = tk if k_sum is None else k_sum + tk
                t1 = k_sum + up(k_sum, 1)
                both.append(jnp.where(row == 0, t1, jnp.where(row == 1, up(t1, 2) + up(k_sum, 4), jnp.where(
                    row == 2, up(k_sum, 5), 0.0))))
            store_heads(9 + t * 2 + y, both[0] + pltpu.roll(both[1], 4, 0))
    gh = []
    for t in range(2):
        v = jnp.concatenate([g_ref[t, 0].astype(F32), g_ref[t, 1].astype(F32)], 0)
        gh.append(split_heads(tiles_of(v)))
    for h in range(HEADS):
        gs[h] = jnp.concatenate([gh[0][h], gh[1][h]], 0).astype(BF16)

    pl.semaphore_wait(barrier, 31 + ZS - 1 + 6)

    def to_heads(k):
        peer = head_peer(k)
        send(A2A_P, sb.at[peer[1]], rb.at[k], peer)
        send(A2A_G, gs.at[peer[1]], gr.at[k], peer)
    each(HEADS, to_heads)
    rb[0] = sb[n]
    gr[0] = gs[n]
    arrived(A2A_P, rb.at[pl.ds(1, HEADS - 1)])
    arrived(A2A_G, gr.at[pl.ds(1, HEADS - 1)])

    row8 = iota((8, 128), 0)
    from_col = [lax.rem(n - h + HEADS, HEADS) for h in range(HEADS)]
    for grp in range(9):
        parts = [rb[from_col[h], grp * 8:grp * 8 + 8, :] for h in range(HEADS)]
        rolled = [pltpu.roll(parts[2 * j + 1], 4, 0) for j in range(4)]
        for j in range(4):
            v = parts[2 * j] + jnp.where(row8 >= 4, rolled[j], 0.0)
            if j:
                v = v + jnp.where(row8 == 0, rolled[j - 1], 0.0)
            pe[grp * 32 + j * 8:grp * 32 + j * 8 + 8, :] = v
    for grp in range(4):
        parts = [rb[from_col[h], 72 + grp * 8:80 + grp * 8, :] for h in range(HEADS)]
        for m in range(2):
            if m == 0:
                own = [jnp.where(row8 < 4, p, 0.0) for p in parts]
            else:
                own = [pltpu.roll(jnp.where(row8 >= 4, p, 0.0), 4, 0) for p in parts]
            last = [pltpu.roll(own[4 * j + 3], 6, 0) for j in range(2)]
            for j in range(2):
                v = own[4 * j] + pltpu.roll(own[4 * j + 1], 2, 0) + pltpu.roll(own[4 * j + 2], 4, 0)
                v = v + jnp.where(row8 >= 4, last[j], 0.0)
                if j:
                    v = v + jnp.where(row8 == 0, last[0], 0.0)
                at = 288 + m * 64 + grp * 16 + j * 8
                pe[at:at + 8, :] = v

    def pq(t, y):
        return pe[(t * 3 + y) * 32:(t * 3 + y) * 32 + 32, :]

    def pkv(m, t, y):
        at = 288 + m * 64 + (t * 2 + y) * 16
        return pe[at:at + 16, :]

    hs[0:96, :] = jnp.concatenate([pq(0, 2), pq(1, 2), pkv(0, 0, 1), pkv(1, 0, 1)], 0).astype(BF16)
    hs[96:192, :] = jnp.concatenate([pq(2, 0), pq(2, 1), pkv(0, 1, 0), pkv(1, 1, 0)], 0).astype(BF16)
    hs[192:256, :] = jnp.concatenate([pq(2, 2), pkv(0, 1, 1), pkv(1, 1, 1)], 0).astype(BF16)
    spans = (pl.ds(0, 96), pl.ds(96, 96), pl.ds(192, 64))
    for stage, span, d in zip((FWD_ROW, FWD_FRAME, FWD_CORNER), spans, (1, 16, 17)):
        send(stage, hs.at[span], hr.at[span], seq_peer(d))

    parts = [gr[from_col[h]].astype(F32) for h in range(HEADS)]
    for t in range(2):
        for y in range(2):
            vs = []
            for j in range(4):
                a, b = parts[2 * j][t * 8:t * 8 + 8], parts[2 * j + 1][t * 8:t * 8 + 8]
                if y == 0:
                    vs.append(jnp.where(row8 < 4, a, pltpu.roll(b, 4, 0)))
                else:
                    vs.append(jnp.where(row8 < 4, pltpu.roll(a, 4, 0), b))
            at = 128 + (t * 2 + y) * 32
            qgr[0, at:at + 32, :] = jnp.concatenate(vs, 0).astype(BF16)
    gsc[...] = jnp.zeros_like(gsc)
    gsc[0:3, 0:HD] = gain_ref[...]

    for stage, span in zip((FWD_ROW, FWD_FRAME, FWD_CORNER), spans):
        arrived(stage, hr.at[span])
    has_u = (u > 0).astype(F32)
    has_g = (group > 0).astype(F32)

    def border(lo, count, has):
        return hr[lo:lo + count, :].astype(F32) * has

    has_c = has_u * has_g
    q00 = pq(0, 0) + border(0, 32, has_u) + border(96, 32, has_g) + border(192, 32, has_c)
    q01 = pq(0, 1) + border(128, 32, has_g)
    q10 = pq(1, 0) + border(32, 32, has_u)
    k00 = pkv(0, 0, 0) + border(64, 16, has_u) + border(160, 16, has_g) + border(224, 16, has_c)
    v00 = pkv(1, 0, 0) + border(80, 16, has_u) + border(176, 16, has_g) + border(240, 16, has_c)
    pooled = jnp.concatenate([q00, q01, q10, pq(1, 1), k00, v00], 0)
    lane = iota((160, 128), 1)
    which = iota((160, 128), 0)
    gain = jnp.where(which < 128, gsc[0:1, :], jnp.where(which < 144, gsc[1:2, :], gsc[2:3, :]))
    centred = jnp.where(lane < HD, pooled - jnp.sum(pooled, 1, keepdims=True) * (1.0 / HD), 0.0)
    rstd = lax.rsqrt(jnp.sum(centred * centred, 1, keepdims=True) * (1.0 / HD) + 1e-6)
    unit = centred * rstd
    normed = (unit * gain).astype(BF16)
    norm[0] = unit
    norm[1] = jnp.broadcast_to(rstd, (160, 128))
    norm[2] = gain
    qgr[0, 0:128, :] = normed[0:128]
    kvg[0] = normed[128:160]

    each(ZS, lambda k: send(GATHER, kvg.at[0], kvg.at[k], z_peer(k)))
    for k in range(1, 4):
        send(QUAD, qgr.at[0], qgr.at[k], (quad_seq(k), n))
    arrived(QUAD, qgr.at[pl.ds(1, 3)])
    arrived(GATHER, kvg.at[pl.ds(1, ZS - 1)])

    keys = kvg[:, 0:16, :].reshape(256, 128)
    values = kvg[:, 16:32, :].reshape(256, 128)
    queries = qgr[:, 0:128, :].reshape(512, 128)
    grads = qgr[:, 128:256, :].reshape(512, 128)
    nt = (((1,), (1,)), ((), ()))
    raised_ref[...] = jnp.exp(lax.dot_general(keys, queries, nt, preferred_element_type=F32) * SCALE)
    ga_ref[...] = lax.dot_general(values, grads, nt, preferred_element_type=F32)
    total = jnp.sum(raised_ref[...], 0, keepdims=True)
    delta = jnp.sum(raised_ref[...] * ga_ref[...], 0, keepdims=True)
    for j in range(4):
        st[0, j:j + 1, :] = total[:, j * 128:(j + 1) * 128]
        st[0, 4 + j:5 + j, :] = delta[:, j * 128:(j + 1) * 128]
    for k in range(1, 4):
        send(STATS, st.at[0], st.at[k], (quad_seq(k), n))
    arrived(STATS, st.at[pl.ds(1, 3)])

    def quad_sum(at):
        outs = []
        for j in range(4):
            v = st[0, at + j:at + j + 1, :]
            for k in range(1, 4):
                i = at + (j ^ k)
                v = v + st[k, i:i + 1, :]
            outs.append(v)
        return jnp.concatenate(outs, 1)

    inverse = 1.0 / quad_sum(0)
    row_delta = quad_sum(4) * inverse
    attention = raised_ref[...] * inverse
    grad_scores = (attention * (ga_ref[...] - row_delta)).astype(BF16)
    grad_query = lax.dot_general(grad_scores, keys, (((0,), (0,)), ((), ())), preferred_element_type=F32)
    dqb[...] = grad_query.reshape(4, 128, 128)
    for k in range(1, 4):
        send(DQ, dqb.at[k], dqr.at[k], (quad_seq(k), n))
    grad_key = jnp.dot(grad_scores, queries, preferred_element_type=F32) * SCALE
    grad_value = jnp.dot(attention.astype(BF16), grads, preferred_element_type=F32)
    zb[:, 0:16, :] = grad_key.reshape(ZS, 16, 128).astype(zb.dtype)
    zb[:, 16:32, :] = grad_value.reshape(ZS, 16, 128).astype(zb.dtype)
    each(ZS, lambda k: send(SCATTER, zb.at[k], zr.at[k], z_peer(ZS - k)))
    zr[0] = zb[0]
    dqr[0] = dqb[0]
    arrived(DQ, dqr.at[pl.ds(1, 3)])
    arrived(SCATTER, zr.at[pl.ds(1, ZS - 1)])

    dq = dqr[0] + dqr[1] + dqr[2] + dqr[3]
    dkv = jnp.sum(zr[...].astype(F32), 0)
    grad_normed = jnp.concatenate([dq * SCALE + qgr[0, 128:256, :].astype(F32), dkv], 0)
    unit = norm[0]
    gain_rows = grad_normed * unit
    gsc[0:1, :] = jnp.sum(gain_rows[0:128], 0, keepdims=True)
    gsc[1:2, :] = jnp.sum(gain_rows[128:144], 0, keepdims=True)
    gsc[2:3, :] = jnp.sum(gain_rows[144:160], 0, keepdims=True)
    inner = grad_normed * norm[2]
    mean_1 = jnp.sum(inner, 1, keepdims=True) * (1.0 / HD)
    mean_2 = jnp.sum(inner * unit, 1, keepdims=True) * (1.0 / HD)
    grad_pooled = norm[1] * jnp.where(lane < HD, inner - mean_1 - unit * mean_2, 0.0)

    qg = [grad_pooled[i * 32:i * 32 + 32] for i in range(4)]
    kvgr = grad_pooled[128:160]
    hb[0:96, :] = jnp.concatenate([qg[0], qg[2], kvgr], 0).astype(BF16)
    hb[96:192, :] = jnp.concatenate([qg[0], qg[1], kvgr], 0).astype(BF16)
    hb[192:256, :] = jnp.concatenate([qg[0], kvgr], 0).astype(BF16)
    for stage, span, d in zip((BWD_ROW, BWD_FRAME, BWD_CORNER), spans, (-1, -16, -17)):
        send(stage, hb.at[span], hbr.at[span], seq_peer(d))
    for i, grp in enumerate(OWN_Q):
        ge[grp * 32:grp * 32 + 32, :] = qg[i]
    ge[288:304, :] = kvgr[0:16]
    ge[352:368, :] = kvgr[16:32]
    for stage, span in zip((BWD_ROW, BWD_FRAME, BWD_CORNER), spans):
        arrived(stage, hbr.at[span])
    has_u = (u < ROW_GROUPS - 1).astype(F32)
    has_g = (group < SEQ // ROW_GROUPS - 1).astype(F32)

    def returned(lo, count, has):
        return hbr[lo:lo + count, :].astype(F32) * has

    has_c = has_u * has_g
    ge[2 * 32:3 * 32, :] = returned(0, 32, has_u)
    ge[5 * 32:6 * 32, :] = returned(32, 32, has_u)
    ge[6 * 32:7 * 32, :] = returned(96, 32, has_g)
    ge[7 * 32:8 * 32, :] = returned(128, 32, has_g)
    ge[8 * 32:9 * 32, :] = returned(192, 32, has_c)
    for m in range(2):
        at = 288 + m * 64
        ge[at + 16:at + 32, :] = returned(64 + 16 * m, 16, has_u)
        ge[at + 32:at + 48, :] = returned(160 + 16 * m, 16, has_g)
        ge[at + 48:at + 64, :] = returned(224 + 16 * m, 16, has_c)

    zero = jnp.zeros((8, 128), F32)
    out_rows = [[] for _ in range(HEADS)]
    for grp in range(9):
        vs = [ge[grp * 32 + j * 8:grp * 32 + j * 8 + 8, :] for j in range(4)] + [zero]
        half = [pltpu.roll(v, 4, 0) for v in vs]
        for h in range(HEADS):
            j = h // 2
            out_rows[h].append(vs[j] if h % 2 == 0 else jnp.where(row8 < 4, half[j], half[j + 1]))
    for grp in range(4):
        vs = [[ge[at:at + 8, :] for at in (288 + m * 64 + grp * 16, 296 + m * 64 + grp * 16)] + [zero] for m in range(2)]
        for h in range(HEADS):
            j, i = h // 4, h % 4
            parts = []
            for m in range(2):
                v = pltpu.roll(vs[m][j], 8 - 2 * i, 0) if i else vs[m][j]
                if i == 3:
                    v = jnp.where(row8 < 2, v, pltpu.roll(vs[m][j + 1], 2, 0))
                parts.append(v)
            out_rows[h].append(jnp.where(row8 < 4, parts[0], pltpu.roll(parts[1], 4, 0)))
    for h in range(HEADS):
        sb2[h] = jnp.concatenate(out_rows[h] + [zero], 0).astype(BF16)

    def to_columns(k):
        peer = head_peer(k)
        send(A2A_B, sb2.at[peer[1]], rb2.at[k], peer)
    each(HEADS, to_columns)
    rb2[0] = sb2[n]
    arrived(A2A_B, rb2.at[pl.ds(1, HEADS - 1)])

    tiles = merge_heads([rb2[from_col[h]].astype(F32) for h in range(HEADS)])
    for j in range(6):
        gall[:, j * 128:(j + 1) * 128] = tiles[j].astype(BF16)
    r = iota((208, 112), 0)
    grp, second, i = r >> 4, (r >> 3) & 1, r & 7
    target = grp * 8 + jnp.where(grp < 9, (i >> 1) + second, ((i + 1) >> 2) + 4 * second)
    spread = jnp.where(iota((208, 112), 1) == target, 1.0, 0.0).astype(BF16)
    ex[...] = jnp.dot(spread, gall[...], preferred_element_type=F32)

    def g_at(grp, second):
        at = grp * 16 + second * 8
        return ex[at:at + 8, :]

    def pairs(pair_list, a):
        return [(f, t) for t, entries in enumerate(pair_list) for f, tap in entries if tap == a]

    for a in range(3):
        for b in range(3):
            sums = [None] * 4
            for f, t in pairs(PAIRS_Q, a):
                for rr, y in pairs(PAIRS_Q, b):
                    v = fine(0, f, rr)
                    for second in range(2):
                        term = v * g_at(t * 3 + y, second)
                        sums[second] = term if sums[second] is None else sums[second] + term
            for f, t in pairs(PAIRS_K, a):
                for rr, y in pairs(PAIRS_K, b):
                    for m in (1, 2):
                        term = fine(m, f, rr) * g_at(9 + t * 2 + y, m - 1)
                        sums[1 + m] = term if sums[1 + m] is None else sums[1 + m] + term
            for i in range(4):
                sw[i, a * 3 + b] = sums[i]

    wb[480:512, :] = jnp.zeros((32, 128), F32)
    wb[486:489, :] = gsc[0:3, :]

    def by_tap(ab, carry):
        for m in range(3):
            if m == 0:
                first, second = sw[0, ab], sw[1, ab]
                e_rows = (jnp.where(row % 2 == 1, second, 0.0), jnp.where(row % 2 == 0, first, 0.0),
                          jnp.where(row % 2 == 1, first, 0.0))
            else:
                v = sw[1 + m, ab]
                e_rows = tuple(jnp.where(row % 4 == c, v, 0.0) for c in (3, 0, 1))
            for e in range(3):
                v = jnp.sum(e_rows[e], 0, keepdims=True)
                for j in range(6):
                    wb[pl.ds(j * 81 + m * 27 + ab * 3 + e, 1), :] = v[:, j * 128:(j + 1) * 128]
        return carry
    lax.fori_loop(0, 9, by_tap, 0)

    def piece_of(p):
        quad = lax.rem(yl + p // 16, 2) * 2 + lax.rem(core + p // 8 % 2, 2)
        return quad * HEADS + lax.rem(n + p % HEADS, HEADS)

    def piece(p):
        return pl.ds(pl.multiple_of(piece_of(p) * 16, 16), 16)

    each(32, lambda p: send(SUM_PLANE, wb.at[piece(p)], kr.at[p], plane_peer(p)))
    kr[0] = wb[piece(0), :]

    for f in range(4):
        for rr in range(4):
            q_sum = None
            for t, a in [(t, a) for t, entries in enumerate(PAIRS_Q) for ff, a in entries if ff == f]:
                for y, b in [(y, b) for y, entries in enumerate(PAIRS_Q) for ff, b in entries if ff == rr]:
                    term = g_at(t * 3 + y, 0) * wt[0, a * 3 + b] + g_at(t * 3 + y, 1) * wt[1, a * 3 + b]
                    q_sum = term if q_sum is None else q_sum + term
            gx_ref[f, rr, 0] = q_sum.astype(BF16)
            for m in (1, 2):
                k_sum = jnp.zeros((8, 768), F32)
                for t, a in [(t, a) for t, entries in enumerate(PAIRS_K) for ff, a in entries if ff == f]:
                    for y, b in [(y, b) for y, entries in enumerate(PAIRS_K) for ff, b in entries if ff == rr]:
                        k_sum = g_at(9 + t * 2 + y, m - 1) * wt[1 + m, a * 3 + b]
                gx_ref[f, rr, m] = k_sum.astype(BF16)

    arrived(SUM_PLANE, kr.at[pl.ds(1, 31)])
    zs[0] = jnp.sum(kr[...], 0)
    each(ZS, lambda k: send(SUM_Z, zs.at[0], zs.at[k], z_peer(k)))
    arrived(SUM_Z, zs.at[pl.ds(1, ZS - 1)])
    v = zs[lax.rem(z, ZS)]
    for k in range(1, ZS):
        v = v + zs[lax.rem(z - k + ZS, ZS)]
    fr[0] = v
    each(32, lambda p: send(SPREAD, fr.at[0], fr.at[p], plane_peer(p)))
    arrived(SPREAD, fr.at[pl.ds(1, 31)])

    def place(p, carry):
        q, k = p // HEADS, p % HEADS
        quad = lax.rem(yl + q // 2, 2) * 2 + lax.rem(core + q % 2, 2)
        at = (quad * HEADS + lax.rem(n - k + HEADS, HEADS)) * 16
        flat[pl.ds(pl.multiple_of(at, 16), 16), :] = fr[p]
        return carry
    lax.fori_loop(0, 32, place, 0)
    for j in range(6):
        for m in range(3):
            at = j * 81 + m * 27
            gw_ref[m, :, j * 128:(j + 1) * 128] = flat[at:at + 27, :]
    gg_ref[...] = flat[486:489, 0:HD]

    sent(A2A_P, rb.at[pl.ds(1, HEADS - 1)])
    sent(A2A_G, gr.at[pl.ds(1, HEADS - 1)])
    for stage, span in zip((FWD_ROW, FWD_FRAME, FWD_CORNER), spans):
        sent(stage, hr.at[span])
    sent(GATHER, kvg.at[pl.ds(1, ZS - 1)])
    sent(QUAD, qgr.at[pl.ds(1, 3)])
    sent(STATS, st.at[pl.ds(1, 3)])
    sent(DQ, dqr.at[pl.ds(1, 3)])
    sent(SCATTER, zr.at[pl.ds(1, ZS - 1)])
    for stage, span in zip((BWD_ROW, BWD_FRAME, BWD_CORNER), spans):
        sent(stage, hbr.at[span])
    sent(A2A_B, rb2.at[pl.ds(1, HEADS - 1)])
    sent(SUM_PLANE, kr.at[pl.ds(1, 31)])
    sent(SUM_Z, zs.at[pl.ds(1, ZS - 1)])
    sent(SPREAD, fr.at[pl.ds(1, 31)])


def shards(qkv_fine, grad_out, pool_weight, norm_gain):
    x = qkv_fine[0].transpose(0, 1, 3, 2, 4)
    w = pool_weight.transpose(1, 0, 2).astype(F32)
    vmem = pl.BlockSpec(memory_space=pltpu.VMEM)
    scratch = [
        ((4, 9, 8, 768), F32),
        ((8, 104, 128), F32),
        ((8, 16, 128), BF16),
        ((8, 104, 128), F32),
        ((8, 16, 128), BF16),
        ((416, 128), F32),
        ((256, 128), BF16),
        ((256, 128), BF16),
        ((3, 160, 128), F32),
        ((ZS, 32, 128), BF16),
        ((4, 256, 128), BF16),
        ((256, 512), F32),
        ((256, 512), F32),
        ((4, 8, 128), F32),
        ((4, 128, 128), F32),
        ((4, 128, 128), F32),
        ((ZS, 32, 128), BF16),
        ((ZS, 32, 128), BF16),
        ((256, 128), BF16),
        ((256, 128), BF16),
        ((416, 128), F32),
        ((8, 112, 128), BF16),
        ((8, 112, 128), BF16),
        ((112, 768), BF16),
        ((208, 768), F32),
        ((4, 9, 8, 768), F32),
        ((512, 128), F32),
        ((32, 16, 128), F32),
        ((ZS, 16, 128), F32),
        ((32, 16, 128), F32),
        ((512, 128), F32),
        ((8, 128), F32),
    ]
    gx, gw, gg = pl.pallas_call(
        kernel,
        out_shape=(jax.ShapeDtypeStruct(x.shape, BF16), jax.ShapeDtypeStruct(w.shape, F32),
                   jax.ShapeDtypeStruct(norm_gain.shape, F32)),
        in_specs=[vmem] * 4,
        out_specs=(vmem,) * 3,
        scratch_shapes=[pltpu.VMEM(shape, kind) for shape, kind in scratch]
        + [pltpu.SemaphoreType.DMA((17,)), pltpu.SemaphoreType.DMA((17,))],
        compiler_params=pltpu.CompilerParams(collective_id=0, has_side_effects=True,
                                             vmem_limit_bytes=48 * 1024 * 1024),
    )(x, grad_out[0], w, norm_gain)
    return gx.transpose(0, 1, 3, 2, 4)[None], gw.transpose(1, 0, 2), gg


def solution(mesh):
    in_specs = (P("seq", None, None, "head", None, None), P("seq", None, None, "head", None), P(), P())
    out_specs = (P("seq", None, None, "head", None, None), P(), P())
    return jax.shard_map(shards, mesh=mesh, in_specs=in_specs, out_specs=out_specs, check_vma=False)
```

```python
import jax
import jax.numpy as jnp
from jax import lax
from jax.experimental import pallas as pl
from jax.experimental.pallas import tpu as pltpu
from jax.sharding import PartitionSpec as P

MESH = pl.DeviceIdType.MESH
F32 = jnp.float32
BF16 = jnp.bfloat16
HD = 96
HEADS = 8
ROW_GROUPS = 16
SEQ = 64
ZS = 16
SCALE = HD ** -0.5

PAIRS_Q = (((0, 1), (1, 2)), ((1, 0), (2, 1), (3, 2)), ((3, 0),))
PAIRS_K = (((0, 1), (1, 2)), ((3, 0),))
OWN_Q = (0, 1, 3, 4)

(A2A_F, FINE, KV_ROW, KV_FRAME, KV_CORNER, Q_ROW, Q_FRAME, Q_CORNER, GATHER, QUAD, STATS, DQ, SCATTER, BQ_ROW, BQ_FRAME,
 BQ_CORNER, BK_ROW, BK_FRAME, BK_CORNER, A2A_B, SUM_QUAD, SUM_Z, SPREAD) = range(23)
FAR_FIRST = (8, 7, 9, 6, 10, 5, 11, 4, 12, 3, 13, 2, 14, 1, 15)
KV_SPANS = ((0, 32), (32, 32), (64, 32))
Q_SPANS = ((96, 64), (160, 64), (224, 32))


def iota(shape, dim):
    return lax.broadcasted_iota(jnp.int32, shape, dim)


def up(x, by):
    size = x.shape[0]
    return pltpu.roll(x, (size - by) % size, 0)


def split_heads(tiles):
    lane = iota(tiles[0].shape, 1)
    heads = []
    for n in range(HEADS):
        t = tiles[n // 4 * 3:n // 4 * 3 + 3]
        if n % 4 == 0:
            v = t[0]
        elif n % 4 == 1:
            v = jnp.where(lane < 32, pltpu.roll(t[0], 32, 1), pltpu.roll(t[1], 32, 1))
        elif n % 4 == 2:
            v = jnp.where(lane < 64, pltpu.roll(t[1], 64, 1), pltpu.roll(t[2], 64, 1))
        else:
            v = pltpu.roll(t[2], 96, 1)
        heads.append(jnp.where(lane < HD, v, 0.0))
    return heads


def merge_heads(h):
    lane = iota(h[0].shape, 1)
    tiles = []
    for half in (0, 4):
        a, b, c, d = h[half:half + 4]
        tiles.append(jnp.where(lane < 96, a, pltpu.roll(b, 96, 1)))
        tiles.append(jnp.where(lane < 64, pltpu.roll(b, 96, 1), pltpu.roll(c, 64, 1)))
        tiles.append(jnp.where(lane < 32, pltpu.roll(c, 64, 1), pltpu.roll(d, 32, 1)))
    return tiles


def tiles_of(v):
    return [v[:, j * 128:(j + 1) * 128] for j in range(6)]


def kernel(x_ref, g_ref, w_ref, gain_ref, gx_ref, gw_ref, gg_ref,
           xv, wf, wt, sb, rb, xs, xr, xf, pe, hs, hr, norm, kvg, qgr, raised_ref, ga_ref, st, dqb, dqr, zb, zr,
           hb, hbr, ge, exh, sb2, rb2, gall, ex, gxv, wg, wb, kr, zs, fr, flat, gsc, ss, rs, local):
    s = lax.axis_index("seq")
    n = lax.axis_index("head")
    group, u = s // ROW_GROUPS, s % ROW_GROUPS
    yl, z, core = s // (2 * ZS), s // 2 % ZS, s % 2

    load = pltpu.make_async_copy(x_ref, xv, local.at[0])
    load.start()

    def head_peer(k):
        return (s, lax.rem(n + k, HEADS))

    def z_peer(k):
        return (yl * (2 * ZS) + lax.rem(z + k, ZS) * 2 + core, n)

    def quad_peer(k):
        return (lax.rem(yl + k // 2, 2) * (2 * ZS) + z * 2 + lax.rem(core + k % 2, 2), n)

    def quad_index(k):
        return lax.rem(yl + k // 2, 2) * 2 + lax.rem(core + k % 2, 2)

    def plane_peer(p):
        return (quad_peer(p // HEADS)[0], lax.rem(n + p % HEADS, HEADS))

    def seq_peer(d):
        return (lax.rem(s + d + SEQ, SEQ), n)

    barrier = pltpu.get_barrier_semaphore()
    greeted = [seq_peer(d) for d in (16, 17, -16, -17)] + [z_peer(k) for k in FAR_FIRST]
    greeted += [seq_peer(1), seq_peer(-1)] + [quad_peer(k) for k in (3, 2, 1)] + [head_peer(k) for k in range(1, HEADS)]
    for peer in greeted:
        pl.semaphore_signal(barrier, inc=1, device_id=peer, device_id_type=MESH)

    def send(stage, src, dst, peer):
        pltpu.make_async_remote_copy(src_ref=src, dst_ref=dst, send_sem=ss.at[stage], recv_sem=rs.at[stage],
                                     device_id=peer, device_id_type=MESH).start()

    def arrived(stage, ref):
        pltpu.make_async_copy(ref, ref, rs.at[stage]).wait()

    pending = []

    def drain():
        for stage, ref in pending:
            pltpu.make_async_copy(ref, ref, ss.at[stage]).wait()

    row = iota((8, 768), 0)
    row8 = iota((8, 128), 0)
    lane8 = iota((8, 128), 1)
    wf[...] = w_ref[...].astype(F32)

    def taps(ab, carry):
        def one(m, e):
            return jnp.broadcast_to(wf[m, pl.ds(ab * 3 + e, 1), :], (8, 768))
        wt[0, ab] = jnp.where(row % 2 == 0, one(0, 1), one(0, 2))
        wt[1, ab] = jnp.where(row % 2 == 1, one(0, 0), 0.0)
        for m in (1, 2):
            wt[1 + m, ab] = jnp.where(row % 4 == 0, one(m, 1), jnp.where(
                row % 4 == 1, one(m, 2), jnp.where(row % 4 == 3, one(m, 0), 0.0)))
        return carry
    lax.fori_loop(0, 9, taps, 0)
    gsc[...] = jnp.zeros_like(gsc)
    gsc[0:3, 0:HD] = gain_ref[...]
    load.wait()

    def fine(m, f, r):
        return xv[(f * 4 + r) * 3 + m].astype(F32)

    groups = []
    for t in range(3):
        for y in range(3):
            a_sum = b_sum = None
            for f, a in PAIRS_Q[t]:
                for r, b in PAIRS_Q[y]:
                    v = fine(0, f, r)
                    ta, tb = v * wt[0, a * 3 + b], v * wt[1, a * 3 + b]
                    a_sum = ta if a_sum is None else a_sum + ta
                    b_sum = tb if b_sum is None else b_sum + tb
            b1 = pltpu.roll(b_sum, 1, 0)
            e = a_sum + up(a_sum, 1) + jnp.where(row == 0, 0.0, b1)
            v = jnp.where(row == 0, e, jnp.where(row == 1, up(e, 1), jnp.where(row == 2, up(e, 2), jnp.where(
                row == 3, up(e, 3), jnp.where(row == 4, up(b1, 4), 0.0)))))
            groups.append(v)
    for t in range(2):
        for y in range(2):
            both = []
            for m in (1, 2):
                k_sum = None
                for f, a in PAIRS_K[t]:
                    for r, b in PAIRS_K[y]:
                        tk = fine(m, f, r) * wt[1 + m, a * 3 + b]
                        k_sum = tk if k_sum is None else k_sum + tk
                t1 = k_sum + up(k_sum, 1)
                both.append(jnp.where(row == 0, t1, jnp.where(row == 1, up(t1, 2) + up(k_sum, 4), jnp.where(
                    row == 2, up(k_sum, 5), 0.0))))
            groups.append(both[0] + pltpu.roll(both[1], 4, 0))
    groups.append(jnp.zeros((8, 768), F32))
    for t in range(2):
        groups.append(jnp.concatenate([g_ref[t, 0].astype(F32), g_ref[t, 1].astype(F32)], 0))
    for p in range(8):
        v = jnp.concatenate(groups[2 * p:2 * p + 2], 0)
        for h, part in enumerate(split_heads(tiles_of(v))):
            sb[h, p * 16:p * 16 + 16, :] = part.astype(BF16)

    pl.semaphore_wait(barrier, len(greeted))
    for k in range(1, HEADS):
        peer = head_peer(k)
        send(A2A_F, sb.at[peer[1]], rb.at[k], peer)
    pending.append((A2A_F, rb.at[pl.ds(1, HEADS - 1)]))
    rb[0] = sb[n]

    def split_fine(p, carry):
        v = jnp.concatenate([xv[2 * p].astype(F32), xv[2 * p + 1].astype(F32)], 0)
        for h, part in enumerate(split_heads(tiles_of(v))):
            xs[h, pl.ds(pl.multiple_of(p * 16, 16), 16), :] = part.astype(BF16)
        return carry
    lax.fori_loop(0, 24, split_fine, 0)
    arrived(A2A_F, rb.at[pl.ds(1, HEADS - 1)])

    from_col = [lax.rem(n - h + HEADS, HEADS) for h in range(HEADS)]
    sets = [rb[from_col[h]].astype(F32) for h in range(HEADS)]
    for grp in range(4):
        parts = [v[72 + grp * 8:80 + grp * 8] for v in sets]
        for m in range(2):
            if m == 0:
                own = [jnp.where(row8 < 4, p, 0.0) for p in parts]
            else:
                own = [pltpu.roll(jnp.where(row8 >= 4, p, 0.0), 4, 0) for p in parts]
            last = [pltpu.roll(own[4 * j + 3], 6, 0) for j in range(2)]
            for j in range(2):
                v = own[4 * j] + pltpu.roll(own[4 * j + 1], 2, 0) + pltpu.roll(own[4 * j + 2], 4, 0)
                v = v + jnp.where(row8 >= 4, last[j], 0.0)
                if j:
                    v = v + jnp.where(row8 == 0, last[0], 0.0)
                at = 288 + m * 64 + grp * 16 + j * 8
                pe[at:at + 8, :] = v

    def pq(t, y):
        return pe[(t * 3 + y) * 32:(t * 3 + y) * 32 + 32, :]

    def pkv(t, y):
        at = 288 + (t * 2 + y) * 16
        return jnp.concatenate([pe[at:at + 16, :], pe[at + 64:at + 80, :]], 0)

    def exchange(stages, spans, src, dst, distances):
        for stage, (lo, count), d in zip(stages, spans, distances):
            send(stage, src.at[pl.ds(lo, count)], dst.at[pl.ds(lo, count)], seq_peer(d))
            pending.append((stage, dst.at[pl.ds(lo, count)]))

    def exchanged(stages, spans, dst):
        for stage, (lo, count) in zip(stages, spans):
            arrived(stage, dst.at[pl.ds(lo, count)])

    hs[0:96, :] = jnp.concatenate([pkv(0, 1), pkv(1, 0), pkv(1, 1)], 0).astype(BF16)
    exchange((KV_ROW, KV_FRAME, KV_CORNER), KV_SPANS, hs, hr, (1, 16, 17))
    for grp in range(9):
        parts = [v[grp * 8:grp * 8 + 8] for v in sets]
        rolled = [pltpu.roll(parts[2 * j + 1], 4, 0) for j in range(4)]
        for j in range(4):
            v = parts[2 * j] + jnp.where(row8 >= 4, rolled[j], 0.0)
            if j:
                v = v + jnp.where(row8 == 0, rolled[j - 1], 0.0)
            pe[grp * 32 + j * 8:grp * 32 + j * 8 + 8, :] = v
    hs[96:256, :] = jnp.concatenate([pq(0, 2), pq(1, 2), pq(2, 0), pq(2, 1), pq(2, 2)], 0).astype(BF16)
    exchange((Q_ROW, Q_FRAME, Q_CORNER), Q_SPANS, hs, hr, (1, 16, 17))
    for k in range(1, HEADS):
        peer = head_peer(k)
        send(FINE, xs.at[peer[1]], xr.at[k], peer)
    pending.append((FINE, xr.at[pl.ds(1, HEADS - 1)]))
    xr[0] = xs[n]

    for t in range(2):
        for y in range(2):
            vs = []
            for j in range(4):
                a, b = (sets[2 * j + i][112 + t * 8:120 + t * 8] for i in range(2))
                if y == 0:
                    vs.append(jnp.where(row8 < 4, a, pltpu.roll(b, 4, 0)))
                else:
                    vs.append(jnp.where(row8 < 4, pltpu.roll(a, 4, 0), b))
            at = 128 + (t * 2 + y) * 32
            qgr[0, at:at + 32, :] = jnp.concatenate(vs, 0).astype(BF16)

    def layer_norm(pooled, lo, count, gain):
        lane = iota((count, 128), 1)
        centred = jnp.where(lane < HD, pooled - jnp.sum(pooled, 1, keepdims=True) * (1.0 / HD), 0.0)
        rstd = lax.rsqrt(jnp.sum(centred * centred, 1, keepdims=True) * (1.0 / HD) + 1e-6)
        unit = centred * rstd
        norm[0, lo:lo + count, :] = unit
        norm[1, lo:lo + count, :] = jnp.broadcast_to(rstd, (count, 128))
        return (unit * gain).astype(BF16)

    has_u = (u > 0).astype(F32)
    has_g = (group > 0).astype(F32)
    has_c = has_u * has_g

    def border(lo, count, has):
        return hr[lo:lo + count, :].astype(F32) * has

    exchanged((KV_ROW, KV_FRAME, KV_CORNER), KV_SPANS, hr)
    gain_kv = jnp.where(iota((32, 128), 0) < 16, gsc[1:2, :], gsc[2:3, :])
    gain_q = jnp.broadcast_to(gsc[0:1, :], (128, 128))
    kvg[0] = layer_norm(pkv(0, 0) + border(0, 32, has_u) + border(32, 32, has_g) + border(64, 32, has_c), 128, 32, gain_kv)
    for k in FAR_FIRST:
        send(GATHER, kvg.at[0], kvg.at[k], z_peer(k))
    pending.append((GATHER, kvg.at[pl.ds(1, ZS - 1)]))

    exchanged((Q_ROW, Q_FRAME, Q_CORNER), Q_SPANS, hr)
    q00 = pq(0, 0) + border(96, 32, has_u) + border(160, 32, has_g) + border(224, 32, has_c)
    q01 = pq(0, 1) + border(192, 32, has_g)
    q10 = pq(1, 0) + border(128, 32, has_u)
    qgr[0, 0:128, :] = layer_norm(jnp.concatenate([q00, q01, q10, pq(1, 1)], 0), 0, 128, gain_q)
    for k in (2, 3, 1):
        send(QUAD, qgr.at[0], qgr.at[k], quad_peer(k))
    pending.append((QUAD, qgr.at[pl.ds(1, 3)]))
    arrived(QUAD, qgr.at[pl.ds(1, 3)])
    arrived(GATHER, kvg.at[pl.ds(1, ZS - 1)])

    keys = kvg[:, 0:16, :].reshape(256, 128)
    values = kvg[:, 16:32, :].reshape(256, 128)
    queries = qgr[:, 0:128, :].reshape(512, 128)
    grads = qgr[:, 128:256, :].reshape(512, 128)
    nt = (((1,), (1,)), ((), ()))
    raised_ref[...] = jnp.exp(lax.dot_general(keys, queries, nt, preferred_element_type=F32) * SCALE)
    ga_ref[...] = lax.dot_general(values, grads, nt, preferred_element_type=F32)
    total = jnp.sum(raised_ref[...], 0, keepdims=True)
    delta = jnp.sum(raised_ref[...] * ga_ref[...], 0, keepdims=True)
    for j in range(4):
        st[0, j:j + 1, :] = total[:, j * 128:(j + 1) * 128]
        st[0, 4 + j:5 + j, :] = delta[:, j * 128:(j + 1) * 128]
    for k in (2, 3, 1):
        send(STATS, st.at[0], st.at[k], quad_peer(k))
    pending.append((STATS, st.at[pl.ds(1, 3)]))
    arrived(STATS, st.at[pl.ds(1, 3)])

    def quad_sum(at):
        outs = []
        for j in range(4):
            v = st[0, at + j:at + j + 1, :]
            for k in range(1, 4):
                i = at + (j ^ k)
                v = v + st[k, i:i + 1, :]
            outs.append(v)
        return jnp.concatenate(outs, 1)

    inverse = 1.0 / quad_sum(0)
    row_delta = quad_sum(4) * inverse
    attention = raised_ref[...] * inverse
    grad_scores = (attention * (ga_ref[...] - row_delta)).astype(BF16)
    grad_key = jnp.dot(grad_scores, queries, preferred_element_type=F32) * SCALE
    grad_value = jnp.dot(attention.astype(BF16), grads, preferred_element_type=F32)
    zb[:, 0:16, :] = grad_key.reshape(ZS, 16, 128).astype(BF16)
    zb[:, 16:32, :] = grad_value.reshape(ZS, 16, 128).astype(BF16)
    for k in FAR_FIRST:
        send(SCATTER, zb.at[k], zr.at[k], z_peer(ZS - k))
    pending.append((SCATTER, zr.at[pl.ds(1, ZS - 1)]))
    grad_query = lax.dot_general(grad_scores, keys, (((0,), (0,)), ((), ())), preferred_element_type=F32)
    dqb[...] = grad_query.reshape(4, 128, 128)
    for k in (2, 3, 1):
        send(DQ, dqb.at[k], dqr.at[k], quad_peer(k))
    pending.append((DQ, dqr.at[pl.ds(1, 3)]))
    zr[0] = zb[0]
    dqr[0] = dqb[0]

    def norm_backward(grad_normed, lo, count, gain):
        lane = iota((count, 128), 1)
        unit = norm[0, lo:lo + count, :]
        inner = grad_normed * gain
        mean_1 = jnp.sum(inner, 1, keepdims=True) * (1.0 / HD)
        mean_2 = jnp.sum(inner * unit, 1, keepdims=True) * (1.0 / HD)
        out = norm[1, lo:lo + count, :] * jnp.where(lane < HD, inner - mean_1 - unit * mean_2, 0.0)
        return out, grad_normed * unit

    arrived(DQ, dqr.at[pl.ds(1, 3)])
    dq = dqr[0] + dqr[1] + dqr[2] + dqr[3]
    gq, gain_rows = norm_backward(dq * SCALE + qgr[0, 128:256, :].astype(F32), 0, 128, gain_q)
    wg[80:88, :] = jnp.zeros((8, 128), F32)
    wg[81:82, :] = jnp.sum(gain_rows, 0, keepdims=True)
    hb[96:256, :] = jnp.concatenate([gq[0:32], gq[64:96], gq[0:64], gq[0:32]], 0).astype(BF16)
    exchange((BQ_ROW, BQ_FRAME, BQ_CORNER), Q_SPANS, hb, hbr, (-1, -16, -17))
    for i, grp in enumerate(OWN_Q):
        ge[grp * 32:grp * 32 + 32, :] = gq[i * 32:i * 32 + 32]

    arrived(FINE, xr.at[pl.ds(1, HEADS - 1)])
    for h in range(HEADS):
        xf[:, h * 8:h * 8 + 8, :] = xr[from_col[h]].astype(F32).reshape(48, 8, 128)

    arrived(SCATTER, zr.at[pl.ds(1, ZS - 1)])
    gkv, gain_rows = norm_backward(jnp.sum(zr[...].astype(F32), 0), 128, 32, gain_kv)
    wg[82:83, :] = jnp.sum(gain_rows[0:16], 0, keepdims=True)
    wg[83:84, :] = jnp.sum(gain_rows[16:32], 0, keepdims=True)
    hb[0:96, :] = jnp.concatenate([gkv, gkv, gkv], 0).astype(BF16)
    exchange((BK_ROW, BK_FRAME, BK_CORNER), KV_SPANS, hb, hbr, (-1, -16, -17))
    ge[288:304, :] = gkv[0:16]
    ge[352:368, :] = gkv[16:32]
    back_u = (u < ROW_GROUPS - 1).astype(F32)
    back_g = (group < SEQ // ROW_GROUPS - 1).astype(F32)
    back_c = back_u * back_g

    def returned(lo, count, has):
        return hbr[lo:lo + count, :].astype(F32) * has

    exchanged((BQ_ROW, BQ_FRAME, BQ_CORNER), Q_SPANS, hbr)
    ge[2 * 32:3 * 32, :] = returned(96, 32, back_u)
    ge[5 * 32:6 * 32, :] = returned(128, 32, back_u)
    ge[6 * 32:8 * 32, :] = returned(160, 64, back_g)
    ge[8 * 32:9 * 32, :] = returned(224, 32, back_c)

    def pairs(pair_list, a):
        return [(f, t) for t, entries in enumerate(pair_list) for f, tap in entries if tap == a]

    def spread(rows, cols, target):
        return jnp.where(iota((rows, cols), 1) == target, 1.0, 0.0).astype(BF16)

    r = iota((128, 32), 0)
    spread_q = spread(128, 32, ((r & 63) >> 1) + (r >> 6))
    spread_k = spread(64, 16, (iota((64, 16), 0) + 1) >> 2)
    row64 = iota((64, 128), 0)
    for grp in range(9):
        exh[grp * 128:grp * 128 + 128, :] = jnp.dot(spread_q, ge[grp * 32:grp * 32 + 32, :].astype(BF16),
                                                    preferred_element_type=F32)

    def tap_rows(masked, m, ab):
        for e, v in enumerate(masked):
            wg[m * 27 + ab * 3 + e:m * 27 + ab * 3 + e + 1, :] = jnp.sum(v, 0, keepdims=True)

    for a in range(3):
        for b in range(3):
            first = second = None
            for f, t in pairs(PAIRS_Q, a):
                for rr, y in pairs(PAIRS_Q, b):
                    v, at = xf[(f * 4 + rr) * 3], (t * 3 + y) * 128
                    t1, t2 = v * exh[at:at + 64, :], v * exh[at + 64:at + 128, :]
                    first = t1 if first is None else first + t1
                    second = t2 if second is None else second + t2
            tap_rows((jnp.where(row64 % 2 == 1, second, 0.0), jnp.where(row64 % 2 == 0, first, 0.0),
                      jnp.where(row64 % 2 == 1, first, 0.0)), 0, a * 3 + b)

    exchanged((BK_ROW, BK_FRAME, BK_CORNER), KV_SPANS, hbr)
    for lo, at, has in ((0, 16, back_u), (32, 32, back_g), (64, 48, back_c)):
        v = returned(lo, 32, has)
        ge[288 + at:304 + at, :] = v[0:16]
        ge[352 + at:368 + at, :] = v[16:32]
    for m in (1, 2):
        wide = [jnp.dot(spread_k, ge[at:at + 16, :].astype(BF16), preferred_element_type=F32)
                for at in range(224 + m * 64, 288 + m * 64, 16)]
        for a in range(3):
            for b in range(3):
                (f, t), = pairs(PAIRS_K, a)
                (rr, y), = pairs(PAIRS_K, b)
                v = xf[(f * 4 + rr) * 3 + m] * wide[t * 2 + y]
                tap_rows(tuple(jnp.where(row64 % 4 == c, v, 0.0) for c in (3, 0, 1)), m, a * 3 + b)

    t16, t8 = wg[64:80, :], wg[80:88, :]
    tail = jnp.concatenate([pltpu.roll(t16, 96, 1), pltpu.roll(t16, 64, 1), pltpu.roll(t16, 32, 1),
                            jnp.where(row8 < 4, pltpu.roll(t8, 96, 1), pltpu.roll(pltpu.roll(t8, 64, 1), 4, 0)),
                            pltpu.roll(t8, 32, 1)], 0)
    wb[...] = jnp.where(iota((64, 128), 1) < HD, wg[0:64, :], tail)

    def piece(k):
        return pl.ds(pl.multiple_of(quad_index(k) * 16, 16), 16)

    for k in (2, 3, 1):
        send(SUM_QUAD, wb.at[piece(k)], kr.at[k], quad_peer(k))
    pending.append((SUM_QUAD, kr.at[pl.ds(1, 3)]))
    kr[0] = wb[piece(0), :]

    zero = jnp.zeros((8, 128), F32)
    out_rows = [[] for _ in range(HEADS)]
    for grp in range(9):
        vs = [ge[grp * 32 + j * 8:grp * 32 + j * 8 + 8, :] for j in range(4)] + [zero]
        half = [pltpu.roll(v, 4, 0) for v in vs]
        for h in range(HEADS):
            j = h // 2
            out_rows[h].append(vs[j] if h % 2 == 0 else jnp.where(row8 < 4, half[j], half[j + 1]))
    for grp in range(4):
        vs = [[ge[at:at + 8, :] for at in (288 + m * 64 + grp * 16, 296 + m * 64 + grp * 16)] + [zero] for m in range(2)]
        for h in range(HEADS):
            j, i = h // 4, h % 4
            parts = []
            for m in range(2):
                v = pltpu.roll(vs[m][j], 8 - 2 * i, 0) if i else vs[m][j]
                if i == 3:
                    v = jnp.where(row8 < 2, v, pltpu.roll(vs[m][j + 1], 2, 0))
                parts.append(v)
            out_rows[h].append(jnp.where(row8 < 4, parts[0], pltpu.roll(parts[1], 4, 0)))
    for h in range(HEADS):
        sb2[h] = jnp.concatenate(out_rows[h] + [zero], 0).astype(BF16)
    for k in range(1, HEADS):
        peer = head_peer(k)
        send(A2A_B, sb2.at[peer[1]], rb2.at[k], peer)
    pending.append((A2A_B, rb2.at[pl.ds(1, HEADS - 1)]))
    rb2[0] = sb2[n]

    arrived(SUM_QUAD, kr.at[pl.ds(1, 3)])
    zs[0] = (kr[0] + kr[1] + kr[2] + kr[3]).astype(zs.dtype)
    for k in FAR_FIRST:
        send(SUM_Z, zs.at[0], zs.at[k], z_peer(k))
    pending.append((SUM_Z, zs.at[pl.ds(1, ZS - 1)]))

    arrived(A2A_B, rb2.at[pl.ds(1, HEADS - 1)])
    tiles = merge_heads([rb2[from_col[h]].astype(F32) for h in range(HEADS)])
    for j in range(6):
        gall[:, j * 128:(j + 1) * 128] = tiles[j].astype(BF16)
    r = iota((208, 112), 0)
    grp, late, i = r >> 4, (r >> 3) & 1, r & 7
    ex[...] = jnp.dot(spread(208, 112, grp * 8 + jnp.where(grp < 9, (i >> 1) + late, ((i + 1) >> 2) + 4 * late)),
                      gall[...], preferred_element_type=F32)

    def g_at(grp, late):
        at = grp * 16 + late * 8
        return ex[at:at + 8, :]

    def reached(pair_list, f):
        return [(t, a) for t, entries in enumerate(pair_list) for ff, a in entries if ff == f]

    for f in range(4):
        for rr in range(4):
            q_sum = None
            for t, a in reached(PAIRS_Q, f):
                for y, b in reached(PAIRS_Q, rr):
                    term = g_at(t * 3 + y, 0) * wt[0, a * 3 + b] + g_at(t * 3 + y, 1) * wt[1, a * 3 + b]
                    q_sum = term if q_sum is None else q_sum + term
            gxv[(f * 4 + rr) * 3] = q_sum.astype(BF16)
            for m in (1, 2):
                k_sum = jnp.zeros((8, 768), F32)
                for t, a in reached(PAIRS_K, f):
                    for y, b in reached(PAIRS_K, rr):
                        k_sum = g_at(9 + t * 2 + y, m - 1) * wt[1 + m, a * 3 + b]
                gxv[(f * 4 + rr) * 3 + m] = k_sum.astype(BF16)
    store = pltpu.make_async_copy(gxv, gx_ref, local.at[1])
    store.start()

    arrived(SUM_Z, zs.at[pl.ds(1, ZS - 1)])
    v = zs[z].astype(F32)
    for k in range(1, ZS):
        v = v + zs[lax.rem(z - k + ZS, ZS)].astype(F32)
    fr[0] = v
    for p in range(31, 0, -1):
        send(SPREAD, fr.at[0], fr.at[p], plane_peer(p))
    pending.append((SPREAD, fr.at[pl.ds(1, 31)]))
    arrived(SPREAD, fr.at[pl.ds(1, 31)])

    lane16 = iota((16, 128), 1)
    unpacked, gains = [], None
    for h in range(HEADS):
        at = [fr[lax.rem(yl + q // 2, 2) * (2 * HEADS) + lax.rem(core + q % 2, 2) * HEADS + from_col[h]] for q in range(4)]
        t16 = jnp.where(lane16 < 32, pltpu.roll(at[0], 32, 1), jnp.where(
            lane16 < 64, pltpu.roll(at[1], 64, 1), pltpu.roll(at[2], 96, 1)))
        lo, hi = at[3][0:8], at[3][8:16]
        t8 = jnp.where(lane8 < 32, pltpu.roll(lo, 32, 1), jnp.where(
            lane8 < 64, pltpu.roll(pltpu.roll(lo, 64, 1), 4, 0), pltpu.roll(hi, 96, 1)))
        gains = t8 if gains is None else gains + t8
        unpacked.append(jnp.concatenate(at + [t16, t8], 0))
    for j, v in enumerate(merge_heads(unpacked)):
        flat[j * 88:j * 88 + 88, :] = v
    for j in range(6):
        for m in range(3):
            gw_ref[m, :, j * 128:(j + 1) * 128] = flat[j * 88 + m * 27:j * 88 + m * 27 + 27, :]
    gg_ref[...] = gains[1:4, 0:HD]
    store.wait()
    drain()


def shards(qkv_fine, grad_out, pool_weight, norm_gain):
    x = qkv_fine[0].transpose(0, 1, 3, 2, 4).reshape(48, 8, 768)
    w = pool_weight.transpose(1, 0, 2)
    vmem = pl.BlockSpec(memory_space=pltpu.VMEM)
    hbm = pl.BlockSpec(memory_space=pl.ANY)
    scratch = [
        ((48, 8, 768), BF16),
        ((3, 27, 768), F32),
        ((4, 9, 8, 768), F32),
        ((8, 128, 128), BF16),
        ((8, 128, 128), BF16),
        ((8, 384, 128), BF16),
        ((8, 384, 128), BF16),
        ((48, 64, 128), F32),
        ((416, 128), F32),
        ((256, 128), BF16),
        ((256, 128), BF16),
        ((2, 160, 128), F32),
        ((ZS, 32, 128), BF16),
        ((4, 256, 128), BF16),
        ((256, 512), F32),
        ((256, 512), F32),
        ((4, 8, 128), F32),
        ((4, 128, 128), F32),
        ((4, 128, 128), F32),
        ((ZS, 32, 128), BF16),
        ((ZS, 32, 128), BF16),
        ((256, 128), BF16),
        ((256, 128), BF16),
        ((416, 128), F32),
        ((9 * 128, 128), F32),
        ((8, 112, 128), BF16),
        ((8, 112, 128), BF16),
        ((112, 768), BF16),
        ((208, 768), F32),
        ((48, 8, 768), BF16),
        ((88, 128), F32),
        ((64, 128), F32),
        ((4, 16, 128), F32),
        ((ZS, 16, 128), BF16),
        ((32, 16, 128), F32),
        ((6 * 88, 128), F32),
        ((8, 128), F32),
    ]
    gx, gw, gg = pl.pallas_call(
        kernel,
        out_shape=(jax.ShapeDtypeStruct(x.shape, BF16), jax.ShapeDtypeStruct(w.shape, F32),
                   jax.ShapeDtypeStruct(norm_gain.shape, F32)),
        in_specs=[hbm] + [vmem] * 3,
        out_specs=(hbm, vmem, vmem),
        scratch_shapes=[pltpu.VMEM(shape, kind) for shape, kind in scratch]
        + [pltpu.SemaphoreType.DMA((23,)), pltpu.SemaphoreType.DMA((23,)), pltpu.SemaphoreType.DMA((2,))],
        compiler_params=pltpu.CompilerParams(collective_id=0, has_side_effects=True,
                                             vmem_limit_bytes=60 * 1024 * 1024),
    )(x, grad_out[0], w, norm_gain)
    return gx.reshape(4, 4, 3, 8, 768).transpose(0, 1, 3, 2, 4)[None], gw.transpose(1, 0, 2), gg


def solution(mesh):
    in_specs = (P("seq", None, None, "head", None, None), P("seq", None, None, "head", None), P(), P())
    out_specs = (P("seq", None, None, "head", None, None), P(), P())
    return jax.shard_map(shards, mesh=mesh, in_specs=in_specs, out_specs=out_specs, check_vma=False)
```

```python
import jax
import jax.numpy as jnp
from jax import lax
from jax.experimental import pallas as pl
from jax.experimental.pallas import tpu as pltpu
from jax.sharding import PartitionSpec as P

MESH = pl.DeviceIdType.MESH
F32 = jnp.float32
BF16 = jnp.bfloat16
HD = 96
HEADS = 8
ROW_GROUPS = 16
SEQ = 64
ZS = 16
SCALE = HD ** -0.5

PAIRS_Q = (((0, 1), (1, 2)), ((1, 0), (2, 1), (3, 2)), ((3, 0),))
PAIRS_K = (((0, 1), (1, 2)), ((3, 0),))
OWN_Q = (0, 1, 3, 4)

(A2A_K, A2A_Q, FINE, KV_ROW, KV_FRAME, KV_CORNER, Q_ROW, Q_FRAME, Q_CORNER, GATHER, QUAD, STATS, DQ, SCATTER, BQ_ROW, BQ_FRAME,
 BQ_CORNER, BK_ROW, BK_FRAME, BK_CORNER, A2A_B, SUM_QUAD, SUM_Z, SPREAD) = range(24)
FAR_FIRST = (8, 7, 9, 6, 10, 5, 11, 4, 12, 3, 13, 2, 14, 1, 15)
KV_SPANS = ((0, 32), (32, 32), (64, 32))
Q_SPANS = ((96, 64), (160, 64), (224, 32))


def iota(shape, dim):
    return lax.broadcasted_iota(jnp.int32, shape, dim)


def up(x, by):
    size = x.shape[0]
    return pltpu.roll(x, (size - by) % size, 0)


def split_heads(tiles):
    lane = iota(tiles[0].shape, 1)
    heads = []
    for n in range(HEADS):
        t = tiles[n // 4 * 3:n // 4 * 3 + 3]
        if n % 4 == 0:
            v = t[0]
        elif n % 4 == 1:
            v = jnp.where(lane < 32, pltpu.roll(t[0], 32, 1), pltpu.roll(t[1], 32, 1))
        elif n % 4 == 2:
            v = jnp.where(lane < 64, pltpu.roll(t[1], 64, 1), pltpu.roll(t[2], 64, 1))
        else:
            v = pltpu.roll(t[2], 96, 1)
        heads.append(jnp.where(lane < HD, v, 0.0))
    return heads


def merge_heads(h):
    lane = iota(h[0].shape, 1)
    tiles = []
    for half in (0, 4):
        a, b, c, d = h[half:half + 4]
        tiles.append(jnp.where(lane < 96, a, pltpu.roll(b, 96, 1)))
        tiles.append(jnp.where(lane < 64, pltpu.roll(b, 96, 1), pltpu.roll(c, 64, 1)))
        tiles.append(jnp.where(lane < 32, pltpu.roll(c, 64, 1), pltpu.roll(d, 32, 1)))
    return tiles


def tiles_of(v):
    return [v[:, j * 128:(j + 1) * 128] for j in range(6)]


def kernel(x_ref, g_ref, w_ref, gain_ref, gx_ref, gw_ref, gg_ref,
           xv, wf, wt, sbk, rbk, sbq, rbq, xs, xr, xf, pe, hs, hr, norm, kvg, qgr, raised_ref, ga_ref, st, dqb, dqr, zb, zr,
           hb, hbr, ge, exh, sb2, rb2, gall, ex, gxv, wg, wb, kr, zs, fr, flat, gsc, ss, rs, local):
    s = lax.axis_index("seq")
    n = lax.axis_index("head")
    group, u = s // ROW_GROUPS, s % ROW_GROUPS
    yl, z, core = s // (2 * ZS), s // 2 % ZS, s % 2

    load = pltpu.make_async_copy(x_ref, xv, local.at[0])
    load.start()

    def head_peer(k):
        return (s, lax.rem(n + k, HEADS))

    def z_peer(k):
        return (yl * (2 * ZS) + lax.rem(z + k, ZS) * 2 + core, n)

    def quad_peer(k):
        return (lax.rem(yl + k // 2, 2) * (2 * ZS) + z * 2 + lax.rem(core + k % 2, 2), n)

    def quad_index(k):
        return lax.rem(yl + k // 2, 2) * 2 + lax.rem(core + k % 2, 2)

    def plane_peer(p):
        return (quad_peer(p // HEADS)[0], lax.rem(n + p % HEADS, HEADS))

    def seq_peer(d):
        return (lax.rem(s + d + SEQ, SEQ), n)

    barrier = pltpu.get_barrier_semaphore()
    greeted = [seq_peer(d) for d in (16, 17, -16, -17)] + [z_peer(k) for k in FAR_FIRST]
    greeted += [seq_peer(1), seq_peer(-1)] + [quad_peer(k) for k in (3, 2, 1)] + [head_peer(k) for k in range(1, HEADS)]
    for peer in greeted:
        pl.semaphore_signal(barrier, inc=1, device_id=peer, device_id_type=MESH)

    def send(stage, src, dst, peer):
        pltpu.make_async_remote_copy(src_ref=src, dst_ref=dst, send_sem=ss.at[stage], recv_sem=rs.at[stage],
                                     device_id=peer, device_id_type=MESH).start()

    def arrived(stage, ref):
        pltpu.make_async_copy(ref, ref, rs.at[stage]).wait()

    pending = []

    def drain():
        for stage, ref in pending:
            pltpu.make_async_copy(ref, ref, ss.at[stage]).wait()

    row = iota((8, 768), 0)
    row8 = iota((8, 128), 0)
    lane8 = iota((8, 128), 1)
    wf[...] = w_ref[...].astype(F32)

    def taps(ab, carry):
        def one(m, e):
            return jnp.broadcast_to(wf[m, pl.ds(ab * 3 + e, 1), :], (8, 768))
        wt[0, ab] = jnp.where(row % 2 == 0, one(0, 1), one(0, 2))
        wt[1, ab] = jnp.where(row % 2 == 1, one(0, 0), 0.0)
        for m in (1, 2):
            wt[1 + m, ab] = jnp.where(row % 4 == 0, one(m, 1), jnp.where(
                row % 4 == 1, one(m, 2), jnp.where(row % 4 == 3, one(m, 0), 0.0)))
        return carry
    lax.fori_loop(0, 9, taps, 0)
    gsc[...] = jnp.zeros_like(gsc)
    gsc[0:3, 0:HD] = gain_ref[...]
    load.wait()

    def fine(m, f, r):
        return xv[(f * 4 + r) * 3 + m].astype(F32)

    def store_heads(dst, groups):
        for p in range(len(groups) // 2):
            v = jnp.concatenate(groups[2 * p:2 * p + 2], 0)
            for h, part in enumerate(split_heads(tiles_of(v))):
                dst[h, p * 16:p * 16 + 16, :] = part.astype(BF16)

    groups = []
    for t in range(2):
        for y in range(2):
            both = []
            for m in (1, 2):
                k_sum = None
                for f, a in PAIRS_K[t]:
                    for r, b in PAIRS_K[y]:
                        tk = fine(m, f, r) * wt[1 + m, a * 3 + b]
                        k_sum = tk if k_sum is None else k_sum + tk
                t1 = k_sum + up(k_sum, 1)
                both.append(jnp.where(row == 0, t1, jnp.where(row == 1, up(t1, 2) + up(k_sum, 4), jnp.where(
                    row == 2, up(k_sum, 5), 0.0))))
            groups.append(both[0] + pltpu.roll(both[1], 4, 0))
    store_heads(sbk, groups)
    groups = []
    for t in range(3):
        for y in range(3):
            a_sum = b_sum = None
            for f, a in PAIRS_Q[t]:
                for r, b in PAIRS_Q[y]:
                    v = fine(0, f, r)
                    ta, tb = v * wt[0, a * 3 + b], v * wt[1, a * 3 + b]
                    a_sum = ta if a_sum is None else a_sum + ta
                    b_sum = tb if b_sum is None else b_sum + tb
            b1 = pltpu.roll(b_sum, 1, 0)
            e = a_sum + up(a_sum, 1) + jnp.where(row == 0, 0.0, b1)
            v = jnp.where(row == 0, e, jnp.where(row == 1, up(e, 1), jnp.where(row == 2, up(e, 2), jnp.where(
                row == 3, up(e, 3), jnp.where(row == 4, up(b1, 4), 0.0)))))
            groups.append(v)
    groups.append(jnp.zeros((8, 768), F32))
    for t in range(2):
        groups.append(jnp.concatenate([g_ref[t, 0].astype(F32), g_ref[t, 1].astype(F32)], 0))
    store_heads(sbq, groups)

    def split_fine(p, carry):
        v = jnp.concatenate([xv[2 * p].astype(F32), xv[2 * p + 1].astype(F32)], 0)
        for h, part in enumerate(split_heads(tiles_of(v))):
            xs[h, pl.ds(pl.multiple_of(p * 16, 16), 16), :] = part.astype(BF16)
        return carry
    lax.fori_loop(0, 24, split_fine, 0)

    pl.semaphore_wait(barrier, len(greeted))
    for stage, src, dst in ((A2A_K, sbk, rbk), (A2A_Q, sbq, rbq)):
        for k in (4, 5, 3, 7, 1, 2, 6):
            peer = head_peer(k)
            send(stage, src.at[peer[1]], dst.at[k], peer)
        pending.append((stage, dst.at[pl.ds(1, HEADS - 1)]))
        dst[0] = src[n]
    arrived(A2A_K, rbk.at[pl.ds(1, HEADS - 1)])

    from_col = [lax.rem(n - h + HEADS, HEADS) for h in range(HEADS)]
    sets = [rbk[from_col[h]].astype(F32) for h in range(HEADS)]
    for grp in range(4):
        parts = [v[grp * 8:grp * 8 + 8] for v in sets]
        for m in range(2):
            if m == 0:
                own = [jnp.where(row8 < 4, p, 0.0) for p in parts]
            else:
                own = [pltpu.roll(jnp.where(row8 >= 4, p, 0.0), 4, 0) for p in parts]
            last = [pltpu.roll(own[4 * j + 3], 6, 0) for j in range(2)]
            for j in range(2):
                v = own[4 * j] + pltpu.roll(own[4 * j + 1], 2, 0) + pltpu.roll(own[4 * j + 2], 4, 0)
                v = v + jnp.where(row8 >= 4, last[j], 0.0)
                if j:
                    v = v + jnp.where(row8 == 0, last[0], 0.0)
                at = 288 + m * 64 + grp * 16 + j * 8
                pe[at:at + 8, :] = v

    def pq(t, y):
        return pe[(t * 3 + y) * 32:(t * 3 + y) * 32 + 32, :]

    def pkv(t, y):
        at = 288 + (t * 2 + y) * 16
        return jnp.concatenate([pe[at:at + 16, :], pe[at + 64:at + 80, :]], 0)

    def exchange(stages, spans, src, dst, distances):
        for stage, (lo, count), d in zip(stages, spans, distances):
            send(stage, src.at[pl.ds(lo, count)], dst.at[pl.ds(lo, count)], seq_peer(d))
            pending.append((stage, dst.at[pl.ds(lo, count)]))

    def exchanged(stages, spans, dst):
        for stage, (lo, count) in zip(stages, spans):
            arrived(stage, dst.at[pl.ds(lo, count)])

    hs[0:96, :] = jnp.concatenate([pkv(0, 1), pkv(1, 0), pkv(1, 1)], 0).astype(BF16)
    exchange((KV_ROW, KV_FRAME, KV_CORNER), KV_SPANS, hs, hr, (1, 16, 17))
    arrived(A2A_Q, rbq.at[pl.ds(1, HEADS - 1)])
    sets = [rbq[from_col[h]].astype(F32) for h in range(HEADS)]
    for grp in range(9):
        parts = [v[grp * 8:grp * 8 + 8] for v in sets]
        rolled = [pltpu.roll(parts[2 * j + 1], 4, 0) for j in range(4)]
        for j in range(4):
            v = parts[2 * j] + jnp.where(row8 >= 4, rolled[j], 0.0)
            if j:
                v = v + jnp.where(row8 == 0, rolled[j - 1], 0.0)
            pe[grp * 32 + j * 8:grp * 32 + j * 8 + 8, :] = v
    hs[96:256, :] = jnp.concatenate([pq(0, 2), pq(1, 2), pq(2, 0), pq(2, 1), pq(2, 2)], 0).astype(BF16)
    exchange((Q_ROW, Q_FRAME, Q_CORNER), Q_SPANS, hs, hr, (1, 16, 17))
    for k in range(1, HEADS):
        peer = head_peer(k)
        send(FINE, xs.at[peer[1]], xr.at[k], peer)
    pending.append((FINE, xr.at[pl.ds(1, HEADS - 1)]))
    xr[0] = xs[n]

    for t in range(2):
        for y in range(2):
            vs = []
            for j in range(4):
                a, b = (sets[2 * j + i][80 + t * 8:88 + t * 8] for i in range(2))
                if y == 0:
                    vs.append(jnp.where(row8 < 4, a, pltpu.roll(b, 4, 0)))
                else:
                    vs.append(jnp.where(row8 < 4, pltpu.roll(a, 4, 0), b))
            at = 128 + (t * 2 + y) * 32
            qgr[0, at:at + 32, :] = jnp.concatenate(vs, 0).astype(BF16)

    def layer_norm(pooled, lo, count, gain):
        lane = iota((count, 128), 1)
        centred = jnp.where(lane < HD, pooled - jnp.sum(pooled, 1, keepdims=True) * (1.0 / HD), 0.0)
        rstd = lax.rsqrt(jnp.sum(centred * centred, 1, keepdims=True) * (1.0 / HD) + 1e-6)
        unit = centred * rstd
        norm[0, lo:lo + count, :] = unit
        norm[1, lo:lo + count, :] = jnp.broadcast_to(rstd, (count, 128))
        return (unit * gain).astype(BF16)

    has_u = (u > 0).astype(F32)
    has_g = (group > 0).astype(F32)
    has_c = has_u * has_g

    def border(lo, count, has):
        return hr[lo:lo + count, :].astype(F32) * has

    exchanged((KV_ROW, KV_FRAME, KV_CORNER), KV_SPANS, hr)
    gain_kv = jnp.where(iota((32, 128), 0) < 16, gsc[1:2, :], gsc[2:3, :])
    gain_q = jnp.broadcast_to(gsc[0:1, :], (128, 128))
    kvg[0] = layer_norm(pkv(0, 0) + border(0, 32, has_u) + border(32, 32, has_g) + border(64, 32, has_c), 128, 32, gain_kv)
    for k in FAR_FIRST:
        send(GATHER, kvg.at[0], kvg.at[k], z_peer(k))
    pending.append((GATHER, kvg.at[pl.ds(1, ZS - 1)]))

    exchanged((Q_ROW, Q_FRAME, Q_CORNER), Q_SPANS, hr)
    q00 = pq(0, 0) + border(96, 32, has_u) + border(160, 32, has_g) + border(224, 32, has_c)
    q01 = pq(0, 1) + border(192, 32, has_g)
    q10 = pq(1, 0) + border(128, 32, has_u)
    qgr[0, 0:128, :] = layer_norm(jnp.concatenate([q00, q01, q10, pq(1, 1)], 0), 0, 128, gain_q)
    for k in (2, 3, 1):
        send(QUAD, qgr.at[0], qgr.at[k], quad_peer(k))
    pending.append((QUAD, qgr.at[pl.ds(1, 3)]))
    arrived(QUAD, qgr.at[pl.ds(1, 3)])
    arrived(GATHER, kvg.at[pl.ds(1, ZS - 1)])

    keys = kvg[:, 0:16, :].reshape(256, 128)
    values = kvg[:, 16:32, :].reshape(256, 128)
    queries = qgr[:, 0:128, :].reshape(512, 128)
    grads = qgr[:, 128:256, :].reshape(512, 128)
    nt = (((1,), (1,)), ((), ()))
    raised_ref[...] = jnp.exp(lax.dot_general(keys, queries, nt, preferred_element_type=F32) * SCALE)
    ga_ref[...] = lax.dot_general(values, grads, nt, preferred_element_type=F32)
    total = jnp.sum(raised_ref[...], 0, keepdims=True)
    delta = jnp.sum(raised_ref[...] * ga_ref[...], 0, keepdims=True)
    for j in range(4):
        st[0, j:j + 1, :] = total[:, j * 128:(j + 1) * 128]
        st[0, 4 + j:5 + j, :] = delta[:, j * 128:(j + 1) * 128]
    for k in (2, 3, 1):
        send(STATS, st.at[0], st.at[k], quad_peer(k))
    pending.append((STATS, st.at[pl.ds(1, 3)]))
    arrived(STATS, st.at[pl.ds(1, 3)])

    def quad_sum(at):
        outs = []
        for j in range(4):
            v = st[0, at + j:at + j + 1, :]
            for k in range(1, 4):
                i = at + (j ^ k)
                v = v + st[k, i:i + 1, :]
            outs.append(v)
        return jnp.concatenate(outs, 1)

    inverse = 1.0 / quad_sum(0)
    row_delta = quad_sum(4) * inverse
    attention = raised_ref[...] * inverse
    grad_scores = (attention * (ga_ref[...] - row_delta)).astype(BF16)
    grad_key = jnp.dot(grad_scores, queries, preferred_element_type=F32) * SCALE
    grad_value = jnp.dot(attention.astype(BF16), grads, preferred_element_type=F32)
    zb[:, 0:16, :] = grad_key.reshape(ZS, 16, 128).astype(BF16)
    zb[:, 16:32, :] = grad_value.reshape(ZS, 16, 128).astype(BF16)
    for k in FAR_FIRST:
        send(SCATTER, zb.at[k], zr.at[k], z_peer(ZS - k))
    pending.append((SCATTER, zr.at[pl.ds(1, ZS - 1)]))
    grad_query = lax.dot_general(grad_scores, keys, (((0,), (0,)), ((), ())), preferred_element_type=F32)
    dqb[...] = grad_query.reshape(4, 128, 128)
    for k in (2, 3, 1):
        send(DQ, dqb.at[k], dqr.at[k], quad_peer(k))
    pending.append((DQ, dqr.at[pl.ds(1, 3)]))
    zr[0] = zb[0]
    dqr[0] = dqb[0]

    def norm_backward(grad_normed, lo, count, gain):
        lane = iota((count, 128), 1)
        unit = norm[0, lo:lo + count, :]
        inner = grad_normed * gain
        mean_1 = jnp.sum(inner, 1, keepdims=True) * (1.0 / HD)
        mean_2 = jnp.sum(inner * unit, 1, keepdims=True) * (1.0 / HD)
        out = norm[1, lo:lo + count, :] * jnp.where(lane < HD, inner - mean_1 - unit * mean_2, 0.0)
        return out, grad_normed * unit

    arrived(DQ, dqr.at[pl.ds(1, 3)])
    dq = dqr[0] + dqr[1] + dqr[2] + dqr[3]
    gq, gain_rows = norm_backward(dq * SCALE + qgr[0, 128:256, :].astype(F32), 0, 128, gain_q)
    wg[80:88, :] = jnp.zeros((8, 128), F32)
    wg[81:82, :] = jnp.sum(gain_rows, 0, keepdims=True)
    hb[96:256, :] = jnp.concatenate([gq[0:32], gq[64:96], gq[0:64], gq[0:32]], 0).astype(BF16)
    exchange((BQ_ROW, BQ_FRAME, BQ_CORNER), Q_SPANS, hb, hbr, (-1, -16, -17))
    for i, grp in enumerate(OWN_Q):
        ge[grp * 32:grp * 32 + 32, :] = gq[i * 32:i * 32 + 32]

    arrived(FINE, xr.at[pl.ds(1, HEADS - 1)])
    for h in range(HEADS):
        xf[:, h * 8:h * 8 + 8, :] = xr[from_col[h]].astype(F32).reshape(48, 8, 128)

    arrived(SCATTER, zr.at[pl.ds(1, ZS - 1)])
    gkv, gain_rows = norm_backward(jnp.sum(zr[...].astype(F32), 0), 128, 32, gain_kv)
    wg[82:83, :] = jnp.sum(gain_rows[0:16], 0, keepdims=True)
    wg[83:84, :] = jnp.sum(gain_rows[16:32], 0, keepdims=True)
    hb[0:96, :] = jnp.concatenate([gkv, gkv, gkv], 0).astype(BF16)
    exchange((BK_ROW, BK_FRAME, BK_CORNER), KV_SPANS, hb, hbr, (-1, -16, -17))
    ge[288:304, :] = gkv[0:16]
    ge[352:368, :] = gkv[16:32]
    back_u = (u < ROW_GROUPS - 1).astype(F32)
    back_g = (group < SEQ // ROW_GROUPS - 1).astype(F32)
    back_c = back_u * back_g

    def returned(lo, count, has):
        return hbr[lo:lo + count, :].astype(F32) * has

    exchanged((BQ_ROW, BQ_FRAME, BQ_CORNER), Q_SPANS, hbr)
    ge[2 * 32:3 * 32, :] = returned(96, 32, back_u)
    ge[5 * 32:6 * 32, :] = returned(128, 32, back_u)
    ge[6 * 32:8 * 32, :] = returned(160, 64, back_g)
    ge[8 * 32:9 * 32, :] = returned(224, 32, back_c)

    def pairs(pair_list, a):
        return [(f, t) for t, entries in enumerate(pair_list) for f, tap in entries if tap == a]

    def spread(rows, cols, target):
        return jnp.where(iota((rows, cols), 1) == target, 1.0, 0.0).astype(BF16)

    r = iota((128, 32), 0)
    spread_q = spread(128, 32, ((r & 63) >> 1) + (r >> 6))
    spread_k = spread(64, 16, (iota((64, 16), 0) + 1) >> 2)
    row64 = iota((64, 128), 0)
    for grp in range(9):
        exh[grp * 128:grp * 128 + 128, :] = jnp.dot(spread_q, ge[grp * 32:grp * 32 + 32, :].astype(BF16),
                                                    preferred_element_type=F32)

    def tap_rows(masked, m, ab):
        for e, v in enumerate(masked):
            wg[m * 27 + ab * 3 + e:m * 27 + ab * 3 + e + 1, :] = jnp.sum(v, 0, keepdims=True)

    for a in range(3):
        for b in range(3):
            first = second = None
            for f, t in pairs(PAIRS_Q, a):
                for rr, y in pairs(PAIRS_Q, b):
                    v, at = xf[(f * 4 + rr) * 3], (t * 3 + y) * 128
                    t1, t2 = v * exh[at:at + 64, :], v * exh[at + 64:at + 128, :]
                    first = t1 if first is None else first + t1
                    second = t2 if second is None else second + t2
            tap_rows((jnp.where(row64 % 2 == 1, second, 0.0), jnp.where(row64 % 2 == 0, first, 0.0),
                      jnp.where(row64 % 2 == 1, first, 0.0)), 0, a * 3 + b)

    def key_taps(m, wide, chosen):
        for a, b in chosen:
            (f, t), = pairs(PAIRS_K, a)
            (rr, y), = pairs(PAIRS_K, b)
            v = xf[(f * 4 + rr) * 3 + m] * wide[t * 2 + y]
            tap_rows(tuple(jnp.where(row64 % 4 == c, v, 0.0) for c in (3, 0, 1)), m, a * 3 + b)

    def wide_key(m, group):
        at = 224 + m * 64 + group * 16
        return jnp.dot(spread_k, ge[at:at + 16, :].astype(BF16), preferred_element_type=F32)

    for m in (1, 2):
        key_taps(m, (wide_key(m, 0),), ((1, 1), (1, 2), (2, 1), (2, 2)))
    exchanged((BK_ROW, BK_FRAME, BK_CORNER), KV_SPANS, hbr)
    for lo, at, has in ((0, 16, back_u), (32, 32, back_g), (64, 48, back_c)):
        v = returned(lo, 32, has)
        ge[288 + at:304 + at, :] = v[0:16]
        ge[352 + at:368 + at, :] = v[16:32]
    for m in (1, 2):
        key_taps(m, (None,) + tuple(wide_key(m, group) for group in (1, 2, 3)), ((0, 0), (0, 1), (0, 2), (1, 0), (2, 0)))

    t16, t8 = wg[64:80, :], wg[80:88, :]
    tail = jnp.concatenate([pltpu.roll(t16, 96, 1), pltpu.roll(t16, 64, 1), pltpu.roll(t16, 32, 1),
                            jnp.where(row8 < 4, pltpu.roll(t8, 96, 1), pltpu.roll(pltpu.roll(t8, 64, 1), 4, 0)),
                            pltpu.roll(t8, 32, 1)], 0)
    wb[...] = jnp.where(iota((64, 128), 1) < HD, wg[0:64, :], tail)

    def piece(k):
        return pl.ds(pl.multiple_of(quad_index(k) * 16, 16), 16)

    for k in (2, 3, 1):
        send(SUM_QUAD, wb.at[piece(k)], kr.at[k], quad_peer(k))
    pending.append((SUM_QUAD, kr.at[pl.ds(1, 3)]))
    kr[0] = wb[piece(0), :]

    zero = jnp.zeros((8, 128), F32)
    out_rows = [[] for _ in range(HEADS)]
    for grp in range(9):
        vs = [ge[grp * 32 + j * 8:grp * 32 + j * 8 + 8, :] for j in range(4)] + [zero]
        half = [pltpu.roll(v, 4, 0) for v in vs]
        for h in range(HEADS):
            j = h // 2
            out_rows[h].append(vs[j] if h % 2 == 0 else jnp.where(row8 < 4, half[j], half[j + 1]))
    for grp in range(4):
        vs = [[ge[at:at + 8, :] for at in (288 + m * 64 + grp * 16, 296 + m * 64 + grp * 16)] + [zero] for m in range(2)]
        for h in range(HEADS):
            j, i = h // 4, h % 4
            parts = []
            for m in range(2):
                v = pltpu.roll(vs[m][j], 8 - 2 * i, 0) if i else vs[m][j]
                if i == 3:
                    v = jnp.where(row8 < 2, v, pltpu.roll(vs[m][j + 1], 2, 0))
                parts.append(v)
            out_rows[h].append(jnp.where(row8 < 4, parts[0], pltpu.roll(parts[1], 4, 0)))
    for h in range(HEADS):
        sb2[h] = jnp.concatenate(out_rows[h] + [zero], 0).astype(BF16)
    for k in range(1, HEADS):
        peer = head_peer(k)
        send(A2A_B, sb2.at[peer[1]], rb2.at[k], peer)
    pending.append((A2A_B, rb2.at[pl.ds(1, HEADS - 1)]))
    rb2[0] = sb2[n]

    arrived(SUM_QUAD, kr.at[pl.ds(1, 3)])
    zs[0] = (kr[0] + kr[1] + kr[2] + kr[3]).astype(zs.dtype)
    for k in FAR_FIRST:
        send(SUM_Z, zs.at[0], zs.at[k], z_peer(k))
    pending.append((SUM_Z, zs.at[pl.ds(1, ZS - 1)]))

    arrived(A2A_B, rb2.at[pl.ds(1, HEADS - 1)])
    tiles = merge_heads([rb2[from_col[h]].astype(F32) for h in range(HEADS)])
    for j in range(6):
        gall[:, j * 128:(j + 1) * 128] = tiles[j].astype(BF16)
    r = iota((208, 112), 0)
    grp, late, i = r >> 4, (r >> 3) & 1, r & 7
    ex[...] = jnp.dot(spread(208, 112, grp * 8 + jnp.where(grp < 9, (i >> 1) + late, ((i + 1) >> 2) + 4 * late)),
                      gall[...], preferred_element_type=F32)

    def g_at(grp, late):
        at = grp * 16 + late * 8
        return ex[at:at + 8, :]

    def reached(pair_list, f):
        return [(t, a) for t, entries in enumerate(pair_list) for ff, a in entries if ff == f]

    for f in range(4):
        for rr in range(4):
            q_sum = None
            for t, a in reached(PAIRS_Q, f):
                for y, b in reached(PAIRS_Q, rr):
                    term = g_at(t * 3 + y, 0) * wt[0, a * 3 + b] + g_at(t * 3 + y, 1) * wt[1, a * 3 + b]
                    q_sum = term if q_sum is None else q_sum + term
            gxv[(f * 4 + rr) * 3] = q_sum.astype(BF16)
            for m in (1, 2):
                k_sum = jnp.zeros((8, 768), F32)
                for t, a in reached(PAIRS_K, f):
                    for y, b in reached(PAIRS_K, rr):
                        k_sum = g_at(9 + t * 2 + y, m - 1) * wt[1 + m, a * 3 + b]
                gxv[(f * 4 + rr) * 3 + m] = k_sum.astype(BF16)
    store = pltpu.make_async_copy(gxv, gx_ref, local.at[1])
    store.start()

    arrived(SUM_Z, zs.at[pl.ds(1, ZS - 1)])
    v = zs[z].astype(F32)
    for k in range(1, ZS):
        v = v + zs[lax.rem(z - k + ZS, ZS)].astype(F32)
    fr[0] = v.astype(BF16)
    for p in range(31, 0, -1):
        send(SPREAD, fr.at[0], fr.at[p], plane_peer(p))
    pending.append((SPREAD, fr.at[pl.ds(1, 31)]))
    arrived(SPREAD, fr.at[pl.ds(1, 31)])

    lane16 = iota((16, 128), 1)
    unpacked, gains = [], None
    for h in range(HEADS):
        at = [fr[lax.rem(yl + q // 2, 2) * (2 * HEADS) + lax.rem(core + q % 2, 2) * HEADS + from_col[h]].astype(F32) for q in range(4)]
        t16 = jnp.where(lane16 < 32, pltpu.roll(at[0], 32, 1), jnp.where(
            lane16 < 64, pltpu.roll(at[1], 64, 1), pltpu.roll(at[2], 96, 1)))
        lo, hi = at[3][0:8], at[3][8:16]
        t8 = jnp.where(lane8 < 32, pltpu.roll(lo, 32, 1), jnp.where(
            lane8 < 64, pltpu.roll(pltpu.roll(lo, 64, 1), 4, 0), pltpu.roll(hi, 96, 1)))
        gains = t8 if gains is None else gains + t8
        unpacked.append(jnp.concatenate(at + [t16, t8], 0))
    for j, v in enumerate(merge_heads(unpacked)):
        flat[j * 88:j * 88 + 88, :] = v
    for j in range(6):
        for m in range(3):
            gw_ref[m, :, j * 128:(j + 1) * 128] = flat[j * 88 + m * 27:j * 88 + m * 27 + 27, :]
    gg_ref[...] = gains[1:4, 0:HD]
    store.wait()
    drain()


def shards(qkv_fine, grad_out, pool_weight, norm_gain):
    x = qkv_fine[0].transpose(0, 1, 3, 2, 4).reshape(48, 8, 768)
    w = pool_weight.transpose(1, 0, 2)
    vmem = pl.BlockSpec(memory_space=pltpu.VMEM)
    hbm = pl.BlockSpec(memory_space=pl.ANY)
    scratch = [
        ((48, 8, 768), BF16),
        ((3, 27, 768), F32),
        ((4, 9, 8, 768), F32),
        ((8, 32, 128), BF16),
        ((8, 32, 128), BF16),
        ((8, 96, 128), BF16),
        ((8, 96, 128), BF16),
        ((8, 384, 128), BF16),
        ((8, 384, 128), BF16),
        ((48, 64, 128), F32),
        ((416, 128), F32),
        ((256, 128), BF16),
        ((256, 128), BF16),
        ((2, 160, 128), F32),
        ((ZS, 32, 128), BF16),
        ((4, 256, 128), BF16),
        ((256, 512), F32),
        ((256, 512), F32),
        ((4, 8, 128), F32),
        ((4, 128, 128), F32),
        ((4, 128, 128), F32),
        ((ZS, 32, 128), BF16),
        ((ZS, 32, 128), BF16),
        ((256, 128), BF16),
        ((256, 128), BF16),
        ((416, 128), F32),
        ((9 * 128, 128), F32),
        ((8, 112, 128), BF16),
        ((8, 112, 128), BF16),
        ((112, 768), BF16),
        ((208, 768), F32),
        ((48, 8, 768), BF16),
        ((88, 128), F32),
        ((64, 128), F32),
        ((4, 16, 128), F32),
        ((ZS, 16, 128), BF16),
        ((32, 16, 128), BF16),
        ((6 * 88, 128), F32),
        ((8, 128), F32),
    ]
    gx, gw, gg = pl.pallas_call(
        kernel,
        out_shape=(jax.ShapeDtypeStruct(x.shape, BF16), jax.ShapeDtypeStruct(w.shape, F32),
                   jax.ShapeDtypeStruct(norm_gain.shape, F32)),
        in_specs=[hbm] + [vmem] * 3,
        out_specs=(hbm, vmem, vmem),
        scratch_shapes=[pltpu.VMEM(shape, kind) for shape, kind in scratch]
        + [pltpu.SemaphoreType.DMA((24,)), pltpu.SemaphoreType.DMA((24,)), pltpu.SemaphoreType.DMA((2,))],
        compiler_params=pltpu.CompilerParams(collective_id=0, has_side_effects=True,
                                             vmem_limit_bytes=60 * 1024 * 1024),
    )(x, grad_out[0], w, norm_gain)
    return gx.reshape(4, 4, 3, 8, 768).transpose(0, 1, 3, 2, 4)[None], gw.transpose(1, 0, 2), gg


def solution(mesh):
    in_specs = (P("seq", None, None, "head", None, None), P("seq", None, None, "head", None), P(), P())
    out_specs = (P("seq", None, None, "head", None, None), P(), P())
    return jax.shard_map(shards, mesh=mesh, in_specs=in_specs, out_specs=out_specs, check_vma=False)
```

```python
import jax
import jax.numpy as jnp
from jax import lax
from jax.experimental import pallas as pl
from jax.experimental.pallas import tpu as pltpu
from jax.sharding import PartitionSpec as P

MESH = pl.DeviceIdType.MESH
F32 = jnp.float32
BF16 = jnp.bfloat16
HD = 96
HEADS = 8
ROW_GROUPS = 16
SEQ = 64
ZS = 16
SCALE = HD ** -0.5

PAIRS_Q = (((0, 1), (1, 2)), ((1, 0), (2, 1), (3, 2)), ((3, 0),))
PAIRS_K = (((0, 1), (1, 2)), ((3, 0),))
OWN_Q = (0, 1, 3, 4)

(A2A_K, A2A_Q, FINE, KV_OWN, KV_ROW, KV_FRAME, KV_CORNER, Q_ROW, Q_FRAME, Q_CORNER, GATHER, QUAD, STATS, DQ, SCATTER,
 BQ_ROW, BQ_FRAME, BQ_CORNER, BK_OWN, BK_ROW, BK_FRAME, BK_CORNER, A2A_B, SUM_QUAD, SUM_Z, SPREAD) = range(26)
FAR_FIRST = (8, 7, 9, 6, 10, 5, 11, 4, 12, 3, 13, 2, 14, 1, 15)
KV_SPANS = ((0, 32), (32, 32), (64, 32), (96, 32))
Q_SPANS = ((128, 64), (192, 64), (256, 32))
HALF_WAY = 12


def iota(shape, dim):
    return lax.broadcasted_iota(jnp.int32, shape, dim)


def up(x, by):
    size = x.shape[0]
    return pltpu.roll(x, (size - by) % size, 0)


def split_heads(tiles):
    lane = iota(tiles[0].shape, 1)
    heads = []
    for n in range(HEADS):
        t = tiles[n // 4 * 3:n // 4 * 3 + 3]
        if n % 4 == 0:
            v = t[0]
        elif n % 4 == 1:
            v = jnp.where(lane < 32, pltpu.roll(t[0], 32, 1), pltpu.roll(t[1], 32, 1))
        elif n % 4 == 2:
            v = jnp.where(lane < 64, pltpu.roll(t[1], 64, 1), pltpu.roll(t[2], 64, 1))
        else:
            v = pltpu.roll(t[2], 96, 1)
        heads.append(jnp.where(lane < HD, v, 0.0))
    return heads


def merge_heads(h):
    lane = iota(h[0].shape, 1)
    tiles = []
    for half in (0, 4):
        a, b, c, d = h[half:half + 4]
        tiles.append(jnp.where(lane < 96, a, pltpu.roll(b, 96, 1)))
        tiles.append(jnp.where(lane < 64, pltpu.roll(b, 96, 1), pltpu.roll(c, 64, 1)))
        tiles.append(jnp.where(lane < 32, pltpu.roll(c, 64, 1), pltpu.roll(d, 32, 1)))
    return tiles


def tiles_of(v):
    return [v[:, j * 128:(j + 1) * 128] for j in range(6)]


def kernel(x_ref, g_ref, w_ref, gain_ref, gx_ref, gw_ref, gg_ref,
           xv, wf, wt, sbk, rbk, sbq, rbq, xs, xr, xf, pe, hs, hr, norm, kvg, qgr, raised_ref, ga_ref, st, dqb, dqr, zb, zr,
           hb, hbr, ge, exh, sb2, rb2, gall, ex, gxv, wg, wb, kr, zs, fr, flat, gsc, ss, rs, local):
    s = lax.axis_index("seq")
    n = lax.axis_index("head")
    group, u = s // ROW_GROUPS, s % ROW_GROUPS
    yl, z, core = s // (2 * ZS), s // 2 % ZS, s % 2

    load = pltpu.make_async_copy(x_ref, xv, local.at[0])
    load.start()

    def head_peer(k):
        return (s, lax.rem(n + k, HEADS))

    def z_peer(k):
        return (yl * (2 * ZS) + lax.rem(z + k, ZS) * 2 + core, n)

    def quad_peer(k):
        return (lax.rem(yl + k // 2, 2) * (2 * ZS) + z * 2 + lax.rem(core + k % 2, 2), n)

    def quad_index(k):
        return lax.rem(yl + k // 2, 2) * 2 + lax.rem(core + k % 2, 2)

    def plane_peer(p):
        return (quad_peer(p // HEADS)[0], lax.rem(n + p % HEADS, HEADS))

    def seq_peer(d):
        return (lax.rem(s + d + SEQ, SEQ), n)

    def owner(d):
        block = lax.rem(s + d, SEQ)
        return (block // (2 * ZS) * (2 * ZS) + lax.rem(block // 2 % ZS + HALF_WAY, ZS) * 2 + block % 2, n)

    owned = yl * (2 * ZS) + lax.rem(z + ZS - HALF_WAY, ZS) * 2 + core

    def feeder(d):
        return (lax.rem(owned - d + SEQ, SEQ), n)


    barrier = pltpu.get_barrier_semaphore()
    greeted = [seq_peer(d) for d in (16, 17, -16, -17)] + [z_peer(k) for k in FAR_FIRST]
    greeted += [owner(d) for d in (17, 16, 1)] + [feeder(d) for d in (17, 16, 1)]
    greeted += [seq_peer(1), seq_peer(-1)] + [quad_peer(k) for k in (3, 2, 1)] + [head_peer(k) for k in range(1, HEADS)]
    for peer in greeted:
        pl.semaphore_signal(barrier, inc=1, device_id=peer, device_id_type=MESH)

    def send(stage, src, dst, peer):
        pltpu.make_async_remote_copy(src_ref=src, dst_ref=dst, send_sem=ss.at[stage], recv_sem=rs.at[stage],
                                     device_id=peer, device_id_type=MESH).start()

    def arrived(stage, ref):
        pltpu.make_async_copy(ref, ref, rs.at[stage]).wait()

    pending = []

    def drain():
        for stage, ref in pending:
            pltpu.make_async_copy(ref, ref, ss.at[stage]).wait()

    row = iota((8, 768), 0)
    row8 = iota((8, 128), 0)
    lane8 = iota((8, 128), 1)
    wf[...] = w_ref[...].astype(F32)

    def taps(ab, carry):
        def one(m, e):
            return jnp.broadcast_to(wf[m, pl.ds(ab * 3 + e, 1), :], (8, 768))
        wt[0, ab] = jnp.where(row % 2 == 0, one(0, 1), one(0, 2))
        wt[1, ab] = jnp.where(row % 2 == 1, one(0, 0), 0.0)
        for m in (1, 2):
            wt[1 + m, ab] = jnp.where(row % 4 == 0, one(m, 1), jnp.where(
                row % 4 == 1, one(m, 2), jnp.where(row % 4 == 3, one(m, 0), 0.0)))
        return carry
    lax.fori_loop(0, 9, taps, 0)
    gsc[...] = jnp.zeros_like(gsc)
    gsc[0:3, 0:HD] = gain_ref[...]
    load.wait()

    def fine(m, f, r):
        return xv[(f * 4 + r) * 3 + m].astype(F32)

    def store_heads(dst, groups):
        for p in range(len(groups) // 2):
            v = jnp.concatenate(groups[2 * p:2 * p + 2], 0)
            for h, part in enumerate(split_heads(tiles_of(v))):
                dst[h, p * 16:p * 16 + 16, :] = part.astype(BF16)

    groups = []
    for t in range(2):
        for y in range(2):
            both = []
            for m in (1, 2):
                k_sum = None
                for f, a in PAIRS_K[t]:
                    for r, b in PAIRS_K[y]:
                        tk = fine(m, f, r) * wt[1 + m, a * 3 + b]
                        k_sum = tk if k_sum is None else k_sum + tk
                t1 = k_sum + up(k_sum, 1)
                both.append(jnp.where(row == 0, t1, jnp.where(row == 1, up(t1, 2) + up(k_sum, 4), jnp.where(
                    row == 2, up(k_sum, 5), 0.0))))
            groups.append(both[0] + pltpu.roll(both[1], 4, 0))
    store_heads(sbk, groups)
    groups = []
    for t in range(3):
        for y in range(3):
            a_sum = b_sum = None
            for f, a in PAIRS_Q[t]:
                for r, b in PAIRS_Q[y]:
                    v = fine(0, f, r)
                    ta, tb = v * wt[0, a * 3 + b], v * wt[1, a * 3 + b]
                    a_sum = ta if a_sum is None else a_sum + ta
                    b_sum = tb if b_sum is None else b_sum + tb
            b1 = pltpu.roll(b_sum, 1, 0)
            e = a_sum + up(a_sum, 1) + jnp.where(row == 0, 0.0, b1)
            v = jnp.where(row == 0, e, jnp.where(row == 1, up(e, 1), jnp.where(row == 2, up(e, 2), jnp.where(
                row == 3, up(e, 3), jnp.where(row == 4, up(b1, 4), 0.0)))))
            groups.append(v)
    groups.append(jnp.zeros((8, 768), F32))
    for t in range(2):
        groups.append(jnp.concatenate([g_ref[t, 0].astype(F32), g_ref[t, 1].astype(F32)], 0))
    store_heads(sbq, groups)

    def split_fine(p, carry):
        v = jnp.concatenate([xv[2 * p].astype(F32), xv[2 * p + 1].astype(F32)], 0)
        for h, part in enumerate(split_heads(tiles_of(v))):
            xs[h, pl.ds(pl.multiple_of(p * 16, 16), 16), :] = part.astype(BF16)
        return carry
    lax.fori_loop(0, 24, split_fine, 0)

    pl.semaphore_wait(barrier, len(greeted))
    for stage, src, dst in ((A2A_K, sbk, rbk), (A2A_Q, sbq, rbq)):
        for k in (4, 5, 3, 7, 1, 2, 6):
            peer = head_peer(k)
            send(stage, src.at[peer[1]], dst.at[k], peer)
        pending.append((stage, dst.at[pl.ds(1, HEADS - 1)]))
        dst[0] = src[n]
    arrived(A2A_K, rbk.at[pl.ds(1, HEADS - 1)])

    from_col = [lax.rem(n - h + HEADS, HEADS) for h in range(HEADS)]
    sets = [rbk[from_col[h]].astype(F32) for h in range(HEADS)]
    for grp in range(4):
        parts = [v[grp * 8:grp * 8 + 8] for v in sets]
        for m in range(2):
            if m == 0:
                own = [jnp.where(row8 < 4, p, 0.0) for p in parts]
            else:
                own = [pltpu.roll(jnp.where(row8 >= 4, p, 0.0), 4, 0) for p in parts]
            last = [pltpu.roll(own[4 * j + 3], 6, 0) for j in range(2)]
            for j in range(2):
                v = own[4 * j] + pltpu.roll(own[4 * j + 1], 2, 0) + pltpu.roll(own[4 * j + 2], 4, 0)
                v = v + jnp.where(row8 >= 4, last[j], 0.0)
                if j:
                    v = v + jnp.where(row8 == 0, last[0], 0.0)
                at = 288 + m * 64 + grp * 16 + j * 8
                pe[at:at + 8, :] = v

    def pq(t, y):
        return pe[(t * 3 + y) * 32:(t * 3 + y) * 32 + 32, :]

    def pkv(t, y):
        at = 288 + (t * 2 + y) * 16
        return jnp.concatenate([pe[at:at + 16, :], pe[at + 64:at + 80, :]], 0)

    def exchange(stages, spans, src, dst, peers):
        for stage, (lo, count), peer in zip(stages, spans, peers):
            send(stage, src.at[pl.ds(lo, count)], dst.at[pl.ds(lo, count)], peer)
            pending.append((stage, dst.at[pl.ds(lo, count)]))

    def exchanged(stages, spans, dst):
        for stage, (lo, count) in zip(stages, spans):
            arrived(stage, dst.at[pl.ds(lo, count)])

    hs[0:128, :] = jnp.concatenate([pkv(0, 0), pkv(0, 1), pkv(1, 0), pkv(1, 1)], 0).astype(BF16)
    exchange((KV_OWN, KV_ROW, KV_FRAME, KV_CORNER), KV_SPANS, hs, hr, [owner(d) for d in (0, 1, 16, 17)])
    arrived(A2A_Q, rbq.at[pl.ds(1, HEADS - 1)])
    sets = [rbq[from_col[h]].astype(F32) for h in range(HEADS)]
    for grp in range(9):
        parts = [v[grp * 8:grp * 8 + 8] for v in sets]
        rolled = [pltpu.roll(parts[2 * j + 1], 4, 0) for j in range(4)]
        for j in range(4):
            v = parts[2 * j] + jnp.where(row8 >= 4, rolled[j], 0.0)
            if j:
                v = v + jnp.where(row8 == 0, rolled[j - 1], 0.0)
            pe[grp * 32 + j * 8:grp * 32 + j * 8 + 8, :] = v
    hs[128:288, :] = jnp.concatenate([pq(0, 2), pq(1, 2), pq(2, 0), pq(2, 1), pq(2, 2)], 0).astype(BF16)
    exchange((Q_ROW, Q_FRAME, Q_CORNER), Q_SPANS, hs, hr, [seq_peer(d) for d in (1, 16, 17)])
    for k in range(1, HEADS):
        peer = head_peer(k)
        send(FINE, xs.at[peer[1]], xr.at[k], peer)
    pending.append((FINE, xr.at[pl.ds(1, HEADS - 1)]))
    xr[0] = xs[n]

    for t in range(2):
        for y in range(2):
            vs = []
            for j in range(4):
                a, b = (sets[2 * j + i][80 + t * 8:88 + t * 8] for i in range(2))
                if y == 0:
                    vs.append(jnp.where(row8 < 4, a, pltpu.roll(b, 4, 0)))
                else:
                    vs.append(jnp.where(row8 < 4, pltpu.roll(a, 4, 0), b))
            at = 128 + (t * 2 + y) * 32
            qgr[0, at:at + 32, :] = jnp.concatenate(vs, 0).astype(BF16)

    def layer_norm(pooled, lo, count, gain):
        lane = iota((count, 128), 1)
        centred = jnp.where(lane < HD, pooled - jnp.sum(pooled, 1, keepdims=True) * (1.0 / HD), 0.0)
        rstd = lax.rsqrt(jnp.sum(centred * centred, 1, keepdims=True) * (1.0 / HD) + 1e-6)
        unit = centred * rstd
        norm[0, lo:lo + count, :] = unit
        norm[1, lo:lo + count, :] = jnp.broadcast_to(rstd, (count, 128))
        return (unit * gain).astype(BF16)

    has_u = (u > 0).astype(F32)
    has_g = (group > 0).astype(F32)
    has_c = has_u * has_g

    def border(lo, count, has):
        return hr[lo:lo + count, :].astype(F32) * has

    exchanged((KV_OWN, KV_ROW, KV_FRAME, KV_CORNER), KV_SPANS, hr)
    own_u = (owned % ROW_GROUPS > 0).astype(F32)
    own_g = (owned // ROW_GROUPS > 0).astype(F32)
    gain_kv = jnp.where(iota((32, 128), 0) < 16, gsc[1:2, :], gsc[2:3, :])
    gain_q = jnp.broadcast_to(gsc[0:1, :], (128, 128))
    kvg[0] = layer_norm(hr[0:32, :].astype(F32) + border(32, 32, own_u) + border(64, 32, own_g) + border(96, 32, own_u * own_g),
                        128, 32, gain_kv)
    for k in FAR_FIRST:
        send(GATHER, kvg.at[0], kvg.at[k], z_peer(k))
    pending.append((GATHER, kvg.at[pl.ds(1, ZS - 1)]))

    exchanged((Q_ROW, Q_FRAME, Q_CORNER), Q_SPANS, hr)
    q00 = pq(0, 0) + border(128, 32, has_u) + border(192, 32, has_g) + border(256, 32, has_c)
    q01 = pq(0, 1) + border(224, 32, has_g)
    q10 = pq(1, 0) + border(160, 32, has_u)
    qgr[0, 0:128, :] = layer_norm(jnp.concatenate([q00, q01, q10, pq(1, 1)], 0), 0, 128, gain_q)
    for k in (2, 3, 1):
        send(QUAD, qgr.at[0], qgr.at[k], quad_peer(k))
    pending.append((QUAD, qgr.at[pl.ds(1, 3)]))
    arrived(QUAD, qgr.at[pl.ds(1, 3)])
    arrived(GATHER, kvg.at[pl.ds(1, ZS - 1)])

    keys = kvg[:, 0:16, :].reshape(256, 128)
    values = kvg[:, 16:32, :].reshape(256, 128)
    queries = qgr[:, 0:128, :].reshape(512, 128)
    grads = qgr[:, 128:256, :].reshape(512, 128)
    nt = (((1,), (1,)), ((), ()))
    raised_ref[...] = jnp.exp(lax.dot_general(keys, queries, nt, preferred_element_type=F32) * SCALE)
    ga_ref[...] = lax.dot_general(values, grads, nt, preferred_element_type=F32)
    total = jnp.sum(raised_ref[...], 0, keepdims=True)
    delta = jnp.sum(raised_ref[...] * ga_ref[...], 0, keepdims=True)
    for j in range(4):
        st[0, j:j + 1, :] = total[:, j * 128:(j + 1) * 128]
        st[0, 4 + j:5 + j, :] = delta[:, j * 128:(j + 1) * 128]
    for k in (2, 3, 1):
        send(STATS, st.at[0], st.at[k], quad_peer(k))
    pending.append((STATS, st.at[pl.ds(1, 3)]))
    arrived(STATS, st.at[pl.ds(1, 3)])

    def quad_sum(at):
        outs = []
        for j in range(4):
            v = st[0, at + j:at + j + 1, :]
            for k in range(1, 4):
                i = at + (j ^ k)
                v = v + st[k, i:i + 1, :]
            outs.append(v)
        return jnp.concatenate(outs, 1)

    inverse = 1.0 / quad_sum(0)
    row_delta = quad_sum(4) * inverse
    attention = raised_ref[...] * inverse
    grad_scores = (attention * (ga_ref[...] - row_delta)).astype(BF16)
    grad_key = jnp.dot(grad_scores, queries, preferred_element_type=F32) * SCALE
    grad_value = jnp.dot(attention.astype(BF16), grads, preferred_element_type=F32)
    zb[:, 0:16, :] = grad_key.reshape(ZS, 16, 128).astype(BF16)
    zb[:, 16:32, :] = grad_value.reshape(ZS, 16, 128).astype(BF16)
    for k in FAR_FIRST:
        send(SCATTER, zb.at[k], zr.at[k], z_peer(ZS - k))
    pending.append((SCATTER, zr.at[pl.ds(1, ZS - 1)]))
    grad_query = lax.dot_general(grad_scores, keys, (((0,), (0,)), ((), ())), preferred_element_type=F32)
    dqb[...] = grad_query.reshape(4, 128, 128)
    for k in (2, 3, 1):
        send(DQ, dqb.at[k], dqr.at[k], quad_peer(k))
    pending.append((DQ, dqr.at[pl.ds(1, 3)]))
    zr[0] = zb[0]
    dqr[0] = dqb[0]

    def norm_backward(grad_normed, lo, count, gain):
        lane = iota((count, 128), 1)
        unit = norm[0, lo:lo + count, :]
        inner = grad_normed * gain
        mean_1 = jnp.sum(inner, 1, keepdims=True) * (1.0 / HD)
        mean_2 = jnp.sum(inner * unit, 1, keepdims=True) * (1.0 / HD)
        out = norm[1, lo:lo + count, :] * jnp.where(lane < HD, inner - mean_1 - unit * mean_2, 0.0)
        return out, grad_normed * unit

    arrived(DQ, dqr.at[pl.ds(1, 3)])
    dq = dqr[0] + dqr[1] + dqr[2] + dqr[3]
    gq, gain_rows = norm_backward(dq * SCALE + qgr[0, 128:256, :].astype(F32), 0, 128, gain_q)
    wg[80:88, :] = jnp.zeros((8, 128), F32)
    wg[81:82, :] = jnp.sum(gain_rows, 0, keepdims=True)
    hb[128:288, :] = jnp.concatenate([gq[0:32], gq[64:96], gq[0:64], gq[0:32]], 0).astype(BF16)
    exchange((BQ_ROW, BQ_FRAME, BQ_CORNER), Q_SPANS, hb, hbr, [seq_peer(-d) for d in (1, 16, 17)])
    for i, grp in enumerate(OWN_Q):
        ge[grp * 32:grp * 32 + 32, :] = gq[i * 32:i * 32 + 32]

    arrived(FINE, xr.at[pl.ds(1, HEADS - 1)])
    for h in range(HEADS):
        xf[:, h * 8:h * 8 + 8, :] = xr[from_col[h]].astype(F32).reshape(48, 8, 128)

    arrived(SCATTER, zr.at[pl.ds(1, ZS - 1)])
    gkv, gain_rows = norm_backward(jnp.sum(zr[...].astype(F32), 0), 128, 32, gain_kv)
    wg[82:83, :] = jnp.sum(gain_rows[0:16], 0, keepdims=True)
    wg[83:84, :] = jnp.sum(gain_rows[16:32], 0, keepdims=True)
    hb[0:128, :] = jnp.concatenate([gkv] * 4, 0).astype(BF16)
    exchange((BK_OWN, BK_ROW, BK_FRAME, BK_CORNER), KV_SPANS, hb, hbr, [feeder(d) for d in (0, 1, 16, 17)])
    back_u = (u < ROW_GROUPS - 1).astype(F32)
    back_g = (group < SEQ // ROW_GROUPS - 1).astype(F32)
    back_c = back_u * back_g

    def returned(lo, count, has):
        return hbr[lo:lo + count, :].astype(F32) * has

    exchanged((BQ_ROW, BQ_FRAME, BQ_CORNER), Q_SPANS, hbr)
    ge[2 * 32:3 * 32, :] = returned(128, 32, back_u)
    ge[5 * 32:6 * 32, :] = returned(160, 32, back_u)
    ge[6 * 32:8 * 32, :] = returned(192, 64, back_g)
    ge[8 * 32:9 * 32, :] = returned(256, 32, back_c)

    def pairs(pair_list, a):
        return [(f, t) for t, entries in enumerate(pair_list) for f, tap in entries if tap == a]

    def spread(rows, cols, target):
        return jnp.where(iota((rows, cols), 1) == target, 1.0, 0.0).astype(BF16)

    r = iota((128, 32), 0)
    spread_q = spread(128, 32, ((r & 63) >> 1) + (r >> 6))
    spread_k = spread(64, 16, (iota((64, 16), 0) + 1) >> 2)
    row64 = iota((64, 128), 0)
    for grp in range(9):
        exh[grp * 128:grp * 128 + 128, :] = jnp.dot(spread_q, ge[grp * 32:grp * 32 + 32, :].astype(BF16),
                                                    preferred_element_type=F32)

    def tap_rows(masked, m, ab):
        for e, v in enumerate(masked):
            wg[m * 27 + ab * 3 + e:m * 27 + ab * 3 + e + 1, :] = jnp.sum(v, 0, keepdims=True)

    for a in range(3):
        for b in range(3):
            first = second = None
            for f, t in pairs(PAIRS_Q, a):
                for rr, y in pairs(PAIRS_Q, b):
                    v, at = xf[(f * 4 + rr) * 3], (t * 3 + y) * 128
                    t1, t2 = v * exh[at:at + 64, :], v * exh[at + 64:at + 128, :]
                    first = t1 if first is None else first + t1
                    second = t2 if second is None else second + t2
            tap_rows((jnp.where(row64 % 2 == 1, second, 0.0), jnp.where(row64 % 2 == 0, first, 0.0),
                      jnp.where(row64 % 2 == 1, first, 0.0)), 0, a * 3 + b)

    def key_taps(m, wide, chosen):
        for a, b in chosen:
            (f, t), = pairs(PAIRS_K, a)
            (rr, y), = pairs(PAIRS_K, b)
            v = xf[(f * 4 + rr) * 3 + m] * wide[t * 2 + y]
            tap_rows(tuple(jnp.where(row64 % 4 == c, v, 0.0) for c in (3, 0, 1)), m, a * 3 + b)

    def wide_key(m, group):
        at = 224 + m * 64 + group * 16
        return jnp.dot(spread_k, ge[at:at + 16, :].astype(BF16), preferred_element_type=F32)

    exchanged((BK_OWN, BK_ROW, BK_FRAME, BK_CORNER), KV_SPANS, hbr)
    for lo, at, has in ((0, 0, 1.0), (32, 16, back_u), (64, 32, back_g), (96, 48, back_c)):
        v = returned(lo, 32, has)
        ge[288 + at:304 + at, :] = v[0:16]
        ge[352 + at:368 + at, :] = v[16:32]
    for m in (1, 2):
        key_taps(m, [wide_key(m, group) for group in range(4)], [(a, b) for a in range(3) for b in range(3)])

    t16, t8 = wg[64:80, :], wg[80:88, :]
    tail = jnp.concatenate([pltpu.roll(t16, 96, 1), pltpu.roll(t16, 64, 1), pltpu.roll(t16, 32, 1),
                            jnp.where(row8 < 4, pltpu.roll(t8, 96, 1), pltpu.roll(pltpu.roll(t8, 64, 1), 4, 0)),
                            pltpu.roll(t8, 32, 1)], 0)
    wb[...] = jnp.where(iota((64, 128), 1) < HD, wg[0:64, :], tail)

    def piece(k):
        return pl.ds(pl.multiple_of(quad_index(k) * 16, 16), 16)

    for k in (2, 3, 1):
        send(SUM_QUAD, wb.at[piece(k)], kr.at[k], quad_peer(k))
    pending.append((SUM_QUAD, kr.at[pl.ds(1, 3)]))
    kr[0] = wb[piece(0), :]

    zero = jnp.zeros((8, 128), F32)
    out_rows = [[] for _ in range(HEADS)]
    for grp in range(9):
        vs = [ge[grp * 32 + j * 8:grp * 32 + j * 8 + 8, :] for j in range(4)] + [zero]
        half = [pltpu.roll(v, 4, 0) for v in vs]
        for h in range(HEADS):
            j = h // 2
            out_rows[h].append(vs[j] if h % 2 == 0 else jnp.where(row8 < 4, half[j], half[j + 1]))
    for grp in range(4):
        vs = [[ge[at:at + 8, :] for at in (288 + m * 64 + grp * 16, 296 + m * 64 + grp * 16)] + [zero] for m in range(2)]
        for h in range(HEADS):
            j, i = h // 4, h % 4
            parts = []
            for m in range(2):
                v = pltpu.roll(vs[m][j], 8 - 2 * i, 0) if i else vs[m][j]
                if i == 3:
                    v = jnp.where(row8 < 2, v, pltpu.roll(vs[m][j + 1], 2, 0))
                parts.append(v)
            out_rows[h].append(jnp.where(row8 < 4, parts[0], pltpu.roll(parts[1], 4, 0)))
    for h in range(HEADS):
        sb2[h] = jnp.concatenate(out_rows[h] + [zero], 0).astype(BF16)
    for k in range(1, HEADS):
        peer = head_peer(k)
        send(A2A_B, sb2.at[peer[1]], rb2.at[k], peer)
    pending.append((A2A_B, rb2.at[pl.ds(1, HEADS - 1)]))
    rb2[0] = sb2[n]

    arrived(SUM_QUAD, kr.at[pl.ds(1, 3)])
    zs[0] = (kr[0] + kr[1] + kr[2] + kr[3]).astype(zs.dtype)
    for k in FAR_FIRST:
        send(SUM_Z, zs.at[0], zs.at[k], z_peer(k))
    pending.append((SUM_Z, zs.at[pl.ds(1, ZS - 1)]))

    arrived(A2A_B, rb2.at[pl.ds(1, HEADS - 1)])
    tiles = merge_heads([rb2[from_col[h]].astype(F32) for h in range(HEADS)])
    for j in range(6):
        gall[:, j * 128:(j + 1) * 128] = tiles[j].astype(BF16)
    r = iota((208, 112), 0)
    grp, late, i = r >> 4, (r >> 3) & 1, r & 7
    ex[...] = jnp.dot(spread(208, 112, grp * 8 + jnp.where(grp < 9, (i >> 1) + late, ((i + 1) >> 2) + 4 * late)),
                      gall[...], preferred_element_type=F32)

    def g_at(grp, late):
        at = grp * 16 + late * 8
        return ex[at:at + 8, :]

    def reached(pair_list, f):
        return [(t, a) for t, entries in enumerate(pair_list) for ff, a in entries if ff == f]

    for f in range(4):
        for rr in range(4):
            q_sum = None
            for t, a in reached(PAIRS_Q, f):
                for y, b in reached(PAIRS_Q, rr):
                    term = g_at(t * 3 + y, 0) * wt[0, a * 3 + b] + g_at(t * 3 + y, 1) * wt[1, a * 3 + b]
                    q_sum = term if q_sum is None else q_sum + term
            gxv[(f * 4 + rr) * 3] = q_sum.astype(BF16)
            for m in (1, 2):
                k_sum = jnp.zeros((8, 768), F32)
                for t, a in reached(PAIRS_K, f):
                    for y, b in reached(PAIRS_K, rr):
                        k_sum = g_at(9 + t * 2 + y, m - 1) * wt[1 + m, a * 3 + b]
                gxv[(f * 4 + rr) * 3 + m] = k_sum.astype(BF16)
    store = pltpu.make_async_copy(gxv, gx_ref, local.at[1])
    store.start()

    arrived(SUM_Z, zs.at[pl.ds(1, ZS - 1)])
    v = zs[z].astype(F32)
    for k in range(1, ZS):
        v = v + zs[lax.rem(z - k + ZS, ZS)].astype(F32)
    fr[0] = v.astype(BF16)
    for p in range(31, 0, -1):
        send(SPREAD, fr.at[0], fr.at[p], plane_peer(p))
    pending.append((SPREAD, fr.at[pl.ds(1, 31)]))
    arrived(SPREAD, fr.at[pl.ds(1, 31)])

    lane16 = iota((16, 128), 1)
    unpacked, gains = [], None
    for h in range(HEADS):
        at = [fr[lax.rem(yl + q // 2, 2) * (2 * HEADS) + lax.rem(core + q % 2, 2) * HEADS + from_col[h]].astype(F32) for q in range(4)]
        t16 = jnp.where(lane16 < 32, pltpu.roll(at[0], 32, 1), jnp.where(
            lane16 < 64, pltpu.roll(at[1], 64, 1), pltpu.roll(at[2], 96, 1)))
        lo, hi = at[3][0:8], at[3][8:16]
        t8 = jnp.where(lane8 < 32, pltpu.roll(lo, 32, 1), jnp.where(
            lane8 < 64, pltpu.roll(pltpu.roll(lo, 64, 1), 4, 0), pltpu.roll(hi, 96, 1)))
        gains = t8 if gains is None else gains + t8
        unpacked.append(jnp.concatenate(at + [t16, t8], 0))
    for j, v in enumerate(merge_heads(unpacked)):
        flat[j * 88:j * 88 + 88, :] = v
    for j in range(6):
        for m in range(3):
            gw_ref[m, :, j * 128:(j + 1) * 128] = flat[j * 88 + m * 27:j * 88 + m * 27 + 27, :]
    gg_ref[...] = gains[1:4, 0:HD]
    store.wait()
    drain()


def shards(qkv_fine, grad_out, pool_weight, norm_gain):
    x = qkv_fine[0].transpose(0, 1, 3, 2, 4).reshape(48, 8, 768)
    w = pool_weight.transpose(1, 0, 2)
    vmem = pl.BlockSpec(memory_space=pltpu.VMEM)
    hbm = pl.BlockSpec(memory_space=pl.ANY)
    scratch = [
        ((48, 8, 768), BF16),
        ((3, 27, 768), F32),
        ((4, 9, 8, 768), F32),
        ((8, 32, 128), BF16),
        ((8, 32, 128), BF16),
        ((8, 96, 128), BF16),
        ((8, 96, 128), BF16),
        ((8, 384, 128), BF16),
        ((8, 384, 128), BF16),
        ((48, 64, 128), F32),
        ((416, 128), F32),
        ((288, 128), BF16),
        ((288, 128), BF16),
        ((2, 160, 128), F32),
        ((ZS, 32, 128), BF16),
        ((4, 256, 128), BF16),
        ((256, 512), F32),
        ((256, 512), F32),
        ((4, 8, 128), F32),
        ((4, 128, 128), F32),
        ((4, 128, 128), F32),
        ((ZS, 32, 128), BF16),
        ((ZS, 32, 128), BF16),
        ((288, 128), BF16),
        ((288, 128), BF16),
        ((416, 128), F32),
        ((9 * 128, 128), F32),
        ((8, 112, 128), BF16),
        ((8, 112, 128), BF16),
        ((112, 768), BF16),
        ((208, 768), F32),
        ((48, 8, 768), BF16),
        ((88, 128), F32),
        ((64, 128), F32),
        ((4, 16, 128), F32),
        ((ZS, 16, 128), BF16),
        ((32, 16, 128), BF16),
        ((6 * 88, 128), F32),
        ((8, 128), F32),
    ]
    gx, gw, gg = pl.pallas_call(
        kernel,
        out_shape=(jax.ShapeDtypeStruct(x.shape, BF16), jax.ShapeDtypeStruct(w.shape, F32),
                   jax.ShapeDtypeStruct(norm_gain.shape, F32)),
        in_specs=[hbm] + [vmem] * 3,
        out_specs=(hbm, vmem, vmem),
        scratch_shapes=[pltpu.VMEM(shape, kind) for shape, kind in scratch]
        + [pltpu.SemaphoreType.DMA((26,)), pltpu.SemaphoreType.DMA((26,)), pltpu.SemaphoreType.DMA((2,))],
        compiler_params=pltpu.CompilerParams(collective_id=0, has_side_effects=True,
                                             vmem_limit_bytes=60 * 1024 * 1024),
    )(x, grad_out[0], w, norm_gain)
    return gx.reshape(4, 4, 3, 8, 768).transpose(0, 1, 3, 2, 4)[None], gw.transpose(1, 0, 2), gg


def solution(mesh):
    in_specs = (P("seq", None, None, "head", None, None), P("seq", None, None, "head", None), P(), P())
    out_specs = (P("seq", None, None, "head", None, None), P(), P())
    return jax.shard_map(shards, mesh=mesh, in_specs=in_specs, out_specs=out_specs, check_vma=False)
```

```python
import jax
import jax.numpy as jnp
from jax import lax
from jax.experimental import pallas as pl
from jax.experimental.pallas import tpu as pltpu
from jax.sharding import PartitionSpec as P

MESH = pl.DeviceIdType.MESH
F32 = jnp.float32
BF16 = jnp.bfloat16
HD = 96
HEADS = 8
ROW_GROUPS = 16
SEQ = 64
ZS = 16
SCALE = HD ** -0.5

PAIRS_Q = (((0, 1), (1, 2)), ((1, 0), (2, 1), (3, 2)), ((3, 0),))
PAIRS_K = (((0, 1), (1, 2)), ((3, 0),))
OWN_Q = (0, 1, 3, 4)

(A2A_K, A2A_Q, FINE, KV_OWN, KV_ROW, KV_FRAME, KV_CORNER, Q_ROW, Q_FRAME, Q_CORNER, GATHER, QUAD, STATS, DQ, SCATTER,
 BQ_ROW, BQ_FRAME, BQ_CORNER, BK_OWN, BK_ROW, BK_FRAME, BK_CORNER, A2A_B, SUM_QUAD, SUM_Z, SPREAD) = range(26)
FAR_FIRST = (8, 7, 9, 6, 10, 5, 11, 4, 12, 3, 13, 2, 14, 1, 15)
KV_SPANS = ((0, 32), (32, 32), (64, 32), (96, 32))
Q_SPANS = ((128, 64), (192, 64), (256, 32))
HALF_WAY = 12


def iota(shape, dim):
    return lax.broadcasted_iota(jnp.int32, shape, dim)


def up(x, by):
    size = x.shape[0]
    return pltpu.roll(x, (size - by) % size, 0)


def split_heads(tiles):
    lane = iota(tiles[0].shape, 1)
    heads = []
    for n in range(HEADS):
        t = tiles[n // 4 * 3:n // 4 * 3 + 3]
        if n % 4 == 0:
            v = t[0]
        elif n % 4 == 1:
            v = jnp.where(lane < 32, pltpu.roll(t[0], 32, 1), pltpu.roll(t[1], 32, 1))
        elif n % 4 == 2:
            v = jnp.where(lane < 64, pltpu.roll(t[1], 64, 1), pltpu.roll(t[2], 64, 1))
        else:
            v = pltpu.roll(t[2], 96, 1)
        heads.append(jnp.where(lane < HD, v, 0.0))
    return heads


def merge_heads(h):
    lane = iota(h[0].shape, 1)
    tiles = []
    for half in (0, 4):
        a, b, c, d = h[half:half + 4]
        tiles.append(jnp.where(lane < 96, a, pltpu.roll(b, 96, 1)))
        tiles.append(jnp.where(lane < 64, pltpu.roll(b, 96, 1), pltpu.roll(c, 64, 1)))
        tiles.append(jnp.where(lane < 32, pltpu.roll(c, 64, 1), pltpu.roll(d, 32, 1)))
    return tiles


def tiles_of(v):
    return [v[:, j * 128:(j + 1) * 128] for j in range(6)]


def kernel(x_ref, g_hbm, w_hbm, gain_hbm, gx_ref, gw_ref, gg_ref,
           xv, g_ref, w_ref, gain_ref, wf, wt, sbk, rbk, sbq, rbq, xs, xr, xf, pe, hs, hr, norm, kvg, qgr, raised_ref, ga_ref, st, dqb, dqr, zb, zr,
           hb, hbr, ge, exh, sb2, rb2, gall, ex, gxv, wg, wb, kr, zs, fr, flat, gsc, ss, rs, local, ready):
    s = lax.axis_index("seq")
    n = lax.axis_index("head")
    group, u = s // ROW_GROUPS, s % ROW_GROUPS
    yl, z, core = s // (2 * ZS), s // 2 % ZS, s % 2

    loads = [pltpu.make_async_copy(src, dst, local.at[i]) for i, (src, dst) in enumerate(
        ((w_hbm, w_ref), (gain_hbm, gain_ref), (x_ref, xv), (g_hbm, g_ref)))]
    for load in loads:
        load.start()

    def head_peer(k):
        return (s, lax.rem(n + k, HEADS))

    def z_peer(k):
        return (yl * (2 * ZS) + lax.rem(z + k, ZS) * 2 + core, n)

    def quad_peer(k):
        return (lax.rem(yl + k // 2, 2) * (2 * ZS) + z * 2 + lax.rem(core + k % 2, 2), n)

    def quad_index(k):
        return lax.rem(yl + k // 2, 2) * 2 + lax.rem(core + k % 2, 2)

    def plane_peer(p):
        return (quad_peer(p // HEADS)[0], lax.rem(n + p % HEADS, HEADS))

    def seq_peer(d):
        return (lax.rem(s + d + SEQ, SEQ), n)

    def owner(d):
        block = lax.rem(s + d, SEQ)
        return (block // (2 * ZS) * (2 * ZS) + lax.rem(block // 2 % ZS + HALF_WAY, ZS) * 2 + block % 2, n)

    owned = yl * (2 * ZS) + lax.rem(z + ZS - HALF_WAY, ZS) * 2 + core

    def feeder(d):
        return (lax.rem(owned - d + SEQ, SEQ), n)


    barrier = pltpu.get_barrier_semaphore()
    greeted = [z_peer(k) for k in (4, 12, 3, 13, 2, 14, 1, 15)]
    greeted += [owner(d) for d in (17, 16, 1)] + [feeder(d) for d in (17, 16, 1)]
    greeted += [seq_peer(1), seq_peer(-1)] + [quad_peer(k) for k in (3, 2, 1)] + [head_peer(k) for k in range(1, HEADS)]
    for peer in greeted:
        pl.semaphore_signal(barrier, inc=1, device_id=peer, device_id_type=MESH)

    def send(stage, src, dst, peer):
        pltpu.make_async_remote_copy(src_ref=src, dst_ref=dst, send_sem=ss.at[stage], recv_sem=rs.at[stage],
                                     device_id=peer, device_id_type=MESH).start()

    def arrived(stage, ref):
        pltpu.make_async_copy(ref, ref, rs.at[stage]).wait()

    def hand_on(stage, peers):
        for peer in peers:
            pl.semaphore_signal(ready.at[stage], inc=1, device_id=peer, device_id_type=MESH)

    quad, four_on = [quad_peer(k) for k in (2, 3, 1)], [z_peer(4), z_peer(12)]
    pending = []

    def drain():
        for stage, ref in pending:
            pltpu.make_async_copy(ref, ref, ss.at[stage]).wait()

    row = iota((8, 768), 0)
    row8 = iota((8, 128), 0)
    lane8 = iota((8, 128), 1)
    loads[0].wait()
    wf[...] = w_ref[...].astype(F32)

    def taps(ab, carry):
        def one(m, e):
            return jnp.broadcast_to(wf[m, pl.ds(ab * 3 + e, 1), :], (8, 768))
        wt[0, ab] = jnp.where(row % 2 == 0, one(0, 1), one(0, 2))
        wt[1, ab] = jnp.where(row % 2 == 1, one(0, 0), 0.0)
        for m in (1, 2):
            wt[1 + m, ab] = jnp.where(row % 4 == 0, one(m, 1), jnp.where(
                row % 4 == 1, one(m, 2), jnp.where(row % 4 == 3, one(m, 0), 0.0)))
        return carry
    lax.fori_loop(0, 9, taps, 0)
    loads[1].wait()
    gsc[...] = jnp.zeros_like(gsc)
    gsc[0:3, 0:HD] = gain_ref[...]
    loads[2].wait()
    loads[3].wait()

    def fine(m, f, r):
        return xv[(f * 4 + r) * 3 + m].astype(F32)

    def store_heads(dst, groups):
        for p in range(len(groups) // 2):
            v = jnp.concatenate(groups[2 * p:2 * p + 2], 0)
            for h, part in enumerate(split_heads(tiles_of(v))):
                dst[h, p * 16:p * 16 + 16, :] = part.astype(BF16)

    groups = []
    for t in range(2):
        for y in range(2):
            both = []
            for m in (1, 2):
                k_sum = None
                for f, a in PAIRS_K[t]:
                    for r, b in PAIRS_K[y]:
                        tk = fine(m, f, r) * wt[1 + m, a * 3 + b]
                        k_sum = tk if k_sum is None else k_sum + tk
                t1 = k_sum + up(k_sum, 1)
                both.append(jnp.where(row == 0, t1, jnp.where(row == 1, up(t1, 2) + up(k_sum, 4), jnp.where(
                    row == 2, up(k_sum, 5), 0.0))))
            groups.append(both[0] + pltpu.roll(both[1], 4, 0))
    store_heads(sbk, groups)
    groups = []
    for t in range(3):
        for y in range(3):
            a_sum = b_sum = None
            for f, a in PAIRS_Q[t]:
                for r, b in PAIRS_Q[y]:
                    v = fine(0, f, r)
                    ta, tb = v * wt[0, a * 3 + b], v * wt[1, a * 3 + b]
                    a_sum = ta if a_sum is None else a_sum + ta
                    b_sum = tb if b_sum is None else b_sum + tb
            b1 = pltpu.roll(b_sum, 1, 0)
            e = a_sum + up(a_sum, 1) + jnp.where(row == 0, 0.0, b1)
            v = jnp.where(row == 0, e, jnp.where(row == 1, up(e, 1), jnp.where(row == 2, up(e, 2), jnp.where(
                row == 3, up(e, 3), jnp.where(row == 4, up(b1, 4), 0.0)))))
            groups.append(v)
    groups.append(jnp.zeros((8, 768), F32))
    for t in range(2):
        groups.append(jnp.concatenate([g_ref[t, 0].astype(F32), g_ref[t, 1].astype(F32)], 0))
    store_heads(sbq, groups)

    def split_fine(p, carry):
        v = jnp.concatenate([xv[2 * p].astype(F32), xv[2 * p + 1].astype(F32)], 0)
        for h, part in enumerate(split_heads(tiles_of(v))):
            xs[h, pl.ds(pl.multiple_of(p * 16, 16), 16), :] = part.astype(BF16)
        return carry
    lax.fori_loop(0, 24, split_fine, 0)

    pl.semaphore_wait(barrier, len(greeted))
    for stage, src, dst in ((A2A_K, sbk, rbk), (A2A_Q, sbq, rbq)):
        for k in (4, 5, 3, 7, 1, 2, 6):
            peer = head_peer(k)
            send(stage, src.at[peer[1]], dst.at[k], peer)
        pending.append((stage, dst.at[pl.ds(1, HEADS - 1)]))
        dst[0] = src[n]
    hand_on(0, quad)
    pl.semaphore_wait(ready.at[0], 3)
    hand_on(1, four_on)
    arrived(A2A_K, rbk.at[pl.ds(1, HEADS - 1)])

    from_col = [lax.rem(n - h + HEADS, HEADS) for h in range(HEADS)]
    sets = [rbk[from_col[h]].astype(F32) for h in range(HEADS)]
    for grp in range(4):
        parts = [v[grp * 8:grp * 8 + 8] for v in sets]
        for m in range(2):
            if m == 0:
                own = [jnp.where(row8 < 4, p, 0.0) for p in parts]
            else:
                own = [pltpu.roll(jnp.where(row8 >= 4, p, 0.0), 4, 0) for p in parts]
            last = [pltpu.roll(own[4 * j + 3], 6, 0) for j in range(2)]
            for j in range(2):
                v = own[4 * j] + pltpu.roll(own[4 * j + 1], 2, 0) + pltpu.roll(own[4 * j + 2], 4, 0)
                v = v + jnp.where(row8 >= 4, last[j], 0.0)
                if j:
                    v = v + jnp.where(row8 == 0, last[0], 0.0)
                at = 288 + m * 64 + grp * 16 + j * 8
                pe[at:at + 8, :] = v

    def pq(t, y):
        return pe[(t * 3 + y) * 32:(t * 3 + y) * 32 + 32, :]

    def pkv(t, y):
        at = 288 + (t * 2 + y) * 16
        return jnp.concatenate([pe[at:at + 16, :], pe[at + 64:at + 80, :]], 0)

    def exchange(stages, spans, src, dst, peers):
        for stage, (lo, count), peer in zip(stages, spans, peers):
            send(stage, src.at[pl.ds(lo, count)], dst.at[pl.ds(lo, count)], peer)
            pending.append((stage, dst.at[pl.ds(lo, count)]))

    def exchanged(stages, spans, dst):
        for stage, (lo, count) in zip(stages, spans):
            arrived(stage, dst.at[pl.ds(lo, count)])

    hs[0:128, :] = jnp.concatenate([pkv(0, 0), pkv(0, 1), pkv(1, 0), pkv(1, 1)], 0).astype(BF16)
    exchange((KV_OWN, KV_ROW, KV_FRAME, KV_CORNER), KV_SPANS, hs, hr, [owner(d) for d in (0, 1, 16, 17)])
    pl.semaphore_wait(ready.at[1], 2)
    hand_on(2, four_on)
    arrived(A2A_Q, rbq.at[pl.ds(1, HEADS - 1)])
    sets = [rbq[from_col[h]].astype(F32) for h in range(HEADS)]
    for grp in range(9):
        parts = [v[grp * 8:grp * 8 + 8] for v in sets]
        rolled = [pltpu.roll(parts[2 * j + 1], 4, 0) for j in range(4)]
        for j in range(4):
            v = parts[2 * j] + jnp.where(row8 >= 4, rolled[j], 0.0)
            if j:
                v = v + jnp.where(row8 == 0, rolled[j - 1], 0.0)
            pe[grp * 32 + j * 8:grp * 32 + j * 8 + 8, :] = v
    hs[128:288, :] = jnp.concatenate([pq(0, 2), pq(1, 2), pq(2, 0), pq(2, 1), pq(2, 2)], 0).astype(BF16)
    pl.semaphore_wait(ready.at[2], 2)
    exchange((Q_ROW, Q_FRAME, Q_CORNER), Q_SPANS, hs, hr, [seq_peer(d) for d in (1, 16, 17)])
    for k in range(1, HEADS):
        peer = head_peer(k)
        send(FINE, xs.at[peer[1]], xr.at[k], peer)
    pending.append((FINE, xr.at[pl.ds(1, HEADS - 1)]))
    xr[0] = xs[n]

    for t in range(2):
        for y in range(2):
            vs = []
            for j in range(4):
                a, b = (sets[2 * j + i][80 + t * 8:88 + t * 8] for i in range(2))
                if y == 0:
                    vs.append(jnp.where(row8 < 4, a, pltpu.roll(b, 4, 0)))
                else:
                    vs.append(jnp.where(row8 < 4, pltpu.roll(a, 4, 0), b))
            at = 128 + (t * 2 + y) * 32
            qgr[0, at:at + 32, :] = jnp.concatenate(vs, 0).astype(BF16)

    def layer_norm(pooled, lo, count, gain):
        lane = iota((count, 128), 1)
        centred = jnp.where(lane < HD, pooled - jnp.sum(pooled, 1, keepdims=True) * (1.0 / HD), 0.0)
        rstd = lax.rsqrt(jnp.sum(centred * centred, 1, keepdims=True) * (1.0 / HD) + 1e-6)
        unit = centred * rstd
        norm[0, lo:lo + count, :] = unit
        norm[1, lo:lo + count, :] = jnp.broadcast_to(rstd, (count, 128))
        return (unit * gain).astype(BF16)

    has_u = (u > 0).astype(F32)
    has_g = (group > 0).astype(F32)
    has_c = has_u * has_g

    def border(lo, count, has):
        return hr[lo:lo + count, :].astype(F32) * has

    exchanged((KV_OWN, KV_ROW, KV_FRAME, KV_CORNER), KV_SPANS, hr)
    own_u = (owned % ROW_GROUPS > 0).astype(F32)
    own_g = (owned // ROW_GROUPS > 0).astype(F32)
    gain_kv = jnp.where(iota((32, 128), 0) < 16, gsc[1:2, :], gsc[2:3, :])
    gain_q = jnp.broadcast_to(gsc[0:1, :], (128, 128))
    kvg[0] = layer_norm(hr[0:32, :].astype(F32) + border(32, 32, own_u) + border(64, 32, own_g) + border(96, 32, own_u * own_g),
                        128, 32, gain_kv)
    for k in FAR_FIRST:
        send(GATHER, kvg.at[0], kvg.at[k], z_peer(k))
    pending.append((GATHER, kvg.at[pl.ds(1, ZS - 1)]))

    exchanged((Q_ROW, Q_FRAME, Q_CORNER), Q_SPANS, hr)
    q00 = pq(0, 0) + border(128, 32, has_u) + border(192, 32, has_g) + border(256, 32, has_c)
    q01 = pq(0, 1) + border(224, 32, has_g)
    q10 = pq(1, 0) + border(160, 32, has_u)
    qgr[0, 0:128, :] = layer_norm(jnp.concatenate([q00, q01, q10, pq(1, 1)], 0), 0, 128, gain_q)
    for k in (2, 3, 1):
        send(QUAD, qgr.at[0], qgr.at[k], quad_peer(k))
    pending.append((QUAD, qgr.at[pl.ds(1, 3)]))
    arrived(QUAD, qgr.at[pl.ds(1, 3)])
    arrived(GATHER, kvg.at[pl.ds(1, ZS - 1)])

    keys = kvg[:, 0:16, :].reshape(256, 128)
    values = kvg[:, 16:32, :].reshape(256, 128)
    queries = qgr[:, 0:128, :].reshape(512, 128)
    grads = qgr[:, 128:256, :].reshape(512, 128)
    nt = (((1,), (1,)), ((), ()))
    raised_ref[...] = jnp.exp(lax.dot_general(keys, queries, nt, preferred_element_type=F32) * SCALE)
    ga_ref[...] = lax.dot_general(values, grads, nt, preferred_element_type=F32)
    total = jnp.sum(raised_ref[...], 0, keepdims=True)
    delta = jnp.sum(raised_ref[...] * ga_ref[...], 0, keepdims=True)
    for j in range(4):
        st[0, j:j + 1, :] = total[:, j * 128:(j + 1) * 128]
        st[0, 4 + j:5 + j, :] = delta[:, j * 128:(j + 1) * 128]
    for k in (2, 3, 1):
        send(STATS, st.at[0], st.at[k], quad_peer(k))
    pending.append((STATS, st.at[pl.ds(1, 3)]))
    arrived(STATS, st.at[pl.ds(1, 3)])

    def quad_sum(at):
        outs = []
        for j in range(4):
            v = st[0, at + j:at + j + 1, :]
            for k in range(1, 4):
                i = at + (j ^ k)
                v = v + st[k, i:i + 1, :]
            outs.append(v)
        return jnp.concatenate(outs, 1)

    inverse = 1.0 / quad_sum(0)
    row_delta = quad_sum(4) * inverse
    attention = raised_ref[...] * inverse
    grad_scores = (attention * (ga_ref[...] - row_delta)).astype(BF16)
    grad_key = jnp.dot(grad_scores, queries, preferred_element_type=F32) * SCALE
    grad_value = jnp.dot(attention.astype(BF16), grads, preferred_element_type=F32)
    zb[:, 0:16, :] = grad_key.reshape(ZS, 16, 128).astype(BF16)
    zb[:, 16:32, :] = grad_value.reshape(ZS, 16, 128).astype(BF16)
    for k in FAR_FIRST:
        send(SCATTER, zb.at[k], zr.at[k], z_peer(ZS - k))
    pending.append((SCATTER, zr.at[pl.ds(1, ZS - 1)]))
    grad_query = lax.dot_general(grad_scores, keys, (((0,), (0,)), ((), ())), preferred_element_type=F32)
    dqb[...] = grad_query.reshape(4, 128, 128)
    for k in (2, 3, 1):
        send(DQ, dqb.at[k], dqr.at[k], quad_peer(k))
    pending.append((DQ, dqr.at[pl.ds(1, 3)]))
    zr[0] = zb[0]
    dqr[0] = dqb[0]

    def norm_backward(grad_normed, lo, count, gain):
        lane = iota((count, 128), 1)
        unit = norm[0, lo:lo + count, :]
        inner = grad_normed * gain
        mean_1 = jnp.sum(inner, 1, keepdims=True) * (1.0 / HD)
        mean_2 = jnp.sum(inner * unit, 1, keepdims=True) * (1.0 / HD)
        out = norm[1, lo:lo + count, :] * jnp.where(lane < HD, inner - mean_1 - unit * mean_2, 0.0)
        return out, grad_normed * unit

    arrived(DQ, dqr.at[pl.ds(1, 3)])
    dq = dqr[0] + dqr[1] + dqr[2] + dqr[3]
    gq, gain_rows = norm_backward(dq * SCALE + qgr[0, 128:256, :].astype(F32), 0, 128, gain_q)
    wg[80:88, :] = jnp.zeros((8, 128), F32)
    wg[81:82, :] = jnp.sum(gain_rows, 0, keepdims=True)
    hb[128:288, :] = jnp.concatenate([gq[0:32], gq[64:96], gq[0:64], gq[0:32]], 0).astype(BF16)
    exchange((BQ_ROW, BQ_FRAME, BQ_CORNER), Q_SPANS, hb, hbr, [seq_peer(-d) for d in (1, 16, 17)])
    for i, grp in enumerate(OWN_Q):
        ge[grp * 32:grp * 32 + 32, :] = gq[i * 32:i * 32 + 32]

    arrived(FINE, xr.at[pl.ds(1, HEADS - 1)])
    for h in range(HEADS):
        xf[:, h * 8:h * 8 + 8, :] = xr[from_col[h]].astype(F32).reshape(48, 8, 128)

    arrived(SCATTER, zr.at[pl.ds(1, ZS - 1)])
    gkv, gain_rows = norm_backward(jnp.sum(zr[...].astype(F32), 0), 128, 32, gain_kv)
    wg[82:83, :] = jnp.sum(gain_rows[0:16], 0, keepdims=True)
    wg[83:84, :] = jnp.sum(gain_rows[16:32], 0, keepdims=True)
    hb[0:128, :] = jnp.concatenate([gkv] * 4, 0).astype(BF16)
    exchange((BK_OWN, BK_ROW, BK_FRAME, BK_CORNER), KV_SPANS, hb, hbr, [feeder(d) for d in (0, 1, 16, 17)])
    back_u = (u < ROW_GROUPS - 1).astype(F32)
    back_g = (group < SEQ // ROW_GROUPS - 1).astype(F32)
    back_c = back_u * back_g

    def returned(lo, count, has):
        return hbr[lo:lo + count, :].astype(F32) * has

    exchanged((BQ_ROW, BQ_FRAME, BQ_CORNER), Q_SPANS, hbr)
    ge[2 * 32:3 * 32, :] = returned(128, 32, back_u)
    ge[5 * 32:6 * 32, :] = returned(160, 32, back_u)
    ge[6 * 32:8 * 32, :] = returned(192, 64, back_g)
    ge[8 * 32:9 * 32, :] = returned(256, 32, back_c)

    def pairs(pair_list, a):
        return [(f, t) for t, entries in enumerate(pair_list) for f, tap in entries if tap == a]

    def spread(rows, cols, target):
        return jnp.where(iota((rows, cols), 1) == target, 1.0, 0.0).astype(BF16)

    r = iota((128, 32), 0)
    spread_q = spread(128, 32, ((r & 63) >> 1) + (r >> 6))
    spread_k = spread(64, 16, (iota((64, 16), 0) + 1) >> 2)
    odd, by_four = row8 % 2 == 1, row8 % 4

    def over_blocks(v):
        return jnp.sum(v.reshape(HEADS, 8, 128), 0)

    for grp in range(9):
        exh[grp * 128:grp * 128 + 128, :] = jnp.dot(spread_q, ge[grp * 32:grp * 32 + 32, :].astype(BF16),
                                                    preferred_element_type=F32)

    def tap_rows(masked, m, ab):
        for e, v in enumerate(masked):
            wg[m * 27 + ab * 3 + e:m * 27 + ab * 3 + e + 1, :] = jnp.sum(v, 0, keepdims=True)

    for a in range(3):
        for b in range(3):
            first = second = None
            for f, t in pairs(PAIRS_Q, a):
                for rr, y in pairs(PAIRS_Q, b):
                    v, at = xf[(f * 4 + rr) * 3], (t * 3 + y) * 128
                    t1, t2 = v * exh[at:at + 64, :], v * exh[at + 64:at + 128, :]
                    first = t1 if first is None else first + t1
                    second = t2 if second is None else second + t2
            first, second = over_blocks(first), over_blocks(second)
            tap_rows((jnp.where(odd, second, 0.0), jnp.where(odd, 0.0, first), jnp.where(odd, first, 0.0)), 0, a * 3 + b)

    def key_taps(m, wide, chosen):
        for a, b in chosen:
            (f, t), = pairs(PAIRS_K, a)
            (rr, y), = pairs(PAIRS_K, b)
            v = over_blocks(xf[(f * 4 + rr) * 3 + m] * wide[t * 2 + y])
            tap_rows(tuple(jnp.where(by_four == c, v, 0.0) for c in (3, 0, 1)), m, a * 3 + b)

    def wide_key(m, group):
        at = 224 + m * 64 + group * 16
        return jnp.dot(spread_k, ge[at:at + 16, :].astype(BF16), preferred_element_type=F32)

    exchanged((BK_OWN, BK_ROW, BK_FRAME, BK_CORNER), KV_SPANS, hbr)
    for lo, at, has in ((0, 0, 1.0), (32, 16, back_u), (64, 32, back_g), (96, 48, back_c)):
        v = returned(lo, 32, has)
        ge[288 + at:304 + at, :] = v[0:16]
        ge[352 + at:368 + at, :] = v[16:32]
    for m in (1, 2):
        key_taps(m, [wide_key(m, group) for group in range(4)], [(a, b) for a in range(3) for b in range(3)])

    t16, t8 = wg[64:80, :], wg[80:88, :]
    tail = jnp.concatenate([pltpu.roll(t16, 96, 1), pltpu.roll(t16, 64, 1), pltpu.roll(t16, 32, 1),
                            jnp.where(row8 < 4, pltpu.roll(t8, 96, 1), pltpu.roll(pltpu.roll(t8, 64, 1), 4, 0)),
                            pltpu.roll(t8, 32, 1)], 0)
    wb[...] = jnp.where(iota((64, 128), 1) < HD, wg[0:64, :], tail)

    def piece(k):
        return pl.ds(pl.multiple_of(quad_index(k) * 16, 16), 16)

    for k in (2, 3, 1):
        send(SUM_QUAD, wb.at[piece(k)], kr.at[k], quad_peer(k))
    pending.append((SUM_QUAD, kr.at[pl.ds(1, 3)]))
    kr[0] = wb[piece(0), :]

    zero = jnp.zeros((8, 128), F32)
    out_rows = [[] for _ in range(HEADS)]
    for grp in range(9):
        vs = [ge[grp * 32 + j * 8:grp * 32 + j * 8 + 8, :] for j in range(4)] + [zero]
        half = [pltpu.roll(v, 4, 0) for v in vs]
        for h in range(HEADS):
            j = h // 2
            out_rows[h].append(vs[j] if h % 2 == 0 else jnp.where(row8 < 4, half[j], half[j + 1]))
    for grp in range(4):
        vs = [[ge[at:at + 8, :] for at in (288 + m * 64 + grp * 16, 296 + m * 64 + grp * 16)] + [zero] for m in range(2)]
        for h in range(HEADS):
            j, i = h // 4, h % 4
            parts = []
            for m in range(2):
                v = pltpu.roll(vs[m][j], 8 - 2 * i, 0) if i else vs[m][j]
                if i == 3:
                    v = jnp.where(row8 < 2, v, pltpu.roll(vs[m][j + 1], 2, 0))
                parts.append(v)
            out_rows[h].append(jnp.where(row8 < 4, parts[0], pltpu.roll(parts[1], 4, 0)))
    for h in range(HEADS):
        sb2[h] = jnp.concatenate(out_rows[h] + [zero], 0).astype(BF16)
    for k in range(1, HEADS):
        peer = head_peer(k)
        send(A2A_B, sb2.at[peer[1]], rb2.at[k], peer)
    pending.append((A2A_B, rb2.at[pl.ds(1, HEADS - 1)]))
    rb2[0] = sb2[n]

    arrived(SUM_QUAD, kr.at[pl.ds(1, 3)])
    zs[0] = (kr[0] + kr[1] + kr[2] + kr[3]).astype(zs.dtype)
    for k in FAR_FIRST:
        send(SUM_Z, zs.at[0], zs.at[k], z_peer(k))
    pending.append((SUM_Z, zs.at[pl.ds(1, ZS - 1)]))

    arrived(A2A_B, rb2.at[pl.ds(1, HEADS - 1)])
    tiles = merge_heads([rb2[from_col[h]].astype(F32) for h in range(HEADS)])
    for j in range(6):
        gall[:, j * 128:(j + 1) * 128] = tiles[j].astype(BF16)
    r = iota((208, 112), 0)
    grp, late, i = r >> 4, (r >> 3) & 1, r & 7
    ex[...] = jnp.dot(spread(208, 112, grp * 8 + jnp.where(grp < 9, (i >> 1) + late, ((i + 1) >> 2) + 4 * late)),
                      gall[...], preferred_element_type=F32)

    def g_at(grp, late):
        at = grp * 16 + late * 8
        return ex[at:at + 8, :]

    def reached(pair_list, f):
        return [(t, a) for t, entries in enumerate(pair_list) for ff, a in entries if ff == f]

    for f in range(4):
        for rr in range(4):
            q_sum = None
            for t, a in reached(PAIRS_Q, f):
                for y, b in reached(PAIRS_Q, rr):
                    term = g_at(t * 3 + y, 0) * wt[0, a * 3 + b] + g_at(t * 3 + y, 1) * wt[1, a * 3 + b]
                    q_sum = term if q_sum is None else q_sum + term
            gxv[(f * 4 + rr) * 3] = q_sum.astype(BF16)
            for m in (1, 2):
                k_sum = jnp.zeros((8, 768), F32)
                for t, a in reached(PAIRS_K, f):
                    for y, b in reached(PAIRS_K, rr):
                        k_sum = g_at(9 + t * 2 + y, m - 1) * wt[1 + m, a * 3 + b]
                gxv[(f * 4 + rr) * 3 + m] = k_sum.astype(BF16)
    store = pltpu.make_async_copy(gxv, gx_ref, local.at[4])
    store.start()

    arrived(SUM_Z, zs.at[pl.ds(1, ZS - 1)])
    v = zs[z].astype(F32)
    for k in range(1, ZS):
        v = v + zs[lax.rem(z - k + ZS, ZS)].astype(F32)
    fr[0] = v.astype(BF16)
    for p in range(31, 0, -1):
        send(SPREAD, fr.at[0], fr.at[p], plane_peer(p))
    pending.append((SPREAD, fr.at[pl.ds(1, 31)]))
    arrived(SPREAD, fr.at[pl.ds(1, 31)])

    lane16 = iota((16, 128), 1)
    unpacked, gains = [], None
    for h in range(HEADS):
        at = [fr[lax.rem(yl + q // 2, 2) * (2 * HEADS) + lax.rem(core + q % 2, 2) * HEADS + from_col[h]].astype(F32) for q in range(4)]
        t16 = jnp.where(lane16 < 32, pltpu.roll(at[0], 32, 1), jnp.where(
            lane16 < 64, pltpu.roll(at[1], 64, 1), pltpu.roll(at[2], 96, 1)))
        lo, hi = at[3][0:8], at[3][8:16]
        t8 = jnp.where(lane8 < 32, pltpu.roll(lo, 32, 1), jnp.where(
            lane8 < 64, pltpu.roll(pltpu.roll(lo, 64, 1), 4, 0), pltpu.roll(hi, 96, 1)))
        gains = t8 if gains is None else gains + t8
        unpacked.append(jnp.concatenate(at + [t16, t8], 0))
    for j, v in enumerate(merge_heads(unpacked)):
        flat[j * 88:j * 88 + 88, :] = v
    for j in range(6):
        for m in range(3):
            gw_ref[m, :, j * 128:(j + 1) * 128] = flat[j * 88 + m * 27:j * 88 + m * 27 + 27, :]
    gg_ref[...] = gains[1:4, 0:HD]
    store.wait()
    drain()


def shards(qkv_fine, grad_out, pool_weight, norm_gain):
    x = qkv_fine[0].transpose(0, 1, 3, 2, 4).reshape(48, 8, 768)
    w = pool_weight.transpose(1, 0, 2)
    vmem = pl.BlockSpec(memory_space=pltpu.VMEM)
    hbm = pl.BlockSpec(memory_space=pl.ANY)
    scratch = [
        ((48, 8, 768), BF16),
        (grad_out.shape[1:], BF16),
        (w.shape, BF16),
        (norm_gain.shape, F32),
        ((3, 27, 768), F32),
        ((4, 9, 8, 768), F32),
        ((8, 32, 128), BF16),
        ((8, 32, 128), BF16),
        ((8, 96, 128), BF16),
        ((8, 96, 128), BF16),
        ((8, 384, 128), BF16),
        ((8, 384, 128), BF16),
        ((48, 64, 128), F32),
        ((416, 128), F32),
        ((288, 128), BF16),
        ((288, 128), BF16),
        ((2, 160, 128), F32),
        ((ZS, 32, 128), BF16),
        ((4, 256, 128), BF16),
        ((256, 512), F32),
        ((256, 512), F32),
        ((4, 8, 128), F32),
        ((4, 128, 128), F32),
        ((4, 128, 128), F32),
        ((ZS, 32, 128), BF16),
        ((ZS, 32, 128), BF16),
        ((288, 128), BF16),
        ((288, 128), BF16),
        ((416, 128), F32),
        ((9 * 128, 128), F32),
        ((8, 112, 128), BF16),
        ((8, 112, 128), BF16),
        ((112, 768), BF16),
        ((208, 768), F32),
        ((48, 8, 768), BF16),
        ((88, 128), F32),
        ((64, 128), F32),
        ((4, 16, 128), F32),
        ((ZS, 16, 128), BF16),
        ((32, 16, 128), BF16),
        ((6 * 88, 128), F32),
        ((8, 128), F32),
    ]
    gx, gw, gg = pl.pallas_call(
        kernel,
        out_shape=(jax.ShapeDtypeStruct(x.shape, BF16), jax.ShapeDtypeStruct(w.shape, F32),
                   jax.ShapeDtypeStruct(norm_gain.shape, F32)),
        in_specs=[hbm] * 4,
        out_specs=(hbm, vmem, vmem),
        scratch_shapes=[pltpu.VMEM(shape, kind) for shape, kind in scratch]
        + [pltpu.SemaphoreType.DMA((26,)), pltpu.SemaphoreType.DMA((26,)), pltpu.SemaphoreType.DMA((5,)),
           pltpu.SemaphoreType.REGULAR((3,))],
        compiler_params=pltpu.CompilerParams(collective_id=0, has_side_effects=True,
                                             vmem_limit_bytes=60 * 1024 * 1024),
    )(x, grad_out[0], w, norm_gain)
    return gx.reshape(4, 4, 3, 8, 768).transpose(0, 1, 3, 2, 4)[None], gw.transpose(1, 0, 2), gg


def solution(mesh):
    in_specs = (P("seq", None, None, "head", None, None), P("seq", None, None, "head", None), P(), P())
    out_specs = (P("seq", None, None, "head", None, None), P(), P())
    return jax.shard_map(shards, mesh=mesh, in_specs=in_specs, out_specs=out_specs, check_vma=False)
```

```python
import jax
import jax.numpy as jnp
from jax import lax
from jax.experimental import pallas as pl
from jax.experimental.pallas import tpu as pltpu
from jax.sharding import PartitionSpec as P

MESH = pl.DeviceIdType.MESH
F32 = jnp.float32
BF16 = jnp.bfloat16
HD = 96
HEADS = 8
ROW_GROUPS = 16
SEQ = 64
ZS = 16
SCALE = HD ** -0.5

PAIRS_Q = (((0, 1), (1, 2)), ((1, 0), (2, 1), (3, 2)), ((3, 0),))
PAIRS_K = (((0, 1), (1, 2)), ((3, 0),))
OWN_Q = (0, 1, 3, 4)

(A2A_K, A2A_Q, FINE, KV_OWN, KV_ROW, KV_FRAME, KV_CORNER, Q_ROW, Q_FRAME, Q_CORNER, GATHER, QUAD, STATS, DQ, SCATTER,
 BQ_ROW, BQ_FRAME, BQ_CORNER, BK_OWN, BK_ROW, BK_FRAME, BK_CORNER, A2A_B, SUM_QUAD, SUM_Z, SPREAD) = range(26)
FAR_FIRST = (8, 7, 9, 6, 10, 5, 11, 4, 12, 3, 13, 2, 14, 1, 15)
KV_SPANS = ((0, 32), (32, 32), (64, 32), (96, 32))
Q_SPANS = ((128, 64), (192, 64), (256, 32))
HALF_WAY = 12


def iota(shape, dim):
    return lax.broadcasted_iota(jnp.int32, shape, dim)


def up(x, by):
    size = x.shape[0]
    return pltpu.roll(x, (size - by) % size, 0)


def split_heads(tiles):
    lane = iota(tiles[0].shape, 1)
    heads = []
    for n in range(HEADS):
        t = tiles[n // 4 * 3:n // 4 * 3 + 3]
        if n % 4 == 0:
            v = t[0]
        elif n % 4 == 1:
            v = jnp.where(lane < 32, pltpu.roll(t[0], 32, 1), pltpu.roll(t[1], 32, 1))
        elif n % 4 == 2:
            v = jnp.where(lane < 64, pltpu.roll(t[1], 64, 1), pltpu.roll(t[2], 64, 1))
        else:
            v = pltpu.roll(t[2], 96, 1)
        heads.append(jnp.where(lane < HD, v, 0.0))
    return heads


def merge_heads(h):
    lane = iota(h[0].shape, 1)
    tiles = []
    for half in (0, 4):
        a, b, c, d = h[half:half + 4]
        tiles.append(jnp.where(lane < 96, a, pltpu.roll(b, 96, 1)))
        tiles.append(jnp.where(lane < 64, pltpu.roll(b, 96, 1), pltpu.roll(c, 64, 1)))
        tiles.append(jnp.where(lane < 32, pltpu.roll(c, 64, 1), pltpu.roll(d, 32, 1)))
    return tiles


def tiles_of(v):
    return [v[:, j * 128:(j + 1) * 128] for j in range(6)]


def kernel(x_ref, g_hbm, w_hbm, gain_hbm, gx_ref, gw_ref, gg_ref,
           xv, g_ref, w_ref, gain_ref, wf, wt, sbk, rbk, sbq, rbq, xs, xr, xf, pe, hs, hr, norm, kvg, qgr, raised_ref, ga_ref, st, dqb, dqr, zb, zr,
           hb, hbr, ge, exh, sb2, rb2, gall, ex, gxv, wg, wb, kr, zs, fr, flat, gsc, ss, rs, local, ready):
    s = lax.axis_index("seq")
    n = lax.axis_index("head")
    group, u = s // ROW_GROUPS, s % ROW_GROUPS
    yl, z, core = s // (2 * ZS), s // 2 % ZS, s % 2

    loads = [pltpu.make_async_copy(src, dst, local.at[i]) for i, (src, dst) in enumerate(
        ((w_hbm, w_ref), (gain_hbm, gain_ref), (x_ref, xv), (g_hbm, g_ref)))]
    for load in loads:
        load.start()

    def head_peer(k):
        return (s, lax.rem(n + k, HEADS))

    def z_peer(k):
        return (yl * (2 * ZS) + lax.rem(z + k, ZS) * 2 + core, n)

    def quad_peer(k):
        return (lax.rem(yl + k // 2, 2) * (2 * ZS) + z * 2 + lax.rem(core + k % 2, 2), n)

    def quad_index(k):
        return lax.rem(yl + k // 2, 2) * 2 + lax.rem(core + k % 2, 2)

    def plane_peer(p):
        return (quad_peer(p // HEADS)[0], lax.rem(n + p % HEADS, HEADS))

    def seq_peer(d):
        return (lax.rem(s + d + SEQ, SEQ), n)

    def owner(d):
        block = lax.rem(s + d, SEQ)
        return (block // (2 * ZS) * (2 * ZS) + lax.rem(block // 2 % ZS + HALF_WAY, ZS) * 2 + block % 2, n)

    owned = yl * (2 * ZS) + lax.rem(z + ZS - HALF_WAY, ZS) * 2 + core

    def feeder(d):
        return (lax.rem(owned - d + SEQ, SEQ), n)


    barrier = pltpu.get_barrier_semaphore()
    greeted = [z_peer(k) for k in (4, 12, 3, 13, 2, 14, 1, 15)]
    greeted += [owner(d) for d in (17, 16, 1)] + [feeder(d) for d in (17, 16, 1)]
    greeted += [seq_peer(1), seq_peer(-1), seq_peer(1 + SEQ // 2), seq_peer(-1 - SEQ // 2)] + [quad_peer(k) for k in (3, 2, 1)] + [head_peer(k) for k in range(1, HEADS)]
    for peer in greeted:
        pl.semaphore_signal(barrier, inc=1, device_id=peer, device_id_type=MESH)

    def send(stage, src, dst, peer):
        pltpu.make_async_remote_copy(src_ref=src, dst_ref=dst, send_sem=ss.at[stage], recv_sem=rs.at[stage],
                                     device_id=peer, device_id_type=MESH).start()

    def arrived(stage, ref):
        pltpu.make_async_copy(ref, ref, rs.at[stage]).wait()

    def hand_on(stage, peers):
        for peer in peers:
            pl.semaphore_signal(ready.at[stage], inc=1, device_id=peer, device_id_type=MESH)

    four_on = [z_peer(4), z_peer(12)]
    pending = []

    def drain():
        for stage, ref in pending:
            pltpu.make_async_copy(ref, ref, ss.at[stage]).wait()

    row = iota((8, 768), 0)
    row8 = iota((8, 128), 0)
    lane8 = iota((8, 128), 1)
    loads[0].wait()
    wf[...] = w_ref[...].astype(F32)

    def taps(ab, carry):
        def one(m, e):
            return jnp.broadcast_to(wf[m, pl.ds(ab * 3 + e, 1), :], (8, 768))
        wt[0, ab] = jnp.where(row % 2 == 0, one(0, 1), one(0, 2))
        wt[1, ab] = jnp.where(row % 2 == 1, one(0, 0), 0.0)
        for m in (1, 2):
            wt[1 + m, ab] = jnp.where(row % 4 == 0, one(m, 1), jnp.where(
                row % 4 == 1, one(m, 2), jnp.where(row % 4 == 3, one(m, 0), 0.0)))
        return carry
    lax.fori_loop(0, 9, taps, 0)
    loads[1].wait()
    gsc[...] = jnp.zeros_like(gsc)
    gsc[0:3, 0:HD] = gain_ref[...]
    loads[2].wait()
    loads[3].wait()

    def fine(m, f, r):
        return xv[(f * 4 + r) * 3 + m].astype(F32)

    def store_heads(dst, groups):
        for p in range(len(groups) // 2):
            v = jnp.concatenate(groups[2 * p:2 * p + 2], 0)
            for h, part in enumerate(split_heads(tiles_of(v))):
                dst[h, p * 16:p * 16 + 16, :] = part.astype(BF16)

    groups = []
    for t in range(2):
        for y in range(2):
            both = []
            for m in (1, 2):
                k_sum = None
                for f, a in PAIRS_K[t]:
                    for r, b in PAIRS_K[y]:
                        tk = fine(m, f, r) * wt[1 + m, a * 3 + b]
                        k_sum = tk if k_sum is None else k_sum + tk
                t1 = k_sum + up(k_sum, 1)
                both.append(jnp.where(row == 0, t1, jnp.where(row == 1, up(t1, 2) + up(k_sum, 4), jnp.where(
                    row == 2, up(k_sum, 5), 0.0))))
            groups.append(both[0] + pltpu.roll(both[1], 4, 0))
    store_heads(sbk, groups)
    groups = []
    for t in range(3):
        for y in range(3):
            a_sum = b_sum = None
            for f, a in PAIRS_Q[t]:
                for r, b in PAIRS_Q[y]:
                    v = fine(0, f, r)
                    ta, tb = v * wt[0, a * 3 + b], v * wt[1, a * 3 + b]
                    a_sum = ta if a_sum is None else a_sum + ta
                    b_sum = tb if b_sum is None else b_sum + tb
            b1 = pltpu.roll(b_sum, 1, 0)
            e = a_sum + up(a_sum, 1) + jnp.where(row == 0, 0.0, b1)
            v = jnp.where(row == 0, e, jnp.where(row == 1, up(e, 1), jnp.where(row == 2, up(e, 2), jnp.where(
                row == 3, up(e, 3), jnp.where(row == 4, up(b1, 4), 0.0)))))
            groups.append(v)
    groups.append(jnp.zeros((8, 768), F32))
    for t in range(2):
        groups.append(jnp.concatenate([g_ref[t, 0].astype(F32), g_ref[t, 1].astype(F32)], 0))
    store_heads(sbq, groups)

    def split_fine(p, carry):
        v = jnp.concatenate([xv[2 * p].astype(F32), xv[2 * p + 1].astype(F32)], 0)
        for h, part in enumerate(split_heads(tiles_of(v))):
            xs[h, pl.ds(pl.multiple_of(p * 16, 16), 16), :] = part.astype(BF16)
        return carry
    lax.fori_loop(0, 24, split_fine, 0)

    pl.semaphore_wait(barrier, len(greeted))
    hand_on(0, four_on)
    for stage, src, dst in ((A2A_K, sbk, rbk), (A2A_Q, sbq, rbq)):
        for k in (4, 5, 3, 7, 1, 2, 6):
            peer = head_peer(k)
            send(stage, src.at[peer[1]], dst.at[k], peer)
        pending.append((stage, dst.at[pl.ds(1, HEADS - 1)]))
        dst[0] = src[n]
    pl.semaphore_wait(ready.at[0], 2)
    hand_on(1, four_on)
    arrived(A2A_K, rbk.at[pl.ds(1, HEADS - 1)])

    from_col = [lax.rem(n - h + HEADS, HEADS) for h in range(HEADS)]
    sets = [rbk[from_col[h]].astype(F32) for h in range(HEADS)]
    for grp in range(4):
        parts = [v[grp * 8:grp * 8 + 8] for v in sets]
        for m in range(2):
            if m == 0:
                own = [jnp.where(row8 < 4, p, 0.0) for p in parts]
            else:
                own = [pltpu.roll(jnp.where(row8 >= 4, p, 0.0), 4, 0) for p in parts]
            last = [pltpu.roll(own[4 * j + 3], 6, 0) for j in range(2)]
            for j in range(2):
                v = own[4 * j] + pltpu.roll(own[4 * j + 1], 2, 0) + pltpu.roll(own[4 * j + 2], 4, 0)
                v = v + jnp.where(row8 >= 4, last[j], 0.0)
                if j:
                    v = v + jnp.where(row8 == 0, last[0], 0.0)
                at = 288 + m * 64 + grp * 16 + j * 8
                pe[at:at + 8, :] = v

    def pq(t, y):
        return pe[(t * 3 + y) * 32:(t * 3 + y) * 32 + 32, :]

    def pkv(t, y):
        at = 288 + (t * 2 + y) * 16
        return jnp.concatenate([pe[at:at + 16, :], pe[at + 64:at + 80, :]], 0)

    def exchange(stages, spans, src, dst, peers):
        for stage, (lo, count), peer in zip(stages, spans, peers):
            send(stage, src.at[pl.ds(lo, count)], dst.at[pl.ds(lo, count)], peer)
            pending.append((stage, dst.at[pl.ds(lo, count)]))

    def exchanged(stages, spans, dst):
        for stage, (lo, count) in zip(stages, spans):
            arrived(stage, dst.at[pl.ds(lo, count)])

    hs[0:128, :] = jnp.concatenate([pkv(0, 0), pkv(0, 1), pkv(1, 0), pkv(1, 1)], 0).astype(BF16)
    exchange((KV_OWN, KV_ROW, KV_FRAME, KV_CORNER), KV_SPANS, hs, hr, [owner(d) for d in (0, 1, 16, 17)])
    arrived(A2A_Q, rbq.at[pl.ds(1, HEADS - 1)])
    sets = [rbq[from_col[h]].astype(F32) for h in range(HEADS)]
    for grp in range(9):
        parts = [v[grp * 8:grp * 8 + 8] for v in sets]
        rolled = [pltpu.roll(parts[2 * j + 1], 4, 0) for j in range(4)]
        for j in range(4):
            v = parts[2 * j] + jnp.where(row8 >= 4, rolled[j], 0.0)
            if j:
                v = v + jnp.where(row8 == 0, rolled[j - 1], 0.0)
            pe[grp * 32 + j * 8:grp * 32 + j * 8 + 8, :] = v
    hs[128:288, :] = jnp.concatenate([pq(0, 2), pq(1, 2), pq(2, 0), pq(2, 1), pq(2, 2)], 0).astype(BF16)
    pl.semaphore_wait(ready.at[1], 2)
    exchange((Q_ROW, Q_FRAME, Q_CORNER), Q_SPANS, hs, hr, [seq_peer(d) for d in (1, 16, 17)])
    for k in range(1, HEADS):
        peer = head_peer(k)
        send(FINE, xs.at[peer[1]], xr.at[k], peer)
    pending.append((FINE, xr.at[pl.ds(1, HEADS - 1)]))
    xr[0] = xs[n]

    for t in range(2):
        for y in range(2):
            vs = []
            for j in range(4):
                a, b = (sets[2 * j + i][80 + t * 8:88 + t * 8] for i in range(2))
                if y == 0:
                    vs.append(jnp.where(row8 < 4, a, pltpu.roll(b, 4, 0)))
                else:
                    vs.append(jnp.where(row8 < 4, pltpu.roll(a, 4, 0), b))
            at = 128 + (t * 2 + y) * 32
            qgr[0, at:at + 32, :] = jnp.concatenate(vs, 0).astype(BF16)

    def layer_norm(pooled, lo, count, gain):
        lane = iota((count, 128), 1)
        centred = jnp.where(lane < HD, pooled - jnp.sum(pooled, 1, keepdims=True) * (1.0 / HD), 0.0)
        rstd = lax.rsqrt(jnp.sum(centred * centred, 1, keepdims=True) * (1.0 / HD) + 1e-6)
        unit = centred * rstd
        norm[0, lo:lo + count, :] = unit
        norm[1, lo:lo + count, :] = jnp.broadcast_to(rstd, (count, 128))
        return (unit * gain).astype(BF16)

    has_u = (u > 0).astype(F32)
    has_g = (group > 0).astype(F32)
    has_c = has_u * has_g

    def border(lo, count, has):
        return hr[lo:lo + count, :].astype(F32) * has

    exchanged((KV_OWN, KV_ROW, KV_FRAME, KV_CORNER), KV_SPANS, hr)
    own_u = (owned % ROW_GROUPS > 0).astype(F32)
    own_g = (owned // ROW_GROUPS > 0).astype(F32)
    gain_kv = jnp.where(iota((32, 128), 0) < 16, gsc[1:2, :], gsc[2:3, :])
    gain_q = jnp.broadcast_to(gsc[0:1, :], (128, 128))
    kvg[0] = layer_norm(hr[0:32, :].astype(F32) + border(32, 32, own_u) + border(64, 32, own_g) + border(96, 32, own_u * own_g),
                        128, 32, gain_kv)
    for k in FAR_FIRST:
        send(GATHER, kvg.at[0], kvg.at[k], z_peer(k))
    pending.append((GATHER, kvg.at[pl.ds(1, ZS - 1)]))

    exchanged((Q_ROW, Q_FRAME, Q_CORNER), Q_SPANS, hr)
    q00 = pq(0, 0) + border(128, 32, has_u) + border(192, 32, has_g) + border(256, 32, has_c)
    q01 = pq(0, 1) + border(224, 32, has_g)
    q10 = pq(1, 0) + border(160, 32, has_u)
    qgr[0, 0:128, :] = layer_norm(jnp.concatenate([q00, q01, q10, pq(1, 1)], 0), 0, 128, gain_q)
    for k in (2, 3, 1):
        send(QUAD, qgr.at[0], qgr.at[k], quad_peer(k))
    pending.append((QUAD, qgr.at[pl.ds(1, 3)]))
    arrived(QUAD, qgr.at[pl.ds(1, 3)])
    arrived(GATHER, kvg.at[pl.ds(1, ZS - 1)])

    keys = kvg[:, 0:16, :].reshape(256, 128)
    values = kvg[:, 16:32, :].reshape(256, 128)
    queries = qgr[:, 0:128, :].reshape(512, 128)
    grads = qgr[:, 128:256, :].reshape(512, 128)
    nt = (((1,), (1,)), ((), ()))
    raised_ref[...] = jnp.exp(lax.dot_general(keys, queries, nt, preferred_element_type=F32) * SCALE)
    ga_ref[...] = lax.dot_general(values, grads, nt, preferred_element_type=F32)
    total = jnp.sum(raised_ref[...], 0, keepdims=True)
    delta = jnp.sum(raised_ref[...] * ga_ref[...], 0, keepdims=True)
    for j in range(4):
        st[0, j:j + 1, :] = total[:, j * 128:(j + 1) * 128]
        st[0, 4 + j:5 + j, :] = delta[:, j * 128:(j + 1) * 128]
    for k in (2, 3, 1):
        send(STATS, st.at[0], st.at[k], quad_peer(k))
    pending.append((STATS, st.at[pl.ds(1, 3)]))
    arrived(STATS, st.at[pl.ds(1, 3)])

    def quad_sum(at):
        outs = []
        for j in range(4):
            v = st[0, at + j:at + j + 1, :]
            for k in range(1, 4):
                i = at + (j ^ k)
                v = v + st[k, i:i + 1, :]
            outs.append(v)
        return jnp.concatenate(outs, 1)

    inverse = 1.0 / quad_sum(0)
    row_delta = quad_sum(4) * inverse
    attention = raised_ref[...] * inverse
    grad_scores = (attention * (ga_ref[...] - row_delta)).astype(BF16)
    grad_key = jnp.dot(grad_scores, queries, preferred_element_type=F32) * SCALE
    grad_value = jnp.dot(attention.astype(BF16), grads, preferred_element_type=F32)
    zb[:, 0:16, :] = grad_key.reshape(ZS, 16, 128).astype(BF16)
    zb[:, 16:32, :] = grad_value.reshape(ZS, 16, 128).astype(BF16)
    for k in FAR_FIRST:
        send(SCATTER, zb.at[k], zr.at[k], z_peer(ZS - k))
    pending.append((SCATTER, zr.at[pl.ds(1, ZS - 1)]))
    grad_query = lax.dot_general(grad_scores, keys, (((0,), (0,)), ((), ())), preferred_element_type=F32)
    dqb[...] = grad_query.reshape(4, 128, 128)
    for k in (2, 3, 1):
        send(DQ, dqb.at[k], dqr.at[k], quad_peer(k))
    pending.append((DQ, dqr.at[pl.ds(1, 3)]))
    zr[0] = zb[0]
    dqr[0] = dqb[0]

    def norm_backward(grad_normed, lo, count, gain):
        lane = iota((count, 128), 1)
        unit = norm[0, lo:lo + count, :]
        inner = grad_normed * gain
        mean_1 = jnp.sum(inner, 1, keepdims=True) * (1.0 / HD)
        mean_2 = jnp.sum(inner * unit, 1, keepdims=True) * (1.0 / HD)
        out = norm[1, lo:lo + count, :] * jnp.where(lane < HD, inner - mean_1 - unit * mean_2, 0.0)
        return out, grad_normed * unit

    arrived(DQ, dqr.at[pl.ds(1, 3)])
    dq = dqr[0] + dqr[1] + dqr[2] + dqr[3]
    gq, gain_rows = norm_backward(dq * SCALE + qgr[0, 128:256, :].astype(F32), 0, 128, gain_q)
    wg[80:88, :] = jnp.zeros((8, 128), F32)
    wg[81:82, :] = jnp.sum(gain_rows, 0, keepdims=True)
    hb[128:288, :] = jnp.concatenate([gq[0:32], gq[64:96], gq[0:64], gq[0:32]], 0).astype(BF16)
    exchange((BQ_ROW, BQ_FRAME, BQ_CORNER), Q_SPANS, hb, hbr, [seq_peer(-d) for d in (1, 16, 17)])
    for i, grp in enumerate(OWN_Q):
        ge[grp * 32:grp * 32 + 32, :] = gq[i * 32:i * 32 + 32]

    arrived(FINE, xr.at[pl.ds(1, HEADS - 1)])
    for h in range(HEADS):
        xf[:, h * 8:h * 8 + 8, :] = xr[from_col[h]].astype(F32).reshape(48, 8, 128)

    arrived(SCATTER, zr.at[pl.ds(1, ZS - 1)])
    gkv, gain_rows = norm_backward(jnp.sum(zr[...].astype(F32), 0), 128, 32, gain_kv)
    wg[82:83, :] = jnp.sum(gain_rows[0:16], 0, keepdims=True)
    wg[83:84, :] = jnp.sum(gain_rows[16:32], 0, keepdims=True)
    hb[0:128, :] = jnp.concatenate([gkv] * 4, 0).astype(BF16)
    exchange((BK_OWN, BK_ROW, BK_FRAME, BK_CORNER), KV_SPANS, hb, hbr, [feeder(d) for d in (0, 1, 16, 17)])
    back_u = (u < ROW_GROUPS - 1).astype(F32)
    back_g = (group < SEQ // ROW_GROUPS - 1).astype(F32)
    back_c = back_u * back_g

    def returned(lo, count, has):
        return hbr[lo:lo + count, :].astype(F32) * has

    exchanged((BQ_ROW, BQ_FRAME, BQ_CORNER), Q_SPANS, hbr)
    ge[2 * 32:3 * 32, :] = returned(128, 32, back_u)
    ge[5 * 32:6 * 32, :] = returned(160, 32, back_u)
    ge[6 * 32:8 * 32, :] = returned(192, 64, back_g)
    ge[8 * 32:9 * 32, :] = returned(256, 32, back_c)

    def pairs(pair_list, a):
        return [(f, t) for t, entries in enumerate(pair_list) for f, tap in entries if tap == a]

    def spread(rows, cols, target):
        return jnp.where(iota((rows, cols), 1) == target, 1.0, 0.0).astype(BF16)

    r = iota((128, 32), 0)
    spread_q = spread(128, 32, ((r & 63) >> 1) + (r >> 6))
    spread_k = spread(64, 16, (iota((64, 16), 0) + 1) >> 2)
    odd, by_four = row8 % 2 == 1, row8 % 4

    def over_blocks(v):
        return jnp.sum(v.reshape(HEADS, 8, 128), 0)

    for grp in range(9):
        exh[grp * 128:grp * 128 + 128, :] = jnp.dot(spread_q, ge[grp * 32:grp * 32 + 32, :].astype(BF16),
                                                    preferred_element_type=F32)

    def tap_rows(masked, m, ab):
        for e, v in enumerate(masked):
            wg[m * 27 + ab * 3 + e:m * 27 + ab * 3 + e + 1, :] = jnp.sum(v, 0, keepdims=True)

    for a in range(3):
        for b in range(3):
            first = second = None
            for f, t in pairs(PAIRS_Q, a):
                for rr, y in pairs(PAIRS_Q, b):
                    v, at = xf[(f * 4 + rr) * 3], (t * 3 + y) * 128
                    t1, t2 = v * exh[at:at + 64, :], v * exh[at + 64:at + 128, :]
                    first = t1 if first is None else first + t1
                    second = t2 if second is None else second + t2
            first, second = over_blocks(first), over_blocks(second)
            tap_rows((jnp.where(odd, second, 0.0), jnp.where(odd, 0.0, first), jnp.where(odd, first, 0.0)), 0, a * 3 + b)

    def key_taps(m, wide, chosen):
        for a, b in chosen:
            (f, t), = pairs(PAIRS_K, a)
            (rr, y), = pairs(PAIRS_K, b)
            v = over_blocks(xf[(f * 4 + rr) * 3 + m] * wide[t * 2 + y])
            tap_rows(tuple(jnp.where(by_four == c, v, 0.0) for c in (3, 0, 1)), m, a * 3 + b)

    def wide_key(m, group):
        at = 224 + m * 64 + group * 16
        return jnp.dot(spread_k, ge[at:at + 16, :].astype(BF16), preferred_element_type=F32)

    exchanged((BK_OWN, BK_ROW, BK_FRAME, BK_CORNER), KV_SPANS, hbr)
    for lo, at, has in ((0, 0, 1.0), (32, 16, back_u), (64, 32, back_g), (96, 48, back_c)):
        v = returned(lo, 32, has)
        ge[288 + at:304 + at, :] = v[0:16]
        ge[352 + at:368 + at, :] = v[16:32]
    for m in (1, 2):
        key_taps(m, [wide_key(m, group) for group in range(4)], [(a, b) for a in range(3) for b in range(3)])

    t16, t8 = wg[64:80, :], wg[80:88, :]
    tail = jnp.concatenate([pltpu.roll(t16, 96, 1), pltpu.roll(t16, 64, 1), pltpu.roll(t16, 32, 1),
                            jnp.where(row8 < 4, pltpu.roll(t8, 96, 1), pltpu.roll(pltpu.roll(t8, 64, 1), 4, 0)),
                            pltpu.roll(t8, 32, 1)], 0)
    wb[...] = jnp.where(iota((64, 128), 1) < HD, wg[0:64, :], tail)

    def piece(k):
        return pl.ds(pl.multiple_of(quad_index(k) * 16, 16), 16)

    for k in (2, 3, 1):
        send(SUM_QUAD, wb.at[piece(k)], kr.at[k], quad_peer(k))
    pending.append((SUM_QUAD, kr.at[pl.ds(1, 3)]))
    kr[0] = wb[piece(0), :]

    zero = jnp.zeros((8, 128), F32)
    out_rows = [[] for _ in range(HEADS)]
    for grp in range(9):
        vs = [ge[grp * 32 + j * 8:grp * 32 + j * 8 + 8, :] for j in range(4)] + [zero]
        half = [pltpu.roll(v, 4, 0) for v in vs]
        for h in range(HEADS):
            j = h // 2
            out_rows[h].append(vs[j] if h % 2 == 0 else jnp.where(row8 < 4, half[j], half[j + 1]))
    for grp in range(4):
        vs = [[ge[at:at + 8, :] for at in (288 + m * 64 + grp * 16, 296 + m * 64 + grp * 16)] + [zero] for m in range(2)]
        for h in range(HEADS):
            j, i = h // 4, h % 4
            parts = []
            for m in range(2):
                v = pltpu.roll(vs[m][j], 8 - 2 * i, 0) if i else vs[m][j]
                if i == 3:
                    v = jnp.where(row8 < 2, v, pltpu.roll(vs[m][j + 1], 2, 0))
                parts.append(v)
            out_rows[h].append(jnp.where(row8 < 4, parts[0], pltpu.roll(parts[1], 4, 0)))
    for h in range(HEADS):
        sb2[h] = jnp.concatenate(out_rows[h] + [zero], 0).astype(BF16)
    for k in range(1, HEADS):
        peer = head_peer(k)
        send(A2A_B, sb2.at[peer[1]], rb2.at[k], peer)
    pending.append((A2A_B, rb2.at[pl.ds(1, HEADS - 1)]))
    rb2[0] = sb2[n]

    arrived(SUM_QUAD, kr.at[pl.ds(1, 3)])
    zs[0] = (kr[0] + kr[1] + kr[2] + kr[3]).astype(zs.dtype)
    for k in FAR_FIRST:
        send(SUM_Z, zs.at[0], zs.at[k], z_peer(k))
    pending.append((SUM_Z, zs.at[pl.ds(1, ZS - 1)]))

    arrived(A2A_B, rb2.at[pl.ds(1, HEADS - 1)])
    tiles = merge_heads([rb2[from_col[h]].astype(F32) for h in range(HEADS)])
    for j in range(6):
        gall[:, j * 128:(j + 1) * 128] = tiles[j].astype(BF16)
    r = iota((208, 112), 0)
    grp, late, i = r >> 4, (r >> 3) & 1, r & 7
    ex[...] = jnp.dot(spread(208, 112, grp * 8 + jnp.where(grp < 9, (i >> 1) + late, ((i + 1) >> 2) + 4 * late)),
                      gall[...], preferred_element_type=F32)

    def g_at(grp, late):
        at = grp * 16 + late * 8
        return ex[at:at + 8, :]

    def reached(pair_list, f):
        return [(t, a) for t, entries in enumerate(pair_list) for ff, a in entries if ff == f]

    for f in range(4):
        for rr in range(4):
            q_sum = None
            for t, a in reached(PAIRS_Q, f):
                for y, b in reached(PAIRS_Q, rr):
                    term = g_at(t * 3 + y, 0) * wt[0, a * 3 + b] + g_at(t * 3 + y, 1) * wt[1, a * 3 + b]
                    q_sum = term if q_sum is None else q_sum + term
            gxv[(f * 4 + rr) * 3] = q_sum.astype(BF16)
            for m in (1, 2):
                k_sum = jnp.zeros((8, 768), F32)
                for t, a in reached(PAIRS_K, f):
                    for y, b in reached(PAIRS_K, rr):
                        k_sum = g_at(9 + t * 2 + y, m - 1) * wt[1 + m, a * 3 + b]
                gxv[(f * 4 + rr) * 3 + m] = k_sum.astype(BF16)
    store = pltpu.make_async_copy(gxv, gx_ref, local.at[4])
    store.start()

    arrived(SUM_Z, zs.at[pl.ds(1, ZS - 1)])
    v = zs[z].astype(F32)
    for k in range(1, ZS):
        v = v + zs[lax.rem(z - k + ZS, ZS)].astype(F32)
    fr[0] = v.astype(BF16)
    for p in range(31, 0, -1):
        send(SPREAD, fr.at[0], fr.at[p], plane_peer(p))
    pending.append((SPREAD, fr.at[pl.ds(1, 31)]))
    arrived(SPREAD, fr.at[pl.ds(1, 31)])

    lane16 = iota((16, 128), 1)
    unpacked, gains = [], None
    for h in range(HEADS):
        at = [fr[lax.rem(yl + q // 2, 2) * (2 * HEADS) + lax.rem(core + q % 2, 2) * HEADS + from_col[h]].astype(F32) for q in range(4)]
        t16 = jnp.where(lane16 < 32, pltpu.roll(at[0], 32, 1), jnp.where(
            lane16 < 64, pltpu.roll(at[1], 64, 1), pltpu.roll(at[2], 96, 1)))
        lo, hi = at[3][0:8], at[3][8:16]
        t8 = jnp.where(lane8 < 32, pltpu.roll(lo, 32, 1), jnp.where(
            lane8 < 64, pltpu.roll(pltpu.roll(lo, 64, 1), 4, 0), pltpu.roll(hi, 96, 1)))
        gains = t8 if gains is None else gains + t8
        unpacked.append(jnp.concatenate(at + [t16, t8], 0))
    for j, v in enumerate(merge_heads(unpacked)):
        flat[j * 88:j * 88 + 88, :] = v
    for j in range(6):
        for m in range(3):
            gw_ref[m, :, j * 128:(j + 1) * 128] = flat[j * 88 + m * 27:j * 88 + m * 27 + 27, :]
    gg_ref[...] = gains[1:4, 0:HD]
    store.wait()
    drain()


def shards(qkv_fine, grad_out, pool_weight, norm_gain):
    x = qkv_fine[0].transpose(0, 1, 3, 2, 4).reshape(48, 8, 768)
    w = pool_weight.transpose(1, 0, 2)
    vmem = pl.BlockSpec(memory_space=pltpu.VMEM)
    hbm = pl.BlockSpec(memory_space=pl.ANY)
    scratch = [
        ((48, 8, 768), BF16),
        (grad_out.shape[1:], BF16),
        (w.shape, BF16),
        (norm_gain.shape, F32),
        ((3, 27, 768), F32),
        ((4, 9, 8, 768), F32),
        ((8, 32, 128), BF16),
        ((8, 32, 128), BF16),
        ((8, 96, 128), BF16),
        ((8, 96, 128), BF16),
        ((8, 384, 128), BF16),
        ((8, 384, 128), BF16),
        ((48, 64, 128), F32),
        ((416, 128), F32),
        ((288, 128), BF16),
        ((288, 128), BF16),
        ((2, 160, 128), F32),
        ((ZS, 32, 128), BF16),
        ((4, 256, 128), BF16),
        ((256, 512), F32),
        ((256, 512), F32),
        ((4, 8, 128), F32),
        ((4, 128, 128), F32),
        ((4, 128, 128), F32),
        ((ZS, 32, 128), BF16),
        ((ZS, 32, 128), BF16),
        ((288, 128), BF16),
        ((288, 128), BF16),
        ((416, 128), F32),
        ((9 * 128, 128), F32),
        ((8, 112, 128), BF16),
        ((8, 112, 128), BF16),
        ((112, 768), BF16),
        ((208, 768), F32),
        ((48, 8, 768), BF16),
        ((88, 128), F32),
        ((64, 128), F32),
        ((4, 16, 128), F32),
        ((ZS, 16, 128), BF16),
        ((32, 16, 128), BF16),
        ((6 * 88, 128), F32),
        ((8, 128), F32),
    ]
    gx, gw, gg = pl.pallas_call(
        kernel,
        out_shape=(jax.ShapeDtypeStruct(x.shape, BF16), jax.ShapeDtypeStruct(w.shape, F32),
                   jax.ShapeDtypeStruct(norm_gain.shape, F32)),
        in_specs=[hbm] * 4,
        out_specs=(hbm, vmem, vmem),
        scratch_shapes=[pltpu.VMEM(shape, kind) for shape, kind in scratch]
        + [pltpu.SemaphoreType.DMA((26,)), pltpu.SemaphoreType.DMA((26,)), pltpu.SemaphoreType.DMA((5,)),
           pltpu.SemaphoreType.REGULAR((2,))],
        compiler_params=pltpu.CompilerParams(collective_id=0, has_side_effects=True,
                                             vmem_limit_bytes=60 * 1024 * 1024),
    )(x, grad_out[0], w, norm_gain)
    return gx.reshape(4, 4, 3, 8, 768).transpose(0, 1, 3, 2, 4)[None], gw.transpose(1, 0, 2), gg


def solution(mesh):
    in_specs = (P("seq", None, None, "head", None, None), P("seq", None, None, "head", None), P(), P())
    out_specs = (P("seq", None, None, "head", None, None), P(), P())
    return jax.shard_map(shards, mesh=mesh, in_specs=in_specs, out_specs=out_specs, check_vma=False)
```

```python
import jax
import jax.numpy as jnp
from jax import lax
from jax.experimental import pallas as pl
from jax.experimental.pallas import tpu as pltpu
from jax.sharding import PartitionSpec as P

MESH = pl.DeviceIdType.MESH
F32 = jnp.float32
BF16 = jnp.bfloat16
HD = 96
HEADS = 8
ROW_GROUPS = 16
SEQ = 64
ZS = 16
SCALE = HD ** -0.5

PAIRS_Q = (((0, 1), (1, 2)), ((1, 0), (2, 1), (3, 2)), ((3, 0),))
PAIRS_K = (((0, 1), (1, 2)), ((3, 0),))
OWN_Q = (0, 1, 3, 4)

(A2A_K, A2A_Q, FINE, KV_OWN, KV_ROW, KV_FRAME, KV_CORNER, Q_ROW, Q_FRAME, Q_CORNER, GATHER, QUAD, STATS, DQ, SCATTER,
 BQ_ROW, BQ_FRAME, BQ_CORNER, BK_OWN, BK_ROW, BK_FRAME, BK_CORNER, A2A_B, SUM_QUAD, SUM_Z, SPREAD) = range(26)
FAR_FIRST = (8, 7, 9, 6, 10, 5, 11, 4, 12, 3, 13, 2, 14, 1, 15)
KV_SPANS = ((0, 32), (32, 32), (64, 32), (96, 32))
Q_SPANS = ((128, 64), (192, 64), (256, 32))
HALF_WAY = 12


def iota(shape, dim):
    return lax.broadcasted_iota(jnp.int32, shape, dim)


def up(x, by):
    size = x.shape[0]
    return pltpu.roll(x, (size - by) % size, 0)


def split_heads(tiles):
    lane = iota(tiles[0].shape, 1)
    heads = []
    for n in range(HEADS):
        t = tiles[n // 4 * 3:n // 4 * 3 + 3]
        if n % 4 == 0:
            v = t[0]
        elif n % 4 == 1:
            v = jnp.where(lane < 32, pltpu.roll(t[0], 32, 1), pltpu.roll(t[1], 32, 1))
        elif n % 4 == 2:
            v = jnp.where(lane < 64, pltpu.roll(t[1], 64, 1), pltpu.roll(t[2], 64, 1))
        else:
            v = pltpu.roll(t[2], 96, 1)
        heads.append(jnp.where(lane < HD, v, 0.0))
    return heads


def merge_heads(h):
    lane = iota(h[0].shape, 1)
    tiles = []
    for half in (0, 4):
        a, b, c, d = h[half:half + 4]
        tiles.append(jnp.where(lane < 96, a, pltpu.roll(b, 96, 1)))
        tiles.append(jnp.where(lane < 64, pltpu.roll(b, 96, 1), pltpu.roll(c, 64, 1)))
        tiles.append(jnp.where(lane < 32, pltpu.roll(c, 64, 1), pltpu.roll(d, 32, 1)))
    return tiles


def tiles_of(v):
    return [v[:, j * 128:(j + 1) * 128] for j in range(6)]


def kernel(x_ref, g_hbm, w_hbm, gain_hbm, gx_ref, gw_ref, gg_ref,
           xv, g_ref, w_ref, gain_ref, wf, wt, sbk, rbk, sbq, rbq, xs, xr, xf, pe, hs, hr, norm, kvg, qgr, raised_ref, ga_ref, st, dqb, dqr, zb, zr,
           hb, hbr, ge, exh, sb2, rb2, gall, ex, gxv, wg, wb, kr, zs, fr, flat, gsc, ss, rs, local, ready):
    s = lax.axis_index("seq")
    n = lax.axis_index("head")
    group, u = s // ROW_GROUPS, s % ROW_GROUPS
    yl, z, core = s // (2 * ZS), s // 2 % ZS, s % 2

    loads = [pltpu.make_async_copy(src, dst, local.at[i]) for i, (src, dst) in enumerate(
        ((w_hbm, w_ref), (gain_hbm, gain_ref), (x_ref, xv), (g_hbm, g_ref)))]
    for load in loads:
        load.start()

    def head_peer(k):
        return (s, lax.rem(n + k, HEADS))

    def z_peer(k):
        return (yl * (2 * ZS) + lax.rem(z + k, ZS) * 2 + core, n)

    def quad_peer(k):
        return (lax.rem(yl + k // 2, 2) * (2 * ZS) + z * 2 + lax.rem(core + k % 2, 2), n)

    def quad_index(k):
        return lax.rem(yl + k // 2, 2) * 2 + lax.rem(core + k % 2, 2)

    def plane_peer(p):
        return (quad_peer(p // HEADS)[0], lax.rem(n + p % HEADS, HEADS))

    def seq_peer(d):
        return (lax.rem(s + d + SEQ, SEQ), n)

    def owner(d):
        block = lax.rem(s + d, SEQ)
        return (block // (2 * ZS) * (2 * ZS) + lax.rem(block // 2 % ZS + HALF_WAY, ZS) * 2 + block % 2, n)

    owned = yl * (2 * ZS) + lax.rem(z + ZS - HALF_WAY, ZS) * 2 + core

    def feeder(d):
        return (lax.rem(owned - d + SEQ, SEQ), n)


    barrier = pltpu.get_barrier_semaphore()
    greeted = [owner(17), feeder(17), owner(16), feeder(16), owner(1), feeder(1)]
    greeted += [z_peer(k) for k in (4, 12, 3, 13)] + [head_peer(k) for k in (5, 3, 7, 1, 4)]
    greeted += [z_peer(k) for k in (2, 14, 1, 15)] + [seq_peer(1), seq_peer(-1), seq_peer(1 + SEQ // 2), seq_peer(-1 - SEQ // 2)]
    greeted += [head_peer(6), head_peer(2)] + [quad_peer(k) for k in (3, 2, 1)]
    for peer in greeted:
        pl.semaphore_signal(barrier, inc=1, device_id=peer, device_id_type=MESH)

    def send(stage, src, dst, peer):
        pltpu.make_async_remote_copy(src_ref=src, dst_ref=dst, send_sem=ss.at[stage], recv_sem=rs.at[stage],
                                     device_id=peer, device_id_type=MESH).start()

    def arrived(stage, ref):
        pltpu.make_async_copy(ref, ref, rs.at[stage]).wait()

    def hand_on(stage, peers):
        for peer in peers:
            pl.semaphore_signal(ready.at[stage], inc=1, device_id=peer, device_id_type=MESH)

    four_on = [z_peer(4), z_peer(12)]
    pending = []

    def drain():
        for stage, ref in pending:
            pltpu.make_async_copy(ref, ref, ss.at[stage]).wait()

    row = iota((8, 768), 0)
    row8 = iota((8, 128), 0)
    lane8 = iota((8, 128), 1)
    loads[0].wait()
    wf[...] = w_ref[...].astype(F32)

    def taps(ab, carry):
        def one(m, e):
            return jnp.broadcast_to(wf[m, pl.ds(ab * 3 + e, 1), :], (8, 768))
        wt[0, ab] = jnp.where(row % 2 == 0, one(0, 1), one(0, 2))
        wt[1, ab] = jnp.where(row % 2 == 1, one(0, 0), 0.0)
        for m in (1, 2):
            wt[1 + m, ab] = jnp.where(row % 4 == 0, one(m, 1), jnp.where(
                row % 4 == 1, one(m, 2), jnp.where(row % 4 == 3, one(m, 0), 0.0)))
        return carry
    lax.fori_loop(0, 9, taps, 0)
    loads[1].wait()
    gsc[...] = jnp.zeros_like(gsc)
    gsc[0:3, 0:HD] = gain_ref[...]
    loads[2].wait()
    loads[3].wait()

    def fine(m, f, r):
        return xv[(f * 4 + r) * 3 + m].astype(F32)

    def store_heads(dst, groups):
        for p in range(len(groups) // 2):
            v = jnp.concatenate(groups[2 * p:2 * p + 2], 0)
            for h, part in enumerate(split_heads(tiles_of(v))):
                dst[h, p * 16:p * 16 + 16, :] = part.astype(BF16)

    groups = []
    for t in range(2):
        for y in range(2):
            both = []
            for m in (1, 2):
                k_sum = None
                for f, a in PAIRS_K[t]:
                    for r, b in PAIRS_K[y]:
                        tk = fine(m, f, r) * wt[1 + m, a * 3 + b]
                        k_sum = tk if k_sum is None else k_sum + tk
                t1 = k_sum + up(k_sum, 1)
                both.append(jnp.where(row == 0, t1, jnp.where(row == 1, up(t1, 2) + up(k_sum, 4), jnp.where(
                    row == 2, up(k_sum, 5), 0.0))))
            groups.append(both[0] + pltpu.roll(both[1], 4, 0))
    store_heads(sbk, groups)
    groups = []
    for t in range(3):
        for y in range(3):
            a_sum = b_sum = None
            for f, a in PAIRS_Q[t]:
                for r, b in PAIRS_Q[y]:
                    v = fine(0, f, r)
                    ta, tb = v * wt[0, a * 3 + b], v * wt[1, a * 3 + b]
                    a_sum = ta if a_sum is None else a_sum + ta
                    b_sum = tb if b_sum is None else b_sum + tb
            b1 = pltpu.roll(b_sum, 1, 0)
            e = a_sum + up(a_sum, 1) + jnp.where(row == 0, 0.0, b1)
            v = jnp.where(row == 0, e, jnp.where(row == 1, up(e, 1), jnp.where(row == 2, up(e, 2), jnp.where(
                row == 3, up(e, 3), jnp.where(row == 4, up(b1, 4), 0.0)))))
            groups.append(v)
    groups.append(jnp.zeros((8, 768), F32))
    for t in range(2):
        groups.append(jnp.concatenate([g_ref[t, 0].astype(F32), g_ref[t, 1].astype(F32)], 0))
    store_heads(sbq, groups)

    def split_fine(p, carry):
        v = jnp.concatenate([xv[2 * p].astype(F32), xv[2 * p + 1].astype(F32)], 0)
        for h, part in enumerate(split_heads(tiles_of(v))):
            xs[h, pl.ds(pl.multiple_of(p * 16, 16), 16), :] = part.astype(BF16)
        return carry
    lax.fori_loop(0, 24, split_fine, 0)

    pl.semaphore_wait(barrier, len(greeted))
    hand_on(0, four_on)
    for stage, src, dst in ((A2A_K, sbk, rbk), (A2A_Q, sbq, rbq)):
        for k in (5, 3, 7, 1, 4, 6, 2):
            peer = head_peer(k)
            send(stage, src.at[peer[1]], dst.at[k], peer)
        pending.append((stage, dst.at[pl.ds(1, HEADS - 1)]))
        dst[0] = src[n]
    pl.semaphore_wait(ready.at[0], 2)
    hand_on(1, four_on)
    arrived(A2A_K, rbk.at[pl.ds(1, HEADS - 1)])

    from_col = [lax.rem(n - h + HEADS, HEADS) for h in range(HEADS)]
    sets = [rbk[from_col[h]].astype(F32) for h in range(HEADS)]
    for grp in range(4):
        parts = [v[grp * 8:grp * 8 + 8] for v in sets]
        for m in range(2):
            if m == 0:
                own = [jnp.where(row8 < 4, p, 0.0) for p in parts]
            else:
                own = [pltpu.roll(jnp.where(row8 >= 4, p, 0.0), 4, 0) for p in parts]
            last = [pltpu.roll(own[4 * j + 3], 6, 0) for j in range(2)]
            for j in range(2):
                v = own[4 * j] + pltpu.roll(own[4 * j + 1], 2, 0) + pltpu.roll(own[4 * j + 2], 4, 0)
                v = v + jnp.where(row8 >= 4, last[j], 0.0)
                if j:
                    v = v + jnp.where(row8 == 0, last[0], 0.0)
                at = 288 + m * 64 + grp * 16 + j * 8
                pe[at:at + 8, :] = v

    def pq(t, y):
        return pe[(t * 3 + y) * 32:(t * 3 + y) * 32 + 32, :]

    def pkv(t, y):
        at = 288 + (t * 2 + y) * 16
        return jnp.concatenate([pe[at:at + 16, :], pe[at + 64:at + 80, :]], 0)

    def exchange(stages, spans, src, dst, peers):
        for stage, (lo, count), peer in list(zip(stages, spans, peers))[::-1]:
            send(stage, src.at[pl.ds(lo, count)], dst.at[pl.ds(lo, count)], peer)
            pending.append((stage, dst.at[pl.ds(lo, count)]))

    def exchanged(stages, spans, dst):
        for stage, (lo, count) in zip(stages, spans):
            arrived(stage, dst.at[pl.ds(lo, count)])

    hs[0:128, :] = jnp.concatenate([pkv(0, 0), pkv(0, 1), pkv(1, 0), pkv(1, 1)], 0).astype(BF16)
    exchange((KV_OWN, KV_ROW, KV_FRAME, KV_CORNER), KV_SPANS, hs, hr, [owner(d) for d in (0, 1, 16, 17)])
    arrived(A2A_Q, rbq.at[pl.ds(1, HEADS - 1)])
    sets = [rbq[from_col[h]].astype(F32) for h in range(HEADS)]
    for grp in range(9):
        parts = [v[grp * 8:grp * 8 + 8] for v in sets]
        rolled = [pltpu.roll(parts[2 * j + 1], 4, 0) for j in range(4)]
        for j in range(4):
            v = parts[2 * j] + jnp.where(row8 >= 4, rolled[j], 0.0)
            if j:
                v = v + jnp.where(row8 == 0, rolled[j - 1], 0.0)
            pe[grp * 32 + j * 8:grp * 32 + j * 8 + 8, :] = v
    hs[128:288, :] = jnp.concatenate([pq(0, 2), pq(1, 2), pq(2, 0), pq(2, 1), pq(2, 2)], 0).astype(BF16)
    pl.semaphore_wait(ready.at[1], 2)
    exchange((Q_ROW, Q_FRAME, Q_CORNER), Q_SPANS, hs, hr, [seq_peer(d) for d in (1, 16, 17)])
    for k in range(1, HEADS):
        peer = head_peer(k)
        send(FINE, xs.at[peer[1]], xr.at[k], peer)
    pending.append((FINE, xr.at[pl.ds(1, HEADS - 1)]))
    xr[0] = xs[n]

    for t in range(2):
        for y in range(2):
            vs = []
            for j in range(4):
                a, b = (sets[2 * j + i][80 + t * 8:88 + t * 8] for i in range(2))
                if y == 0:
                    vs.append(jnp.where(row8 < 4, a, pltpu.roll(b, 4, 0)))
                else:
                    vs.append(jnp.where(row8 < 4, pltpu.roll(a, 4, 0), b))
            at = 128 + (t * 2 + y) * 32
            qgr[0, at:at + 32, :] = jnp.concatenate(vs, 0).astype(BF16)

    def layer_norm(pooled, lo, count, gain):
        lane = iota((count, 128), 1)
        centred = jnp.where(lane < HD, pooled - jnp.sum(pooled, 1, keepdims=True) * (1.0 / HD), 0.0)
        rstd = lax.rsqrt(jnp.sum(centred * centred, 1, keepdims=True) * (1.0 / HD) + 1e-6)
        unit = centred * rstd
        norm[0, lo:lo + count, :] = unit
        norm[1, lo:lo + count, :] = jnp.broadcast_to(rstd, (count, 128))
        return (unit * gain).astype(BF16)

    has_u = (u > 0).astype(F32)
    has_g = (group > 0).astype(F32)
    has_c = has_u * has_g

    def border(lo, count, has):
        return hr[lo:lo + count, :].astype(F32) * has

    exchanged((KV_OWN, KV_ROW, KV_FRAME, KV_CORNER), KV_SPANS, hr)
    own_u = (owned % ROW_GROUPS > 0).astype(F32)
    own_g = (owned // ROW_GROUPS > 0).astype(F32)
    gain_kv = jnp.where(iota((32, 128), 0) < 16, gsc[1:2, :], gsc[2:3, :])
    gain_q = jnp.broadcast_to(gsc[0:1, :], (128, 128))
    kvg[0] = layer_norm(hr[0:32, :].astype(F32) + border(32, 32, own_u) + border(64, 32, own_g) + border(96, 32, own_u * own_g),
                        128, 32, gain_kv)
    for k in FAR_FIRST:
        send(GATHER, kvg.at[0], kvg.at[k], z_peer(k))
    pending.append((GATHER, kvg.at[pl.ds(1, ZS - 1)]))

    exchanged((Q_ROW, Q_FRAME, Q_CORNER), Q_SPANS, hr)
    q00 = pq(0, 0) + border(128, 32, has_u) + border(192, 32, has_g) + border(256, 32, has_c)
    q01 = pq(0, 1) + border(224, 32, has_g)
    q10 = pq(1, 0) + border(160, 32, has_u)
    qgr[0, 0:128, :] = layer_norm(jnp.concatenate([q00, q01, q10, pq(1, 1)], 0), 0, 128, gain_q)
    for k in (2, 3, 1):
        send(QUAD, qgr.at[0], qgr.at[k], quad_peer(k))
    pending.append((QUAD, qgr.at[pl.ds(1, 3)]))
    arrived(QUAD, qgr.at[pl.ds(1, 3)])
    arrived(GATHER, kvg.at[pl.ds(1, ZS - 1)])

    keys = kvg[:, 0:16, :].reshape(256, 128)
    values = kvg[:, 16:32, :].reshape(256, 128)
    queries = qgr[:, 0:128, :].reshape(512, 128)
    grads = qgr[:, 128:256, :].reshape(512, 128)
    nt = (((1,), (1,)), ((), ()))
    raised_ref[...] = jnp.exp(lax.dot_general(keys, queries, nt, preferred_element_type=F32) * SCALE)
    ga_ref[...] = lax.dot_general(values, grads, nt, preferred_element_type=F32)
    total = jnp.sum(raised_ref[...], 0, keepdims=True)
    delta = jnp.sum(raised_ref[...] * ga_ref[...], 0, keepdims=True)
    for j in range(4):
        st[0, j:j + 1, :] = total[:, j * 128:(j + 1) * 128]
        st[0, 4 + j:5 + j, :] = delta[:, j * 128:(j + 1) * 128]
    for k in (2, 3, 1):
        send(STATS, st.at[0], st.at[k], quad_peer(k))
    pending.append((STATS, st.at[pl.ds(1, 3)]))
    arrived(STATS, st.at[pl.ds(1, 3)])

    def quad_sum(at):
        outs = []
        for j in range(4):
            v = st[0, at + j:at + j + 1, :]
            for k in range(1, 4):
                i = at + (j ^ k)
                v = v + st[k, i:i + 1, :]
            outs.append(v)
        return jnp.concatenate(outs, 1)

    inverse = 1.0 / quad_sum(0)
    row_delta = quad_sum(4) * inverse
    attention = raised_ref[...] * inverse
    grad_scores = (attention * (ga_ref[...] - row_delta)).astype(BF16)
    grad_key = jnp.dot(grad_scores, queries, preferred_element_type=F32) * SCALE
    grad_value = jnp.dot(attention.astype(BF16), grads, preferred_element_type=F32)
    zb[:, 0:16, :] = grad_key.reshape(ZS, 16, 128).astype(BF16)
    zb[:, 16:32, :] = grad_value.reshape(ZS, 16, 128).astype(BF16)
    for k in FAR_FIRST:
        send(SCATTER, zb.at[k], zr.at[k], z_peer(ZS - k))
    pending.append((SCATTER, zr.at[pl.ds(1, ZS - 1)]))
    grad_query = lax.dot_general(grad_scores, keys, (((0,), (0,)), ((), ())), preferred_element_type=F32)
    dqb[...] = grad_query.reshape(4, 128, 128)
    for k in (2, 3, 1):
        send(DQ, dqb.at[k], dqr.at[k], quad_peer(k))
    pending.append((DQ, dqr.at[pl.ds(1, 3)]))
    zr[0] = zb[0]
    dqr[0] = dqb[0]

    def norm_backward(grad_normed, lo, count, gain):
        lane = iota((count, 128), 1)
        unit = norm[0, lo:lo + count, :]
        inner = grad_normed * gain
        mean_1 = jnp.sum(inner, 1, keepdims=True) * (1.0 / HD)
        mean_2 = jnp.sum(inner * unit, 1, keepdims=True) * (1.0 / HD)
        out = norm[1, lo:lo + count, :] * jnp.where(lane < HD, inner - mean_1 - unit * mean_2, 0.0)
        return out, grad_normed * unit

    arrived(DQ, dqr.at[pl.ds(1, 3)])
    dq = dqr[0] + dqr[1] + dqr[2] + dqr[3]
    gq, gain_rows = norm_backward(dq * SCALE + qgr[0, 128:256, :].astype(F32), 0, 128, gain_q)
    wg[80:88, :] = jnp.zeros((8, 128), F32)
    wg[81:82, :] = jnp.sum(gain_rows, 0, keepdims=True)
    hb[128:288, :] = jnp.concatenate([gq[0:32], gq[64:96], gq[0:64], gq[0:32]], 0).astype(BF16)
    exchange((BQ_ROW, BQ_FRAME, BQ_CORNER), Q_SPANS, hb, hbr, [seq_peer(-d) for d in (1, 16, 17)])
    for i, grp in enumerate(OWN_Q):
        ge[grp * 32:grp * 32 + 32, :] = gq[i * 32:i * 32 + 32]

    arrived(FINE, xr.at[pl.ds(1, HEADS - 1)])
    for h in range(HEADS):
        xf[:, h * 8:h * 8 + 8, :] = xr[from_col[h]].astype(F32).reshape(48, 8, 128)

    arrived(SCATTER, zr.at[pl.ds(1, ZS - 1)])
    gkv, gain_rows = norm_backward(jnp.sum(zr[...].astype(F32), 0), 128, 32, gain_kv)
    wg[82:83, :] = jnp.sum(gain_rows[0:16], 0, keepdims=True)
    wg[83:84, :] = jnp.sum(gain_rows[16:32], 0, keepdims=True)
    hb[0:128, :] = jnp.concatenate([gkv] * 4, 0).astype(BF16)
    exchange((BK_OWN, BK_ROW, BK_FRAME, BK_CORNER), KV_SPANS, hb, hbr, [feeder(d) for d in (0, 1, 16, 17)])
    back_u = (u < ROW_GROUPS - 1).astype(F32)
    back_g = (group < SEQ // ROW_GROUPS - 1).astype(F32)
    back_c = back_u * back_g

    def returned(lo, count, has):
        return hbr[lo:lo + count, :].astype(F32) * has

    exchanged((BQ_ROW, BQ_FRAME, BQ_CORNER), Q_SPANS, hbr)
    ge[2 * 32:3 * 32, :] = returned(128, 32, back_u)
    ge[5 * 32:6 * 32, :] = returned(160, 32, back_u)
    ge[6 * 32:8 * 32, :] = returned(192, 64, back_g)
    ge[8 * 32:9 * 32, :] = returned(256, 32, back_c)

    def pairs(pair_list, a):
        return [(f, t) for t, entries in enumerate(pair_list) for f, tap in entries if tap == a]

    def spread(rows, cols, target):
        return jnp.where(iota((rows, cols), 1) == target, 1.0, 0.0).astype(BF16)

    r = iota((128, 32), 0)
    spread_q = spread(128, 32, ((r & 63) >> 1) + (r >> 6))
    spread_k = spread(64, 16, (iota((64, 16), 0) + 1) >> 2)
    odd, by_four = row8 % 2 == 1, row8 % 4

    def over_blocks(v):
        return jnp.sum(v.reshape(HEADS, 8, 128), 0)

    for grp in range(9):
        exh[grp * 128:grp * 128 + 128, :] = jnp.dot(spread_q, ge[grp * 32:grp * 32 + 32, :].astype(BF16),
                                                    preferred_element_type=F32)

    def tap_rows(masked, m, ab):
        for e, v in enumerate(masked):
            wg[m * 27 + ab * 3 + e:m * 27 + ab * 3 + e + 1, :] = jnp.sum(v, 0, keepdims=True)

    for a in range(3):
        for b in range(3):
            first = second = None
            for f, t in pairs(PAIRS_Q, a):
                for rr, y in pairs(PAIRS_Q, b):
                    v, at = xf[(f * 4 + rr) * 3], (t * 3 + y) * 128
                    t1, t2 = v * exh[at:at + 64, :], v * exh[at + 64:at + 128, :]
                    first = t1 if first is None else first + t1
                    second = t2 if second is None else second + t2
            first, second = over_blocks(first), over_blocks(second)
            tap_rows((jnp.where(odd, second, 0.0), jnp.where(odd, 0.0, first), jnp.where(odd, first, 0.0)), 0, a * 3 + b)

    def key_taps(m, wide, chosen):
        for a, b in chosen:
            (f, t), = pairs(PAIRS_K, a)
            (rr, y), = pairs(PAIRS_K, b)
            v = over_blocks(xf[(f * 4 + rr) * 3 + m] * wide[t * 2 + y])
            tap_rows(tuple(jnp.where(by_four == c, v, 0.0) for c in (3, 0, 1)), m, a * 3 + b)

    def wide_key(m, group):
        at = 224 + m * 64 + group * 16
        return jnp.dot(spread_k, ge[at:at + 16, :].astype(BF16), preferred_element_type=F32)

    exchanged((BK_OWN, BK_ROW, BK_FRAME, BK_CORNER), KV_SPANS, hbr)
    for lo, at, has in ((0, 0, 1.0), (32, 16, back_u), (64, 32, back_g), (96, 48, back_c)):
        v = returned(lo, 32, has)
        ge[288 + at:304 + at, :] = v[0:16]
        ge[352 + at:368 + at, :] = v[16:32]
    for m in (1, 2):
        key_taps(m, [wide_key(m, group) for group in range(4)], [(a, b) for a in range(3) for b in range(3)])

    t16, t8 = wg[64:80, :], wg[80:88, :]
    tail = jnp.concatenate([pltpu.roll(t16, 96, 1), pltpu.roll(t16, 64, 1), pltpu.roll(t16, 32, 1),
                            jnp.where(row8 < 4, pltpu.roll(t8, 96, 1), pltpu.roll(pltpu.roll(t8, 64, 1), 4, 0)),
                            pltpu.roll(t8, 32, 1)], 0)
    wb[...] = jnp.where(iota((64, 128), 1) < HD, wg[0:64, :], tail)

    def piece(k):
        return pl.ds(pl.multiple_of(quad_index(k) * 16, 16), 16)

    for k in (2, 3, 1):
        send(SUM_QUAD, wb.at[piece(k)], kr.at[k], quad_peer(k))
    pending.append((SUM_QUAD, kr.at[pl.ds(1, 3)]))
    kr[0] = wb[piece(0), :]

    zero = jnp.zeros((8, 128), F32)
    out_rows = [[] for _ in range(HEADS)]
    for grp in range(9):
        vs = [ge[grp * 32 + j * 8:grp * 32 + j * 8 + 8, :] for j in range(4)] + [zero]
        half = [pltpu.roll(v, 4, 0) for v in vs]
        for h in range(HEADS):
            j = h // 2
            out_rows[h].append(vs[j] if h % 2 == 0 else jnp.where(row8 < 4, half[j], half[j + 1]))
    for grp in range(4):
        vs = [[ge[at:at + 8, :] for at in (288 + m * 64 + grp * 16, 296 + m * 64 + grp * 16)] + [zero] for m in range(2)]
        for h in range(HEADS):
            j, i = h // 4, h % 4
            parts = []
            for m in range(2):
                v = pltpu.roll(vs[m][j], 8 - 2 * i, 0) if i else vs[m][j]
                if i == 3:
                    v = jnp.where(row8 < 2, v, pltpu.roll(vs[m][j + 1], 2, 0))
                parts.append(v)
            out_rows[h].append(jnp.where(row8 < 4, parts[0], pltpu.roll(parts[1], 4, 0)))
    for h in range(HEADS):
        sb2[h] = jnp.concatenate(out_rows[h] + [zero], 0).astype(BF16)
    for k in range(1, HEADS):
        peer = head_peer(k)
        send(A2A_B, sb2.at[peer[1]], rb2.at[k], peer)
    pending.append((A2A_B, rb2.at[pl.ds(1, HEADS - 1)]))
    rb2[0] = sb2[n]

    arrived(SUM_QUAD, kr.at[pl.ds(1, 3)])
    zs[0] = (kr[0] + kr[1] + kr[2] + kr[3]).astype(zs.dtype)
    for k in FAR_FIRST:
        send(SUM_Z, zs.at[0], zs.at[k], z_peer(k))
    pending.append((SUM_Z, zs.at[pl.ds(1, ZS - 1)]))

    arrived(A2A_B, rb2.at[pl.ds(1, HEADS - 1)])
    tiles = merge_heads([rb2[from_col[h]].astype(F32) for h in range(HEADS)])
    for j in range(6):
        gall[:, j * 128:(j + 1) * 128] = tiles[j].astype(BF16)
    r = iota((208, 112), 0)
    grp, late, i = r >> 4, (r >> 3) & 1, r & 7
    ex[...] = jnp.dot(spread(208, 112, grp * 8 + jnp.where(grp < 9, (i >> 1) + late, ((i + 1) >> 2) + 4 * late)),
                      gall[...], preferred_element_type=F32)

    def g_at(grp, late):
        at = grp * 16 + late * 8
        return ex[at:at + 8, :]

    def reached(pair_list, f):
        return [(t, a) for t, entries in enumerate(pair_list) for ff, a in entries if ff == f]

    for f in range(4):
        for rr in range(4):
            q_sum = None
            for t, a in reached(PAIRS_Q, f):
                for y, b in reached(PAIRS_Q, rr):
                    term = g_at(t * 3 + y, 0) * wt[0, a * 3 + b] + g_at(t * 3 + y, 1) * wt[1, a * 3 + b]
                    q_sum = term if q_sum is None else q_sum + term
            gxv[(f * 4 + rr) * 3] = q_sum.astype(BF16)
            for m in (1, 2):
                k_sum = jnp.zeros((8, 768), F32)
                for t, a in reached(PAIRS_K, f):
                    for y, b in reached(PAIRS_K, rr):
                        k_sum = g_at(9 + t * 2 + y, m - 1) * wt[1 + m, a * 3 + b]
                gxv[(f * 4 + rr) * 3 + m] = k_sum.astype(BF16)
    store = pltpu.make_async_copy(gxv, gx_ref, local.at[4])
    store.start()

    arrived(SUM_Z, zs.at[pl.ds(1, ZS - 1)])
    v = zs[z].astype(F32)
    for k in range(1, ZS):
        v = v + zs[lax.rem(z - k + ZS, ZS)].astype(F32)
    fr[0] = v.astype(BF16)
    for p in range(31, 0, -1):
        send(SPREAD, fr.at[0], fr.at[p], plane_peer(p))
    pending.append((SPREAD, fr.at[pl.ds(1, 31)]))
    arrived(SPREAD, fr.at[pl.ds(1, 31)])

    lane16 = iota((16, 128), 1)
    unpacked, gains = [], None
    for h in range(HEADS):
        at = [fr[lax.rem(yl + q // 2, 2) * (2 * HEADS) + lax.rem(core + q % 2, 2) * HEADS + from_col[h]].astype(F32) for q in range(4)]
        t16 = jnp.where(lane16 < 32, pltpu.roll(at[0], 32, 1), jnp.where(
            lane16 < 64, pltpu.roll(at[1], 64, 1), pltpu.roll(at[2], 96, 1)))
        lo, hi = at[3][0:8], at[3][8:16]
        t8 = jnp.where(lane8 < 32, pltpu.roll(lo, 32, 1), jnp.where(
            lane8 < 64, pltpu.roll(pltpu.roll(lo, 64, 1), 4, 0), pltpu.roll(hi, 96, 1)))
        gains = t8 if gains is None else gains + t8
        unpacked.append(jnp.concatenate(at + [t16, t8], 0))
    for j, v in enumerate(merge_heads(unpacked)):
        flat[j * 88:j * 88 + 88, :] = v
    for j in range(6):
        for m in range(3):
            gw_ref[m, :, j * 128:(j + 1) * 128] = flat[j * 88 + m * 27:j * 88 + m * 27 + 27, :]
    gg_ref[...] = gains[1:4, 0:HD]
    store.wait()
    drain()


def shards(qkv_fine, grad_out, pool_weight, norm_gain):
    x = qkv_fine[0].transpose(0, 1, 3, 2, 4).reshape(48, 8, 768)
    w = pool_weight.transpose(1, 0, 2)
    vmem = pl.BlockSpec(memory_space=pltpu.VMEM)
    hbm = pl.BlockSpec(memory_space=pl.ANY)
    scratch = [
        ((48, 8, 768), BF16),
        (grad_out.shape[1:], BF16),
        (w.shape, BF16),
        (norm_gain.shape, F32),
        ((3, 27, 768), F32),
        ((4, 9, 8, 768), F32),
        ((8, 32, 128), BF16),
        ((8, 32, 128), BF16),
        ((8, 96, 128), BF16),
        ((8, 96, 128), BF16),
        ((8, 384, 128), BF16),
        ((8, 384, 128), BF16),
        ((48, 64, 128), F32),
        ((416, 128), F32),
        ((288, 128), BF16),
        ((288, 128), BF16),
        ((2, 160, 128), F32),
        ((ZS, 32, 128), BF16),
        ((4, 256, 128), BF16),
        ((256, 512), F32),
        ((256, 512), F32),
        ((4, 8, 128), F32),
        ((4, 128, 128), F32),
        ((4, 128, 128), F32),
        ((ZS, 32, 128), BF16),
        ((ZS, 32, 128), BF16),
        ((288, 128), BF16),
        ((288, 128), BF16),
        ((416, 128), F32),
        ((9 * 128, 128), F32),
        ((8, 112, 128), BF16),
        ((8, 112, 128), BF16),
        ((112, 768), BF16),
        ((208, 768), F32),
        ((48, 8, 768), BF16),
        ((88, 128), F32),
        ((64, 128), F32),
        ((4, 16, 128), F32),
        ((ZS, 16, 128), BF16),
        ((32, 16, 128), BF16),
        ((6 * 88, 128), F32),
        ((8, 128), F32),
    ]
    gx, gw, gg = pl.pallas_call(
        kernel,
        out_shape=(jax.ShapeDtypeStruct(x.shape, BF16), jax.ShapeDtypeStruct(w.shape, F32),
                   jax.ShapeDtypeStruct(norm_gain.shape, F32)),
        in_specs=[hbm] * 4,
        out_specs=(hbm, vmem, vmem),
        scratch_shapes=[pltpu.VMEM(shape, kind) for shape, kind in scratch]
        + [pltpu.SemaphoreType.DMA((26,)), pltpu.SemaphoreType.DMA((26,)), pltpu.SemaphoreType.DMA((5,)),
           pltpu.SemaphoreType.REGULAR((2,))],
        compiler_params=pltpu.CompilerParams(collective_id=0, has_side_effects=True,
                                             vmem_limit_bytes=60 * 1024 * 1024),
    )(x, grad_out[0], w, norm_gain)
    return gx.reshape(4, 4, 3, 8, 768).transpose(0, 1, 3, 2, 4)[None], gw.transpose(1, 0, 2), gg


def solution(mesh):
    in_specs = (P("seq", None, None, "head", None, None), P("seq", None, None, "head", None), P(), P())
    out_specs = (P("seq", None, None, "head", None, None), P(), P())
    return jax.shard_map(shards, mesh=mesh, in_specs=in_specs, out_specs=out_specs, check_vma=False)
```

```python
import jax
import jax.numpy as jnp
from jax import lax
from jax.experimental import pallas as pl
from jax.experimental.pallas import tpu as pltpu
from jax.sharding import PartitionSpec as P

MESH = pl.DeviceIdType.MESH
F32 = jnp.float32
BF16 = jnp.bfloat16
HD = 96
HEADS = 8
ROW_GROUPS = 16
SEQ = 64
ZS = 16
SCALE = HD ** -0.5

PAIRS_Q = (((0, 1), (1, 2)), ((1, 0), (2, 1), (3, 2)), ((3, 0),))
PAIRS_K = (((0, 1), (1, 2)), ((3, 0),))
OWN_Q = (0, 1, 3, 4)

(A2A_K, A2A_Q, FINE, KV_OWN, KV_ROW, KV_FRAME, KV_CORNER, Q_ROW, Q_FRAME, Q_CORNER, GATHER, QUAD, STATS, DQ, SCATTER,
 BQ_ROW, BQ_FRAME, BQ_CORNER, BK_OWN, BK_ROW, BK_FRAME, BK_CORNER, A2A_B, SUM_QUAD, SUM_Z, SPREAD) = range(26)
FAR_FIRST = (8, 7, 9, 6, 10, 5, 11, 4, 12, 3, 13, 2, 14, 1, 15)
KV_SPANS = ((0, 32), (32, 32), (64, 32), (96, 32))
Q_SPANS = ((128, 64), (192, 64), (256, 32))
HALF_WAY = 12


def iota(shape, dim):
    return lax.broadcasted_iota(jnp.int32, shape, dim)


def up(x, by):
    size = x.shape[0]
    return pltpu.roll(x, (size - by) % size, 0)


def split_heads(tiles):
    lane = iota(tiles[0].shape, 1)
    heads = []
    for n in range(HEADS):
        t = tiles[n // 4 * 3:n // 4 * 3 + 3]
        if n % 4 == 0:
            v = t[0]
        elif n % 4 == 1:
            v = jnp.where(lane < 32, pltpu.roll(t[0], 32, 1), pltpu.roll(t[1], 32, 1))
        elif n % 4 == 2:
            v = jnp.where(lane < 64, pltpu.roll(t[1], 64, 1), pltpu.roll(t[2], 64, 1))
        else:
            v = pltpu.roll(t[2], 96, 1)
        heads.append(jnp.where(lane < HD, v, 0.0))
    return heads


def merge_heads(h):
    lane = iota(h[0].shape, 1)
    tiles = []
    for half in (0, 4):
        a, b, c, d = h[half:half + 4]
        tiles.append(jnp.where(lane < 96, a, pltpu.roll(b, 96, 1)))
        tiles.append(jnp.where(lane < 64, pltpu.roll(b, 96, 1), pltpu.roll(c, 64, 1)))
        tiles.append(jnp.where(lane < 32, pltpu.roll(c, 64, 1), pltpu.roll(d, 32, 1)))
    return tiles


def tiles_of(v):
    return [v[:, j * 128:(j + 1) * 128] for j in range(6)]


def kernel(x_ref, g_hbm, w_hbm, gain_hbm, gx_ref, gw_ref, gg_ref,
           xv, g_ref, w_ref, gain_ref, wf, wt, sbk, rbk, sbq, rbq, xs, xr, xf, pe, hs, hr, norm, kvg, qgr, raised_ref, ga_ref, st, dqb, dqr, zb, zr,
           hb, hbr, ge, exh, sb2, rb2, gall, ex, gxv, wg, wb, kr, zs, fr, flat, gsc, ss, rs, local, ready):
    s = lax.axis_index("seq")
    n = lax.axis_index("head")
    group, u = s // ROW_GROUPS, s % ROW_GROUPS
    yl, z, core = s // (2 * ZS), s // 2 % ZS, s % 2

    loads = [pltpu.make_async_copy(src, dst, local.at[i]) for i, (src, dst) in enumerate(
        ((w_hbm, w_ref), (gain_hbm, gain_ref), (x_ref, xv), (g_hbm, g_ref)))]
    for load in loads:
        load.start()

    def head_peer(k):
        return (s, lax.rem(n + k, HEADS))

    def z_peer(k):
        return (yl * (2 * ZS) + lax.rem(z + k, ZS) * 2 + core, n)

    def quad_peer(k):
        return (lax.rem(yl + k // 2, 2) * (2 * ZS) + z * 2 + lax.rem(core + k % 2, 2), n)

    def quad_index(k):
        return lax.rem(yl + k // 2, 2) * 2 + lax.rem(core + k % 2, 2)

    def plane_peer(p):
        return (quad_peer(p // HEADS)[0], lax.rem(n + p % HEADS, HEADS))

    def seq_peer(d):
        return (lax.rem(s + d + SEQ, SEQ), n)

    def owner(d):
        block = lax.rem(s + d, SEQ)
        return (block // (2 * ZS) * (2 * ZS) + lax.rem(block // 2 % ZS + HALF_WAY, ZS) * 2 + block % 2, n)

    owned = yl * (2 * ZS) + lax.rem(z + ZS - HALF_WAY, ZS) * 2 + core

    def feeder(d):
        return (lax.rem(owned - d + SEQ, SEQ), n)


    barrier = pltpu.get_barrier_semaphore()
    greeted = [z_peer(k) for k in (4, 12, 3, 13, 2, 14, 1, 15)]
    greeted += [owner(d) for d in (17, 16, 1)] + [feeder(d) for d in (17, 16, 1)]
    greeted += [seq_peer(1), seq_peer(-1), seq_peer(1 + SEQ // 2), seq_peer(-1 - SEQ // 2)] + [quad_peer(k) for k in (3, 2, 1)] + [head_peer(k) for k in range(1, HEADS)]
    for peer in greeted:
        pl.semaphore_signal(barrier, inc=1, device_id=peer, device_id_type=MESH)

    def send(stage, src, dst, peer):
        pltpu.make_async_remote_copy(src_ref=src, dst_ref=dst, send_sem=ss.at[stage], recv_sem=rs.at[stage],
                                     device_id=peer, device_id_type=MESH).start()

    def arrived(stage, ref):
        pltpu.make_async_copy(ref, ref, rs.at[stage]).wait()

    def hand_on(stage, peers):
        for peer in peers:
            pl.semaphore_signal(ready.at[stage], inc=1, device_id=peer, device_id_type=MESH)

    four_on = [z_peer(4), z_peer(12)]
    pending = []

    def drain():
        for stage, ref in pending:
            pltpu.make_async_copy(ref, ref, ss.at[stage]).wait()

    row = iota((8, 768), 0)
    row8 = iota((8, 128), 0)
    lane8 = iota((8, 128), 1)
    loads[0].wait()
    wf[...] = w_ref[...].astype(F32)

    def taps(ab, carry):
        def one(m, e):
            return jnp.broadcast_to(wf[m, pl.ds(ab * 3 + e, 1), :], (8, 768))
        wt[0, ab] = jnp.where(row % 2 == 0, one(0, 1), one(0, 2))
        wt[1, ab] = jnp.where(row % 2 == 1, one(0, 0), 0.0)
        for m in (1, 2):
            wt[1 + m, ab] = jnp.where(row % 4 == 0, one(m, 1), jnp.where(
                row % 4 == 1, one(m, 2), jnp.where(row % 4 == 3, one(m, 0), 0.0)))
        return carry
    lax.fori_loop(0, 9, taps, 0)
    loads[1].wait()
    gsc[...] = jnp.zeros_like(gsc)
    gsc[0:3, 0:HD] = gain_ref[...]
    loads[2].wait()
    loads[3].wait()

    def fine(m, f, r):
        return xv[(f * 4 + r) * 3 + m].astype(F32)

    def store_heads(dst, groups):
        for p in range(len(groups) // 2):
            v = jnp.concatenate(groups[2 * p:2 * p + 2], 0)
            for h, part in enumerate(split_heads(tiles_of(v))):
                dst[h, p * 16:p * 16 + 16, :] = part.astype(BF16)

    groups = []
    for t in range(2):
        for y in range(2):
            both = []
            for m in (1, 2):
                k_sum = None
                for f, a in PAIRS_K[t]:
                    for r, b in PAIRS_K[y]:
                        tk = fine(m, f, r) * wt[1 + m, a * 3 + b]
                        k_sum = tk if k_sum is None else k_sum + tk
                t1 = k_sum + up(k_sum, 1)
                both.append(jnp.where(row == 0, t1, jnp.where(row == 1, up(t1, 2) + up(k_sum, 4), jnp.where(
                    row == 2, up(k_sum, 5), 0.0))))
            groups.append(both[0] + pltpu.roll(both[1], 4, 0))
    store_heads(sbk, groups)
    groups = []
    for t in range(3):
        for y in range(3):
            a_sum = b_sum = None
            for f, a in PAIRS_Q[t]:
                for r, b in PAIRS_Q[y]:
                    v = fine(0, f, r)
                    ta, tb = v * wt[0, a * 3 + b], v * wt[1, a * 3 + b]
                    a_sum = ta if a_sum is None else a_sum + ta
                    b_sum = tb if b_sum is None else b_sum + tb
            b1 = pltpu.roll(b_sum, 1, 0)
            e = a_sum + up(a_sum, 1) + jnp.where(row == 0, 0.0, b1)
            v = jnp.where(row == 0, e, jnp.where(row == 1, up(e, 1), jnp.where(row == 2, up(e, 2), jnp.where(
                row == 3, up(e, 3), jnp.where(row == 4, up(b1, 4), 0.0)))))
            groups.append(v)
    groups.append(jnp.zeros((8, 768), F32))
    for t in range(2):
        groups.append(jnp.concatenate([g_ref[t, 0].astype(F32), g_ref[t, 1].astype(F32)], 0))
    store_heads(sbq, groups)

    def split_fine(p, carry):
        v = jnp.concatenate([xv[2 * p].astype(F32), xv[2 * p + 1].astype(F32)], 0)
        for h, part in enumerate(split_heads(tiles_of(v))):
            xs[h, pl.ds(pl.multiple_of(p * 16, 16), 16), :] = part.astype(BF16)
        return carry
    lax.fori_loop(0, 24, split_fine, 0)

    pl.semaphore_wait(barrier, len(greeted))
    hand_on(0, four_on)
    for stage, src, dst in ((A2A_K, sbk, rbk), (A2A_Q, sbq, rbq)):
        for k in (4, 5, 3, 7, 1, 2, 6):
            peer = head_peer(k)
            send(stage, src.at[peer[1]], dst.at[k], peer)
        pending.append((stage, dst.at[pl.ds(1, HEADS - 1)]))
        dst[0] = src[n]
    pl.semaphore_wait(ready.at[0], 2)
    hand_on(1, four_on)
    arrived(A2A_K, rbk.at[pl.ds(1, HEADS - 1)])

    from_col = [lax.rem(n - h + HEADS, HEADS) for h in range(HEADS)]
    sets = [rbk[from_col[h]].astype(F32) for h in range(HEADS)]
    for grp in range(4):
        parts = [v[grp * 8:grp * 8 + 8] for v in sets]
        for m in range(2):
            if m == 0:
                own = [jnp.where(row8 < 4, p, 0.0) for p in parts]
            else:
                own = [pltpu.roll(jnp.where(row8 >= 4, p, 0.0), 4, 0) for p in parts]
            last = [pltpu.roll(own[4 * j + 3], 6, 0) for j in range(2)]
            for j in range(2):
                v = own[4 * j] + pltpu.roll(own[4 * j + 1], 2, 0) + pltpu.roll(own[4 * j + 2], 4, 0)
                v = v + jnp.where(row8 >= 4, last[j], 0.0)
                if j:
                    v = v + jnp.where(row8 == 0, last[0], 0.0)
                at = 288 + m * 64 + grp * 16 + j * 8
                pe[at:at + 8, :] = v

    def pq(t, y):
        return pe[(t * 3 + y) * 32:(t * 3 + y) * 32 + 32, :]

    def pkv(t, y):
        at = 288 + (t * 2 + y) * 16
        return jnp.concatenate([pe[at:at + 16, :], pe[at + 64:at + 80, :]], 0)

    def exchange(stages, spans, src, dst, peers):
        for stage, (lo, count), peer in zip(stages, spans, peers):
            send(stage, src.at[pl.ds(lo, count)], dst.at[pl.ds(lo, count)], peer)
            pending.append((stage, dst.at[pl.ds(lo, count)]))

    def exchanged(stages, spans, dst):
        for stage, (lo, count) in zip(stages, spans):
            arrived(stage, dst.at[pl.ds(lo, count)])

    hs[0:128, :] = jnp.concatenate([pkv(0, 0), pkv(0, 1), pkv(1, 0), pkv(1, 1)], 0).astype(BF16)
    exchange((KV_OWN, KV_ROW, KV_FRAME, KV_CORNER), KV_SPANS, hs, hr, [owner(d) for d in (0, 1, 16, 17)])
    arrived(A2A_Q, rbq.at[pl.ds(1, HEADS - 1)])
    sets = [rbq[from_col[h]].astype(F32) for h in range(HEADS)]
    for grp in range(9):
        parts = [v[grp * 8:grp * 8 + 8] for v in sets]
        rolled = [pltpu.roll(parts[2 * j + 1], 4, 0) for j in range(4)]
        for j in range(4):
            v = parts[2 * j] + jnp.where(row8 >= 4, rolled[j], 0.0)
            if j:
                v = v + jnp.where(row8 == 0, rolled[j - 1], 0.0)
            pe[grp * 32 + j * 8:grp * 32 + j * 8 + 8, :] = v
    hs[128:288, :] = jnp.concatenate([pq(0, 2), pq(1, 2), pq(2, 0), pq(2, 1), pq(2, 2)], 0).astype(BF16)
    pl.semaphore_wait(ready.at[1], 2)
    exchange((Q_ROW, Q_FRAME, Q_CORNER), Q_SPANS, hs, hr, [seq_peer(d) for d in (1, 16, 17)])
    for k in range(1, HEADS):
        peer = head_peer(k)
        send(FINE, xs.at[peer[1]], xr.at[k], peer)
    pending.append((FINE, xr.at[pl.ds(1, HEADS - 1)]))
    xr[0] = xs[n]

    for t in range(2):
        for y in range(2):
            vs = []
            for j in range(4):
                a, b = (sets[2 * j + i][80 + t * 8:88 + t * 8] for i in range(2))
                if y == 0:
                    vs.append(jnp.where(row8 < 4, a, pltpu.roll(b, 4, 0)))
                else:
                    vs.append(jnp.where(row8 < 4, pltpu.roll(a, 4, 0), b))
            at = 128 + (t * 2 + y) * 32
            qgr[0, at:at + 32, :] = jnp.concatenate(vs, 0).astype(BF16)

    def layer_norm(pooled, lo, count, gain):
        lane = iota((count, 128), 1)
        centred = jnp.where(lane < HD, pooled - jnp.sum(pooled, 1, keepdims=True) * (1.0 / HD), 0.0)
        rstd = lax.rsqrt(jnp.sum(centred * centred, 1, keepdims=True) * (1.0 / HD) + 1e-6)
        unit = centred * rstd
        norm[0, lo:lo + count, :] = unit
        norm[1, lo:lo + count, :] = jnp.broadcast_to(rstd, (count, 128))
        return (unit * gain).astype(BF16)

    has_u = (u > 0).astype(F32)
    has_g = (group > 0).astype(F32)
    has_c = has_u * has_g

    def border(lo, count, has):
        return hr[lo:lo + count, :].astype(F32) * has

    exchanged((KV_OWN, KV_ROW, KV_FRAME, KV_CORNER), KV_SPANS, hr)
    own_u = (owned % ROW_GROUPS > 0).astype(F32)
    own_g = (owned // ROW_GROUPS > 0).astype(F32)
    gain_kv = jnp.where(iota((32, 128), 0) < 16, gsc[1:2, :], gsc[2:3, :])
    gain_q = jnp.broadcast_to(gsc[0:1, :], (128, 128))
    kvg[0] = layer_norm(hr[0:32, :].astype(F32) + border(32, 32, own_u) + border(64, 32, own_g) + border(96, 32, own_u * own_g),
                        128, 32, gain_kv)
    for k in FAR_FIRST:
        send(GATHER, kvg.at[0], kvg.at[k], z_peer(k))
    pending.append((GATHER, kvg.at[pl.ds(1, ZS - 1)]))

    exchanged((Q_ROW, Q_FRAME, Q_CORNER), Q_SPANS, hr)
    q00 = pq(0, 0) + border(128, 32, has_u) + border(192, 32, has_g) + border(256, 32, has_c)
    q01 = pq(0, 1) + border(224, 32, has_g)
    q10 = pq(1, 0) + border(160, 32, has_u)
    qgr[0, 0:128, :] = layer_norm(jnp.concatenate([q00, q01, q10, pq(1, 1)], 0), 0, 128, gain_q)
    for k in (2, 3, 1):
        send(QUAD, qgr.at[0], qgr.at[k], quad_peer(k))
    pending.append((QUAD, qgr.at[pl.ds(1, 3)]))
    arrived(QUAD, qgr.at[pl.ds(1, 3)])
    arrived(GATHER, kvg.at[pl.ds(1, ZS - 1)])

    keys = kvg[:, 0:16, :].reshape(256, 128)
    values = kvg[:, 16:32, :].reshape(256, 128)
    queries = qgr[:, 0:128, :].reshape(512, 128)
    grads = qgr[:, 128:256, :].reshape(512, 128)
    nt = (((1,), (1,)), ((), ()))
    raised_ref[...] = jnp.exp(lax.dot_general(keys, queries, nt, preferred_element_type=F32) * SCALE)
    ga_ref[...] = lax.dot_general(values, grads, nt, preferred_element_type=F32)
    total = jnp.sum(raised_ref[...], 0, keepdims=True)
    delta = jnp.sum(raised_ref[...] * ga_ref[...], 0, keepdims=True)
    for j in range(4):
        st[0, j:j + 1, :] = total[:, j * 128:(j + 1) * 128]
        st[0, 4 + j:5 + j, :] = delta[:, j * 128:(j + 1) * 128]
    for k in (2, 3, 1):
        send(STATS, st.at[0], st.at[k], quad_peer(k))
    pending.append((STATS, st.at[pl.ds(1, 3)]))
    arrived(STATS, st.at[pl.ds(1, 3)])

    def quad_sum(at):
        outs = []
        for j in range(4):
            v = st[0, at + j:at + j + 1, :]
            for k in range(1, 4):
                i = at + (j ^ k)
                v = v + st[k, i:i + 1, :]
            outs.append(v)
        return jnp.concatenate(outs, 1)

    inverse = 1.0 / quad_sum(0)
    row_delta = quad_sum(4) * inverse
    attention = raised_ref[...] * inverse
    grad_scores = (attention * (ga_ref[...] - row_delta)).astype(BF16)
    grad_key = jnp.dot(grad_scores, queries, preferred_element_type=F32) * SCALE
    grad_value = jnp.dot(attention.astype(BF16), grads, preferred_element_type=F32)
    zb[:, 0:16, :] = grad_key.reshape(ZS, 16, 128).astype(BF16)
    zb[:, 16:32, :] = grad_value.reshape(ZS, 16, 128).astype(BF16)
    for k in FAR_FIRST:
        send(SCATTER, zb.at[k], zr.at[k], z_peer(ZS - k))
    pending.append((SCATTER, zr.at[pl.ds(1, ZS - 1)]))
    grad_query = lax.dot_general(grad_scores, keys, (((0,), (0,)), ((), ())), preferred_element_type=F32)
    dqb[...] = grad_query.reshape(4, 128, 128)
    for k in (2, 3, 1):
        send(DQ, dqb.at[k], dqr.at[k], quad_peer(k))
    pending.append((DQ, dqr.at[pl.ds(1, 3)]))
    zr[0] = zb[0]
    dqr[0] = dqb[0]

    def norm_backward(grad_normed, lo, count, gain):
        lane = iota((count, 128), 1)
        unit = norm[0, lo:lo + count, :]
        inner = grad_normed * gain
        mean_1 = jnp.sum(inner, 1, keepdims=True) * (1.0 / HD)
        mean_2 = jnp.sum(inner * unit, 1, keepdims=True) * (1.0 / HD)
        out = norm[1, lo:lo + count, :] * jnp.where(lane < HD, inner - mean_1 - unit * mean_2, 0.0)
        return out, grad_normed * unit

    arrived(DQ, dqr.at[pl.ds(1, 3)])
    dq = dqr[0] + dqr[1] + dqr[2] + dqr[3]
    gq, gain_rows = norm_backward(dq * SCALE + qgr[0, 128:256, :].astype(F32), 0, 128, gain_q)
    wg[80:88, :] = jnp.zeros((8, 128), F32)
    wg[81:82, :] = jnp.sum(gain_rows, 0, keepdims=True)
    hb[128:288, :] = jnp.concatenate([gq[0:32], gq[64:96], gq[0:64], gq[0:32]], 0).astype(BF16)
    exchange((BQ_ROW, BQ_FRAME, BQ_CORNER), Q_SPANS, hb, hbr, [seq_peer(-d) for d in (1, 16, 17)])
    for i, grp in enumerate(OWN_Q):
        ge[grp * 32:grp * 32 + 32, :] = gq[i * 32:i * 32 + 32]

    arrived(FINE, xr.at[pl.ds(1, HEADS - 1)])
    for h in range(HEADS):
        xf[:, h * 8:h * 8 + 8, :] = xr[from_col[h]].astype(F32).reshape(48, 8, 128)

    arrived(SCATTER, zr.at[pl.ds(1, ZS - 1)])
    gkv, gain_rows = norm_backward(jnp.sum(zr[...].astype(F32), 0), 128, 32, gain_kv)
    wg[82:83, :] = jnp.sum(gain_rows[0:16], 0, keepdims=True)
    wg[83:84, :] = jnp.sum(gain_rows[16:32], 0, keepdims=True)
    hb[0:128, :] = jnp.concatenate([gkv] * 4, 0).astype(BF16)
    exchange((BK_OWN, BK_ROW, BK_FRAME, BK_CORNER), KV_SPANS, hb, hbr, [feeder(d) for d in (0, 1, 16, 17)])
    back_u = (u < ROW_GROUPS - 1).astype(F32)
    back_g = (group < SEQ // ROW_GROUPS - 1).astype(F32)
    back_c = back_u * back_g

    def returned(lo, count, has):
        return hbr[lo:lo + count, :].astype(F32) * has

    exchanged((BQ_ROW, BQ_FRAME, BQ_CORNER), Q_SPANS, hbr)
    ge[2 * 32:3 * 32, :] = returned(128, 32, back_u)
    ge[5 * 32:6 * 32, :] = returned(160, 32, back_u)
    ge[6 * 32:8 * 32, :] = returned(192, 64, back_g)
    ge[8 * 32:9 * 32, :] = returned(256, 32, back_c)

    def pairs(pair_list, a):
        return [(f, t) for t, entries in enumerate(pair_list) for f, tap in entries if tap == a]

    def spread(rows, cols, target):
        return jnp.where(iota((rows, cols), 1) == target, 1.0, 0.0).astype(BF16)

    r = iota((128, 32), 0)
    spread_q = spread(128, 32, ((r & 63) >> 1) + (r >> 6))
    spread_k = spread(64, 16, (iota((64, 16), 0) + 1) >> 2)
    odd, by_four = row8 % 2 == 1, row8 % 4

    def over_blocks(v):
        return jnp.sum(v.reshape(HEADS, 8, 128), 0)

    for grp in range(9):
        exh[grp * 128:grp * 128 + 128, :] = jnp.dot(spread_q, ge[grp * 32:grp * 32 + 32, :].astype(BF16),
                                                    preferred_element_type=F32)

    def tap_rows(masked, m, ab):
        for e, v in enumerate(masked):
            wg[m * 27 + ab * 3 + e:m * 27 + ab * 3 + e + 1, :] = jnp.sum(v, 0, keepdims=True)

    for a in range(3):
        for b in range(3):
            first = second = None
            for f, t in pairs(PAIRS_Q, a):
                for rr, y in pairs(PAIRS_Q, b):
                    v, at = xf[(f * 4 + rr) * 3], (t * 3 + y) * 128
                    t1, t2 = v * exh[at:at + 64, :], v * exh[at + 64:at + 128, :]
                    first = t1 if first is None else first + t1
                    second = t2 if second is None else second + t2
            first, second = over_blocks(first), over_blocks(second)
            tap_rows((jnp.where(odd, second, 0.0), jnp.where(odd, 0.0, first), jnp.where(odd, first, 0.0)), 0, a * 3 + b)

    def key_taps(m, wide, chosen):
        for a, b in chosen:
            (f, t), = pairs(PAIRS_K, a)
            (rr, y), = pairs(PAIRS_K, b)
            v = over_blocks(xf[(f * 4 + rr) * 3 + m] * wide[t * 2 + y])
            tap_rows(tuple(jnp.where(by_four == c, v, 0.0) for c in (3, 0, 1)), m, a * 3 + b)

    def wide_key(m, group):
        at = 224 + m * 64 + group * 16
        return jnp.dot(spread_k, ge[at:at + 16, :].astype(BF16), preferred_element_type=F32)

    exchanged((BK_OWN, BK_ROW, BK_FRAME, BK_CORNER), KV_SPANS, hbr)
    for lo, at, has in ((0, 0, 1.0), (32, 16, back_u), (64, 32, back_g), (96, 48, back_c)):
        v = returned(lo, 32, has)
        ge[288 + at:304 + at, :] = v[0:16]
        ge[352 + at:368 + at, :] = v[16:32]
    for m in (1, 2):
        key_taps(m, [wide_key(m, group) for group in range(4)], [(a, b) for a in range(3) for b in range(3)])

    t16, t8 = wg[64:80, :], wg[80:88, :]
    tail = jnp.concatenate([pltpu.roll(t16, 96, 1), pltpu.roll(t16, 64, 1), pltpu.roll(t16, 32, 1),
                            jnp.where(row8 < 4, pltpu.roll(t8, 96, 1), pltpu.roll(pltpu.roll(t8, 64, 1), 4, 0)),
                            pltpu.roll(t8, 32, 1)], 0)
    wb[...] = jnp.where(iota((64, 128), 1) < HD, wg[0:64, :], tail)

    def piece(k):
        return pl.ds(pl.multiple_of(quad_index(k) * 16, 16), 16)

    for k in (2, 3, 1):
        send(SUM_QUAD, wb.at[piece(k)], kr.at[k], quad_peer(k))
    pending.append((SUM_QUAD, kr.at[pl.ds(1, 3)]))
    kr[0] = wb[piece(0), :]

    zero = jnp.zeros((8, 128), F32)
    out_rows = [[] for _ in range(HEADS)]
    for grp in range(9):
        vs = [ge[grp * 32 + j * 8:grp * 32 + j * 8 + 8, :] for j in range(4)] + [zero]
        half = [pltpu.roll(v, 4, 0) for v in vs]
        for h in range(HEADS):
            j = h // 2
            out_rows[h].append(vs[j] if h % 2 == 0 else jnp.where(row8 < 4, half[j], half[j + 1]))
    for grp in range(4):
        vs = [[ge[at:at + 8, :] for at in (288 + m * 64 + grp * 16, 296 + m * 64 + grp * 16)] + [zero] for m in range(2)]
        for h in range(HEADS):
            j, i = h // 4, h % 4
            parts = []
            for m in range(2):
                v = pltpu.roll(vs[m][j], 8 - 2 * i, 0) if i else vs[m][j]
                if i == 3:
                    v = jnp.where(row8 < 2, v, pltpu.roll(vs[m][j + 1], 2, 0))
                parts.append(v)
            out_rows[h].append(jnp.where(row8 < 4, parts[0], pltpu.roll(parts[1], 4, 0)))
    for h in range(HEADS):
        sb2[h] = jnp.concatenate(out_rows[h] + [zero], 0).astype(BF16)
    for k in range(1, HEADS):
        peer = head_peer(k)
        send(A2A_B, sb2.at[peer[1]], rb2.at[k], peer)
    pending.append((A2A_B, rb2.at[pl.ds(1, HEADS - 1)]))
    rb2[0] = sb2[n]

    arrived(SUM_QUAD, kr.at[pl.ds(1, 3)])
    zs[0] = (kr[0] + kr[1] + kr[2] + kr[3]).astype(zs.dtype)
    for k in FAR_FIRST:
        send(SUM_Z, zs.at[0], zs.at[k], z_peer(k))
    pending.append((SUM_Z, zs.at[pl.ds(1, ZS - 1)]))

    arrived(SUM_Z, zs.at[pl.ds(1, ZS - 1)])
    v = zs[z].astype(F32)
    for k in range(1, ZS):
        v = v + zs[lax.rem(z - k + ZS, ZS)].astype(F32)
    fr[0] = v.astype(BF16)
    for p in range(31, 0, -1):
        send(SPREAD, fr.at[0], fr.at[p], plane_peer(p))
    pending.append((SPREAD, fr.at[pl.ds(1, 31)]))

    arrived(A2A_B, rb2.at[pl.ds(1, HEADS - 1)])
    tiles = merge_heads([rb2[from_col[h]].astype(F32) for h in range(HEADS)])
    for j in range(6):
        gall[:, j * 128:(j + 1) * 128] = tiles[j].astype(BF16)
    r = iota((208, 112), 0)
    grp, late, i = r >> 4, (r >> 3) & 1, r & 7
    ex[...] = jnp.dot(spread(208, 112, grp * 8 + jnp.where(grp < 9, (i >> 1) + late, ((i + 1) >> 2) + 4 * late)),
                      gall[...], preferred_element_type=F32)

    def g_at(grp, late):
        at = grp * 16 + late * 8
        return ex[at:at + 8, :]

    def reached(pair_list, f):
        return [(t, a) for t, entries in enumerate(pair_list) for ff, a in entries if ff == f]

    for f in range(4):
        for rr in range(4):
            q_sum = None
            for t, a in reached(PAIRS_Q, f):
                for y, b in reached(PAIRS_Q, rr):
                    term = g_at(t * 3 + y, 0) * wt[0, a * 3 + b] + g_at(t * 3 + y, 1) * wt[1, a * 3 + b]
                    q_sum = term if q_sum is None else q_sum + term
            gxv[(f * 4 + rr) * 3] = q_sum.astype(BF16)
            for m in (1, 2):
                k_sum = jnp.zeros((8, 768), F32)
                for t, a in reached(PAIRS_K, f):
                    for y, b in reached(PAIRS_K, rr):
                        k_sum = g_at(9 + t * 2 + y, m - 1) * wt[1 + m, a * 3 + b]
                gxv[(f * 4 + rr) * 3 + m] = k_sum.astype(BF16)
    store = pltpu.make_async_copy(gxv, gx_ref, local.at[4])
    store.start()

    arrived(SPREAD, fr.at[pl.ds(1, 31)])

    lane16 = iota((16, 128), 1)
    unpacked, gains = [], None
    for h in range(HEADS):
        at = [fr[lax.rem(yl + q // 2, 2) * (2 * HEADS) + lax.rem(core + q % 2, 2) * HEADS + from_col[h]].astype(F32) for q in range(4)]
        t16 = jnp.where(lane16 < 32, pltpu.roll(at[0], 32, 1), jnp.where(
            lane16 < 64, pltpu.roll(at[1], 64, 1), pltpu.roll(at[2], 96, 1)))
        lo, hi = at[3][0:8], at[3][8:16]
        t8 = jnp.where(lane8 < 32, pltpu.roll(lo, 32, 1), jnp.where(
            lane8 < 64, pltpu.roll(pltpu.roll(lo, 64, 1), 4, 0), pltpu.roll(hi, 96, 1)))
        gains = t8 if gains is None else gains + t8
        unpacked.append(jnp.concatenate(at + [t16, t8], 0))
    for j, v in enumerate(merge_heads(unpacked)):
        flat[j * 88:j * 88 + 88, :] = v
    for j in range(6):
        for m in range(3):
            gw_ref[m, :, j * 128:(j + 1) * 128] = flat[j * 88 + m * 27:j * 88 + m * 27 + 27, :]
    gg_ref[...] = gains[1:4, 0:HD]
    store.wait()
    drain()


def shards(qkv_fine, grad_out, pool_weight, norm_gain):
    x = qkv_fine[0].transpose(0, 1, 3, 2, 4).reshape(48, 8, 768)
    w = pool_weight.transpose(1, 0, 2)
    vmem = pl.BlockSpec(memory_space=pltpu.VMEM)
    hbm = pl.BlockSpec(memory_space=pl.ANY)
    scratch = [
        ((48, 8, 768), BF16),
        (grad_out.shape[1:], BF16),
        (w.shape, BF16),
        (norm_gain.shape, F32),
        ((3, 27, 768), F32),
        ((4, 9, 8, 768), F32),
        ((8, 32, 128), BF16),
        ((8, 32, 128), BF16),
        ((8, 96, 128), BF16),
        ((8, 96, 128), BF16),
        ((8, 384, 128), BF16),
        ((8, 384, 128), BF16),
        ((48, 64, 128), F32),
        ((416, 128), F32),
        ((288, 128), BF16),
        ((288, 128), BF16),
        ((2, 160, 128), F32),
        ((ZS, 32, 128), BF16),
        ((4, 256, 128), BF16),
        ((256, 512), F32),
        ((256, 512), F32),
        ((4, 8, 128), F32),
        ((4, 128, 128), F32),
        ((4, 128, 128), F32),
        ((ZS, 32, 128), BF16),
        ((ZS, 32, 128), BF16),
        ((288, 128), BF16),
        ((288, 128), BF16),
        ((416, 128), F32),
        ((9 * 128, 128), F32),
        ((8, 112, 128), BF16),
        ((8, 112, 128), BF16),
        ((112, 768), BF16),
        ((208, 768), F32),
        ((48, 8, 768), BF16),
        ((88, 128), F32),
        ((64, 128), F32),
        ((4, 16, 128), F32),
        ((ZS, 16, 128), BF16),
        ((32, 16, 128), BF16),
        ((6 * 88, 128), F32),
        ((8, 128), F32),
    ]
    gx, gw, gg = pl.pallas_call(
        kernel,
        out_shape=(jax.ShapeDtypeStruct(x.shape, BF16), jax.ShapeDtypeStruct(w.shape, F32),
                   jax.ShapeDtypeStruct(norm_gain.shape, F32)),
        in_specs=[hbm] * 4,
        out_specs=(hbm, vmem, vmem),
        scratch_shapes=[pltpu.VMEM(shape, kind) for shape, kind in scratch]
        + [pltpu.SemaphoreType.DMA((26,)), pltpu.SemaphoreType.DMA((26,)), pltpu.SemaphoreType.DMA((5,)),
           pltpu.SemaphoreType.REGULAR((2,))],
        compiler_params=pltpu.CompilerParams(collective_id=0, has_side_effects=True,
                                             vmem_limit_bytes=60 * 1024 * 1024),
    )(x, grad_out[0], w, norm_gain)
    return gx.reshape(4, 4, 3, 8, 768).transpose(0, 1, 3, 2, 4)[None], gw.transpose(1, 0, 2), gg


def solution(mesh):
    in_specs = (P("seq", None, None, "head", None, None), P("seq", None, None, "head", None), P(), P())
    out_specs = (P("seq", None, None, "head", None, None), P(), P())
    return jax.shard_map(shards, mesh=mesh, in_specs=in_specs, out_specs=out_specs, check_vma=False)
```
